256 devices in a mesh: ctx: 64 (over z, x, core), head: 4 (over y).
Axes of the slice: x: 4, y: 4, z: 8, core: 2. Of those that a mesh axis runs over, the one named last changes fastest.
Arguments:
- q_pre: bfloat16 [16384, 2560], P('ctx', 'head'), may hold values from -48 to 48
- k_pre: bfloat16 [16384, 2560], P('ctx', 'head'), may hold values from -48 to 48
- values: bfloat16 [16384, 2560], P('ctx', 'head'), may hold values from -6 to 6
- out_grad: bfloat16 [16384, 2560], P('ctx', 'head'), may hold values from -192 to 192
- q_gain: float32 [2560], P('head'), may hold values from 0.25 to 1.75
- k_gain: float32 [2560], P('head'), may hold values from 0.25 to 1.75
- selected: int32 [128, 20, 7], P('ctx', 'head'), may hold values from 0 to 127, as said below
Outputs:
- dq_pre: bfloat16 [16384, 2560], P('ctx', 'head')
- dk_pre: bfloat16 [16384, 2560], P('ctx', 'head')
- dv: bfloat16 [16384, 2560], P('ctx', 'head')
The draws below stay inside these ranges and needn't reach their ends.
Inputs may be any that keep to these rules, and one draw needn't show every extreme that they name: `selected`: entry [i, h, c] names a tile outside the block of query tile i; the 7 entries of one row lie in 7 different blocks. All query tiles of one block have equal rows for each head. Over the heads of one group of 5 consecutive heads starting at a multiple of 5, the rows of one block name no other block more than 1 times in all, and some block exactly 1 times.
All inputs are finite; a program needn't handle non-finite values.
Results may differ from the reference program's by a relative error of at most 0.011.
Values may be sent and summed in bfloat16 or wider, within the bound.
A program may use at most 128 MiB of HBM per device.

```python
import math
import jax
import jax.numpy as jnp
from jax import lax

HEADS = 20
HD = 128
TILE = 128
REM = 7
QT_DEV = 2
TOKENS = 16384
QTILES = 128
HEADS_DEV = 5
WIDTH = 2560


def shared_pair(key):
    streams = jax.random.split(jax.random.fold_in(key, 31), 4)
    columns = jnp.arange(WIDTH, dtype=jnp.int32)
    rise = jnp.sqrt(1.0 + 2.0 * columns.astype(jnp.float32) / (WIDTH - 1))
    q_cols = jnp.exp(jnp.log(10.0) * jax.random.uniform(streams[0], (WIDTH,))) * rise / 6.0
    k_cols = jnp.exp(jnp.log(10.0) * jax.random.uniform(streams[1], (WIDTH,))) * rise / 6.0
    queries = jnp.clip(jax.random.normal(streams[2], (TOKENS, WIDTH)), -6.0, 6.0) * q_cols
    keyrows = jnp.clip(jax.random.normal(streams[3], (TOKENS, WIDTH)), -6.0, 6.0) * k_cols
    return (jnp.clip(queries, -48.0, 48.0), jnp.clip(keyrows, -48.0, 48.0))


def draw_q_pre(key, part):
    return shared_pair(key)[0].astype(jnp.bfloat16)


def draw_k_pre(key, part):
    return shared_pair(key)[1].astype(jnp.bfloat16)


def draw_selected(key, part):
    n_dev = QTILES // QT_DEV
    groups = HEADS // HEADS_DEV
    per_group = HEADS_DEV * REM
    streams = jax.random.split(jax.random.fold_in(key, 11), 2)
    others = jnp.arange(n_dev - 1, dtype=jnp.int32)
    scores = jax.random.randint(streams[0], (n_dev, groups, n_dev - 1), 0, 1 << 20) * n_dev + others
    sigma = jnp.argsort(scores, axis=-1, stable=True).astype(jnp.int32)
    slots = jnp.arange(per_group, dtype=jnp.int32)
    picked = sigma[:, :, slots % (n_dev - 1)]
    owners = (jnp.arange(n_dev, dtype=jnp.int32)[:, None, None] + 1 + picked) % n_dev
    inside = jax.random.randint(streams[1], (n_dev, groups, per_group), 0, QT_DEV)
    tiles = (owners * QT_DEV + inside).reshape(n_dev, 1, groups, HEADS_DEV, REM)
    tiles = jnp.broadcast_to(tiles, (n_dev, QT_DEV, groups, HEADS_DEV, REM))
    return tiles.reshape(QTILES, HEADS, REM).astype(jnp.int32)


def steps_of(own_key, dims, shards, smallest, high):
    loudness = 1.0
    for axis_at, blocks in shards:
        heights = jax.random.uniform(jax.random.fold_in(jax.random.fold_in(own_key, 6), axis_at), (blocks,), jnp.float32, smallest / len(shards), high / len(shards))
        loudness = loudness * jnp.repeat(jnp.exp(heights), dims[axis_at] // blocks).reshape((-1,) + (1,) * (len(dims) - 1 - axis_at))
    return loudness


def bell_draw(key, shape, deviation, reach, shards=(), kind=jnp.bfloat16):
    drawn = deviation * jax.random.normal(key, shape, jnp.float32)
    if shards:
        drawn = drawn * steps_of(key, shape, shards, -0.22, 0.18)
    return jnp.clip(drawn, -reach, reach).astype(kind)


def setup_inputs(seed: int = 0) -> dict:
    seeds = jax.random.split(jax.random.key(seed), 8)
    q_pre = draw_q_pre(jax.random.fold_in(seeds[7], 71), 0)
    k_pre = draw_k_pre(jax.random.fold_in(seeds[7], 71), 0)
    values = bell_draw(seeds[2], (TOKENS, WIDTH), 1.0, 6.0, ((0, 64), (1, 4)))
    out_grad = bell_draw(seeds[3], (TOKENS, WIDTH), 32.0, 192.0, ((0, 64), (1, 4)))
    q_gain = jnp.clip(1.0 + 0.15 * jax.random.normal(seeds[4], (WIDTH,), jnp.float32), 0.25, 1.75)
    k_gain = jnp.clip(1.0 + 0.15 * jax.random.normal(seeds[5], (WIDTH,), jnp.float32), 0.25, 1.75)
    selected = draw_selected(jax.random.fold_in(seeds[7], 71), 0)
    return {"q_pre": q_pre, "k_pre": k_pre, "values": values, "out_grad": out_grad, "q_gain": q_gain, "k_gain": k_gain, "selected": selected}


epsilon = 1e-06

def rms_normed(pre, gain):
    wide = pre.astype(jnp.float32)
    scale = lax.rsqrt(lax.optimization_barrier(jnp.mean(wide * wide, axis=1, keepdims=True)) + epsilon)
    return (wide, scale, (wide * scale * gain).astype(jnp.bfloat16))

def per_head(array):
    return array.reshape(QTILES, TILE, HEADS, HD).transpose(2, 0, 1, 3)

def rounded_back(array):
    return lax.optimization_barrier(array.astype(jnp.bfloat16)).astype(jnp.float32)

def norm_back(wide, scale, gain, grad):
    dot_mean = lax.optimization_barrier(jnp.mean(gain * grad * wide, axis=1, keepdims=True))
    return (scale * gain * grad - wide * scale ** 3 * dot_mean).astype(jnp.bfloat16)

def reference(q_pre, k_pre, values, out_grad, q_gain, k_gain, selected):
    q_wide, q_scale, q_normed = rms_normed(q_pre, q_gain)
    k_wide, k_scale, k_normed = rms_normed(k_pre, k_gain)
    q_heads = per_head(q_normed)
    k_heads = per_head(k_normed)
    v_heads = per_head(values)
    g_heads = per_head(out_grad)
    head_index = jnp.arange(HEADS, dtype=jnp.int32)[:, None]
    factor = 1.0 / math.sqrt(HD)

    def visit(carry, tile_index):
        dk_all, dv_all = carry
        start = tile_index // QT_DEV * QT_DEV
        near_k = lax.dynamic_slice_in_dim(k_heads, start, QT_DEV, 1).reshape(HEADS, QT_DEV * TILE, HD)
        near_v = lax.dynamic_slice_in_dim(v_heads, start, QT_DEV, 1).reshape(HEADS, QT_DEV * TILE, HD)
        picks = lax.dynamic_index_in_dim(selected, tile_index, 0, keepdims=False).astype(jnp.int32)
        far_k = k_heads[head_index, picks].reshape(HEADS, REM * TILE, HD)
        far_v = v_heads[head_index, picks].reshape(HEADS, REM * TILE, HD)
        keys_all = jnp.concatenate((near_k, far_k), axis=1).astype(jnp.float32)
        vals_all = jnp.concatenate((near_v, far_v), axis=1).astype(jnp.float32)
        query = lax.dynamic_index_in_dim(q_heads, tile_index, 1, keepdims=False).astype(jnp.float32)
        grad = lax.dynamic_index_in_dim(g_heads, tile_index, 1, keepdims=False).astype(jnp.float32)
        scores = jnp.einsum('hqd,hkd->hqk', query, keys_all) * factor
        row_top = lax.optimization_barrier(jnp.max(scores, axis=-1))
        lse = row_top + jnp.log(lax.optimization_barrier(jnp.sum(jnp.exp(scores - row_top[..., None]), axis=-1)))
        probs = jnp.exp(scores - lse[..., None])
        dprob = jnp.einsum('hqd,hkd->hqk', grad, vals_all)
        delta = lax.optimization_barrier(jnp.sum(probs * dprob, axis=-1))
        dscore = rounded_back(probs * (dprob - delta[..., None]) * factor)
        probs_b = rounded_back(probs)
        dq_tile = jnp.einsum('hqk,hkd->hqd', dscore, keys_all)
        dk_part = jnp.einsum('hqk,hqd->hkd', dscore, query)
        dv_part = jnp.einsum('hqk,hqd->hkd', probs_b, grad)
        cut = QT_DEV * TILE
        near_dk = dk_part[:, :cut].reshape(HEADS, QT_DEV, TILE, HD)
        near_dv = dv_part[:, :cut].reshape(HEADS, QT_DEV, TILE, HD)
        dk_all = lax.dynamic_update_slice_in_dim(dk_all, lax.dynamic_slice_in_dim(dk_all, start, QT_DEV, 1) + near_dk, start, 1)
        dv_all = lax.dynamic_update_slice_in_dim(dv_all, lax.dynamic_slice_in_dim(dv_all, start, QT_DEV, 1) + near_dv, start, 1)
        dk_all = dk_all.at[head_index, picks].add(dk_part[:, cut:].reshape(HEADS, REM, TILE, HD))
        dv_all = dv_all.at[head_index, picks].add(dv_part[:, cut:].reshape(HEADS, REM, TILE, HD))
        return ((dk_all, dv_all), dq_tile)
    zeros = jnp.zeros((HEADS, QTILES, TILE, HD), jnp.float32)
    (dk_all, dv_all), dq_tiles = lax.scan(visit, (zeros, zeros), jnp.arange(QTILES, dtype=jnp.int32))
    dq_wide = dq_tiles.transpose(0, 2, 1, 3).reshape(TOKENS, WIDTH)
    dk_wide = dk_all.transpose(1, 2, 0, 3).reshape(TOKENS, WIDTH)
    dv_out = dv_all.transpose(1, 2, 0, 3).reshape(TOKENS, WIDTH).astype(jnp.bfloat16)
    dq_out = norm_back(q_wide, q_scale, q_gain, dq_wide)
    dk_out = norm_back(k_wide, k_scale, k_gain, dk_wide)
    return (dq_out, dk_out, dv_out)
```

```python
import functools
import math

import jax
import jax.numpy as jnp
from jax import lax
from jax.experimental import pallas as pl
from jax.experimental.pallas import tpu as pltpu
from jax.sharding import PartitionSpec as P

HD = 128
TILE = 128
NH = 5
REM = 7
NT = 2 * NH
NZ = 8
NP = 8
NY = 4
TOK = 2 * TILE
EPS = 1e-6
FACTOR = 1.0 / math.sqrt(HD)
MESH = pl.DeviceIdType.MESH
F32 = jnp.float32
BF16 = jnp.bfloat16


def dot_nt(a, b):
    return lax.dot_general(a, b, (((1,), (1,)), ((), ())), preferred_element_type=F32)


def dot_nn(a, b):
    return lax.dot_general(a, b, (((1,), (0,)), ((), ())), preferred_element_type=F32)


def dot_tn(a, b):
    return lax.dot_general(a, b, (((0,), (0,)), ((), ())), preferred_element_type=F32)


def fold_rows(array, op):
    parts = [array[8 * i : 8 * i + 8] for i in range(array.shape[0] // 8)]
    while len(parts) > 1:
        parts = [op(parts[i], parts[i + 1]) for i in range(0, len(parts), 2)]
    return parts[0]


def kernel(width_all, *refs):
    sel, q_in, k_in, v_in, g_in, q_gain, k_gain, dq_out, dk_out, dv_out = refs[:10]
    scratch = list(refs[10:])
    v_bufs = [scratch.pop(0) for _ in range(NZ)]
    k_bufs = [scratch.pop(0) for _ in range(NZ)]
    bufs = (v_bufs, k_bufs)
    (
        staged,
        v_got,
        k_got,
        s_all,
        dp_all,
        ds_all,
        back_x,
        back_z,
        s_near,
        dp_near,
        q_heads,
        g_heads,
        lse_ref,
        delta_ref,
        dq_wide,
        dk_sum,
        dv_sum,
        q_scale_ref,
        k_scale_ref,
        y_out,
        y_in,
        req_v,
        req_s,
        zf_send,
        zf_recv,
        xf_send,
        xf_recv,
        xb_send,
        xb_recv,
        zb_send,
        zb_recv,
        y_send,
        y_recv,
        rq_send,
        rq_recv,
        here_sem,
    ) = scratch
    got = (v_got, k_got)

    me = lax.axis_index("ctx")
    group = lax.axis_index("head")
    z = me // NP
    xc = lax.rem(me, NP)

    def in_plane(p):
        return {"ctx": z * NP + lax.rem(xc + p, NP), "head": group}

    z_next = (
        {"ctx": lax.rem(z + 1, NZ) * NP + xc, "head": group},
        {"ctx": lax.rem(z + NZ - 1, NZ) * NP + xc, "head": group},
    )

    def along_y(p):
        return {"ctx": me, "head": lax.rem(group + p, NY)}

    barrier = pltpu.get_barrier_semaphore()
    for p in range(1, NP):
        pl.semaphore_signal(barrier, inc=1, device_id=in_plane(p), device_id_type=MESH)
    for d in range(2):
        pl.semaphore_signal(barrier, inc=1, device_id=z_next[d], device_id_type=MESH)
    for p in range(1, NY):
        pl.semaphore_signal(barrier, inc=1, device_id=along_y(p), device_id_type=MESH)

    for t in range(2):
        for h in range(NH):
            rows, cols = slice(t * TILE, (t + 1) * TILE), slice(h * HD, (h + 1) * HD)
            v_bufs[0][t * NH + h] = v_in[rows, cols]
    lane = lax.broadcasted_iota(jnp.int32, (8, 128), 1)
    wanted = jnp.full((8, 128), -1, jnp.int32)
    for h in range(NH):
        for c in range(REM):
            tile = sel[0, h, c]
            wanted = jnp.where(lane == (tile >> 1), (tile & 1) * NH + h, wanted)
    req_v[xc] = wanted

    def squares(ref):
        wide = ref[...].astype(F32)
        return jnp.sum(wide * wide, axis=1, keepdims=True)

    lanes_tok = lax.broadcasted_iota(jnp.int32, (TOK, 128), 1)

    def as_rows(first, second):
        both = jnp.where(lanes_tok == 0, first, jnp.where(lanes_tok == 1, second, 0.0))
        return jnp.transpose(both)[:8]

    def as_columns(rows):
        tall = jnp.transpose(jnp.concatenate([rows, jnp.zeros((120, TOK), F32)], axis=0))
        return tall[:, 0:1], tall[:, 1:2]

    def y_copy(n, p):
        return pltpu.make_async_remote_copy(
            src_ref=y_out.at[n],
            dst_ref=y_in.at[n, p - 1],
            send_sem=y_send.at[n, p - 1],
            recv_sem=y_recv.at[n, p - 1],
            device_id=along_y(p),
            device_id_type=MESH,
        )

    def y_start(n, first, second):
        y_out[n] = as_rows(first, second)
        for p in range(1, NY):
            y_copy(n, p).start()

    def y_total(n):
        for p in range(1, NY):
            y_copy(n, p).wait_recv()
        return (y_out[n] + y_in[n, 0]) + (y_in[n, 1] + y_in[n, 2])

    q_square, k_square = squares(q_in), squares(k_in)
    pl.semaphore_wait(barrier, NP - 1 + 2 + NY - 1)

    def req_copy(p):
        return pltpu.make_async_remote_copy(
            src_ref=req_v.at[xc],
            dst_ref=req_v.at[xc],
            send_sem=rq_send.at[p - 1],
            recv_sem=rq_recv.at[p - 1],
            device_id=in_plane(p),
            device_id_type=MESH,
        )

    def zf_copy(d, hop, kind, t):
        source = (NZ + 1 - hop) % NZ if d == 0 else hop - 1
        target = NZ - hop if d == 0 else hop
        at = ((hop - 1) * 2 + kind) * 2 + t
        part = pl.ds(t * NH, NH)
        return pltpu.make_async_remote_copy(
            src_ref=bufs[kind][source].at[part],
            dst_ref=bufs[kind][target].at[part],
            send_sem=zf_send.at[d, at],
            recv_sem=zf_recv.at[d, at],
            device_id=z_next[d],
            device_id_type=MESH,
        )

    y_start(0, q_square, k_square)
    for p in range(1, NP):
        req_copy(p).start()
    for t in range(2):
        for d in range(2):
            zf_copy(d, 1, 0, t).start()

    total = y_total(0)
    q_scale, k_scale = as_columns(lax.rsqrt(total / width_all + EPS))
    q_scale_ref[...] = jnp.broadcast_to(q_scale, (TOK, 128))
    k_scale_ref[...] = jnp.broadcast_to(k_scale, (TOK, 128))
    for t in range(2):
        for h in range(NH):
            rows, cols = slice(t * TILE, (t + 1) * TILE), slice(h * HD, (h + 1) * HD)
            k_bufs[0][t * NH + h] = (
                k_in[rows, cols].astype(F32) * k_scale_ref[rows] * k_gain[:, cols]
            ).astype(BF16)
        for d in range(2):
            zf_copy(d, 1, 1, t).start()

    for p in range(1, NP):
        req_copy(p).wait_recv()
    table = pltpu.make_async_copy(req_v, req_s, here_sem.at[0])
    table.start()
    for h in range(NH):
        cols = slice(h * HD, (h + 1) * HD)
        q_heads[h] = (
            q_in[:, cols].astype(F32) * q_scale_ref[...] * q_gain[:, cols]
        ).astype(BF16)
        g_heads[h] = g_in[:, cols]
    table.wait()

    def plane_of(r):
        return lax.rem(z + r, NZ)

    def xf_copy(kind, r, p):
        return pltpu.make_async_remote_copy(
            src_ref=staged.at[(kind * NZ + r) * NP + p],
            dst_ref=got[kind].at[plane_of(r) * NP + xc],
            send_sem=xf_send.at[kind * NZ + r],
            recv_sem=xf_recv.at[kind * NZ + r],
            device_id=in_plane(p),
            device_id_type=MESH,
        )

    def spread(kind, r):
        slot = plane_of(r) * NP + xc
        source = bufs[kind][r]

        def one(p, carry):
            code = jnp.maximum(req_s[lax.rem(xc + p, NP), 0, slot], 0)
            staged[(kind * NZ + r) * NP + p] = source[code]
            xf_copy(kind, r, p).start()
            return carry

        lax.fori_loop(1, NP, one, 0)
        got[kind][slot] = source[jnp.maximum(req_s[xc, 0, slot], 0)]

    def xf_all(kind, r):
        first = (kind * NZ + r) * NP + 1
        return pltpu.make_async_remote_copy(
            src_ref=staged.at[pl.ds(first, NP - 1)],
            dst_ref=got[kind].at[pl.ds(0, NP - 1)],
            send_sem=xf_send.at[kind * NZ + r],
            recv_sem=xf_recv.at[kind * NZ + r],
            device_id=in_plane(1),
            device_id_type=MESH,
        )

    def scores(r):
        for kind in range(2):
            xf_all(kind, r).wait_recv()

        def one(j, carry):
            slot = plane_of(r) * NP + j
            head = lax.rem(jnp.maximum(req_s[xc, 0, slot], 0), NH)
            s_all[slot] = dot_nt(k_got[slot], q_heads[head]) * FACTOR
            dp_all[slot] = dot_nt(v_got[slot], g_heads[head])
            return carry

        lax.fori_loop(0, NP, one, 0)

    def near_scores():
        def one(h, carry):
            for t in range(2):
                s_near[h, t] = dot_nt(k_bufs[0][t * NH + h], q_heads[h]) * FACTOR
                dp_near[h, t] = dot_nt(v_bufs[0][t * NH + h], g_heads[h])
            return carry

        lax.fori_loop(0, NH, one, 0)

    spread(0, 0)
    spread(1, 0)
    near_scores()
    for hop in range(1, 4):
        for kind in range(2):
            for t in range(2):
                for d in range(2):
                    zf_copy(d, hop, kind, t).wait_recv()
                    if hop < 3 or t == d:
                        zf_copy(d, hop + 1, kind, t).start()
            spread(kind, NZ - hop)
            spread(kind, hop)
        if hop == 1:
            scores(0)
        else:
            scores(NZ - hop + 1)
            scores(hop - 1)
    for kind in range(2):
        zf_copy(0, 4, kind, 0).wait_recv()
        zf_copy(1, 4, kind, 1).wait_recv()
        spread(kind, 4)
    scores(5)
    scores(3)
    scores(4)

    for p in range(1, NP):
        req_copy(p).wait_send()
    for hop in range(1, 5):
        for kind in range(2):
            for t in range(2):
                for d in range(2):
                    if hop < 4 or t == d:
                        zf_copy(d, hop, kind, t).wait_send()
    for kind in range(2):
        for r in range(NZ):
            xf_all(kind, r).wait_send()

    def stats(h, carry):
        places = [sel[0, h, c] >> 1 for c in range(REM)]
        top = jnp.maximum(
            fold_rows(s_near[h, 0], jnp.maximum), fold_rows(s_near[h, 1], jnp.maximum)
        )
        for place in places:
            top = jnp.maximum(top, fold_rows(s_all[place], jnp.maximum))
        row_top = jnp.max(top, axis=0, keepdims=True)
        mass = jnp.zeros((8, TOK), F32)
        drift = jnp.zeros((8, TOK), F32)
        pairs = [(s_near.at[h, t], dp_near.at[h, t]) for t in range(2)]
        for s_ref, dp_ref in pairs:
            e = jnp.exp(s_ref[...] - row_top)
            mass += fold_rows(e, jnp.add)
            drift += fold_rows(e * dp_ref[...], jnp.add)
        for place in places:
            e = jnp.exp(s_all[place] - row_top)
            mass += fold_rows(e, jnp.add)
            drift += fold_rows(e * dp_all[place], jnp.add)
        whole = jnp.sum(mass, axis=0, keepdims=True)
        lse_ref[h] = jnp.broadcast_to(row_top + jnp.log(whole), (8, TOK))
        delta = jnp.sum(drift, axis=0, keepdims=True) / whole
        delta_ref[h] = jnp.broadcast_to(delta, (8, TOK))
        return carry

    lax.fori_loop(0, NH, stats, 0)

    def xb_copy(r, p):
        slot = plane_of(r) * NP + lax.rem(xc + p, NP)
        return pltpu.make_async_remote_copy(
            src_ref=staged.at[pl.ds(slot * 2, 2)],
            dst_ref=back_x.at[r, p],
            send_sem=xb_send.at[r],
            recv_sem=xb_recv.at[r],
            device_id=in_plane(p),
            device_id_type=MESH,
        )

    def xb_all(r):
        return pltpu.make_async_remote_copy(
            src_ref=back_x.at[r, pl.ds(1, NP - 1)],
            dst_ref=back_x.at[r, pl.ds(1, NP - 1)],
            send_sem=xb_send.at[r],
            recv_sem=xb_recv.at[r],
            device_id=in_plane(1),
            device_id_type=MESH,
        )

    def far_terms(r):
        def term(p):
            slot = plane_of(r) * NP + lax.rem(xc + p, NP)
            code = req_s[xc, 0, slot]
            head = lax.rem(jnp.maximum(code, 0), NH)
            probs = jnp.exp(s_all[slot] - lse_ref[head][:1])
            probs = jnp.where(code >= 0, probs, 0.0)
            ds = (probs * (dp_all[slot] - delta_ref[head][:1]) * FACTOR).astype(BF16)
            ds_all[slot] = ds
            staged[slot * 2] = dot_nn(probs.astype(BF16), g_heads[head]).astype(BF16)
            staged[slot * 2 + 1] = dot_nn(ds, q_heads[head]).astype(BF16)

        def one(p, carry):
            term(p)
            xb_copy(r, p).start()
            return carry

        lax.fori_loop(1, NP, one, 0)
        term(0)

    def zb_copy(d, level, kind, t):
        r = level if d == 0 else NZ - level
        part = pl.ds(t * NH, NH)
        at = ((level - 1) * 2 + kind) * 2 + t
        return pltpu.make_async_remote_copy(
            src_ref=bufs[kind][r].at[part],
            dst_ref=back_z.at[d, level - 1, kind, part],
            send_sem=zb_send.at[d, at],
            recv_sem=zb_recv.at[d, at],
            device_id=z_next[d],
            device_id_type=MESH,
        )

    def summed(r, kind, block):
        slot = plane_of(r) * NP + xc
        acc = jnp.where(
            req_s[xc, 0, slot] == block, staged[slot * 2 + kind].astype(F32), 0.0
        )
        for p in range(1, NP):
            code = req_s[lax.rem(xc + NP - p, NP), 0, slot]
            acc += jnp.where(code == block, back_x[r, p, kind].astype(F32), 0.0)
        return acc

    def pass_on(d, level):
        r = level if d == 0 else NZ - level
        for t in (1 - d, d) if level == 3 else ((d,) if level == 4 else (0, 1)):
            chained = level < 3 or (level == 3 and t == d)
            for kind in range(2):
                if chained:
                    zb_copy(d, level + 1, kind, t).wait_recv()

                def one(b, carry):
                    block = t * NH + b
                    acc = summed(r, kind, block)
                    if chained:
                        acc += back_z[d, level, kind, block].astype(F32)
                    bufs[kind][r][block] = acc.astype(BF16)
                    return carry

                lax.fori_loop(0, NH, one, 0)
                zb_copy(d, level, kind, t).start()

    far_terms(4)
    far_terms(5)
    far_terms(3)
    xb_all(4).wait_recv()
    pass_on(0, 4)
    pass_on(1, 4)
    far_terms(6)
    far_terms(2)
    far_terms(7)
    far_terms(1)
    far_terms(0)

    def head_terms(h, carry):
        dq = jnp.zeros((TOK, HD), F32)
        lse, delta = lse_ref[h][:1], delta_ref[h][:1]
        for t in range(2):
            probs = jnp.exp(s_near[h, t] - lse)
            ds = (probs * (dp_near[h, t] - delta) * FACTOR).astype(BF16)
            dv_sum[t * NH + h] = dot_nn(probs.astype(BF16), g_heads[h])
            dk_sum[t * NH + h] = dot_nn(ds, q_heads[h])
            dq += dot_tn(ds, k_bufs[0][t * NH + h])
        for c in range(REM):
            place = sel[0, h, c] >> 1
            dq += dot_tn(ds_all[place], k_got[place])
        dq_wide[h] = dq
        return carry

    xb_all(5).wait_recv()
    pass_on(1, 3)
    xb_all(3).wait_recv()
    pass_on(0, 3)
    lax.fori_loop(0, NH, head_terms, 0)
    dots = jnp.zeros((TOK, HD), F32)
    for h in range(NH):
        cols = slice(h * HD, (h + 1) * HD)
        dots += q_gain[:, cols] * dq_wide[h] * q_in[:, cols].astype(F32)
    y_start(1, jnp.sum(dots, axis=1, keepdims=True), 0.0)
    for level in (2, 1):
        xb_all(NZ - level).wait_recv()
        pass_on(1, level)
        xb_all(level).wait_recv()
        pass_on(0, level)

    def finish(wide, gain, grad, scale, dot_mean):
        return (scale * gain * grad - wide * (scale * scale * scale) * dot_mean).astype(BF16)

    q_dot, _ = as_columns(y_total(1) / width_all)
    for h in range(NH):
        cols = slice(h * HD, (h + 1) * HD)
        dq_out[:, cols] = finish(
            q_in[:, cols].astype(F32), q_gain[:, cols], dq_wide[h], q_scale_ref[...], q_dot
        )

    xb_all(0).wait_recv()

    def own_sum(block, carry):
        dk_sum[block] += summed(0, 1, block)
        dv_sum[block] += summed(0, 0, block)
        return carry

    lax.fori_loop(0, NT, own_sum, 0)
    for kind in range(2):
        for t in range(2):
            for d in range(2):
                zb_copy(d, 1, kind, t).wait_recv()
    for t in range(2):
        rows = slice(t * TILE, (t + 1) * TILE)
        for h in range(NH):
            cols = slice(h * HD, (h + 1) * HD)
            b = t * NH + h
            dv = dv_sum[b] + back_z[0, 0, 0, b].astype(F32) + back_z[1, 0, 0, b].astype(F32)
            dv_out[rows, cols] = dv.astype(BF16)
            dk_sum[b] = dk_sum[b] + back_z[0, 0, 1, b].astype(F32) + back_z[1, 0, 1, b].astype(F32)
    columns = []
    for t in range(2):
        rows = slice(t * TILE, (t + 1) * TILE)
        dots = jnp.zeros((TILE, HD), F32)
        for h in range(NH):
            cols = slice(h * HD, (h + 1) * HD)
            dots += k_gain[:, cols] * dk_sum[t * NH + h] * k_in[rows, cols].astype(F32)
        columns.append(jnp.sum(dots, axis=1, keepdims=True))
    y_start(2, jnp.concatenate(columns, axis=0), 0.0)
    k_dot, _ = as_columns(y_total(2) / width_all)
    for t in range(2):
        rows = slice(t * TILE, (t + 1) * TILE)
        for h in range(NH):
            cols = slice(h * HD, (h + 1) * HD)
            dk_out[rows, cols] = finish(
                k_in[rows, cols].astype(F32),
                k_gain[:, cols],
                dk_sum[t * NH + h],
                k_scale_ref[rows],
                k_dot[rows],
            )

    for n in range(3):
        for p in range(1, NY):
            y_copy(n, p).wait_send()
    for r in range(NZ):
        xb_all(r).wait_send()
    for level in range(1, 5):
        for kind in range(2):
            for t in range(2):
                for d in range(2):
                    if level < 4 or t == d:
                        zb_copy(d, level, kind, t).wait_send()


def on_device(q_pre, k_pre, values, out_grad, q_gain, k_gain, selected):
    width_dev = q_pre.shape[1]
    width_all = float(width_dev * lax.axis_size("head"))
    vmem = pl.BlockSpec(memory_space=pltpu.VMEM)
    dma = pltpu.SemaphoreType.DMA
    slots = NZ * NP
    scratch = [pltpu.VMEM((NT, TILE, HD), BF16) for _ in range(2 * NZ)] + [
        pltpu.VMEM((2 * slots, TILE, HD), BF16),
        pltpu.VMEM((slots, TILE, HD), BF16),
        pltpu.VMEM((slots, TILE, HD), BF16),
        pltpu.VMEM((slots, TILE, TOK), F32),
        pltpu.VMEM((slots, TILE, TOK), F32),
        pltpu.VMEM((slots, TILE, TOK), BF16),
        pltpu.VMEM((NZ, NP, 2, TILE, HD), BF16),
        pltpu.VMEM((2, 4, 2, NT, TILE, HD), BF16),
        pltpu.VMEM((NH, 2, TILE, TOK), F32),
        pltpu.VMEM((NH, 2, TILE, TOK), F32),
        pltpu.VMEM((NH, TOK, HD), BF16),
        pltpu.VMEM((NH, TOK, HD), BF16),
        pltpu.VMEM((NH, 8, TOK), F32),
        pltpu.VMEM((NH, 8, TOK), F32),
        pltpu.VMEM((NH, TOK, HD), F32),
        pltpu.VMEM((NT, TILE, HD), F32),
        pltpu.VMEM((NT, TILE, HD), F32),
        pltpu.VMEM((TOK, 128), F32),
        pltpu.VMEM((TOK, 128), F32),
        pltpu.VMEM((3, 8, TOK), F32),
        pltpu.VMEM((3, NY - 1, 8, TOK), F32),
        pltpu.VMEM((NP, 8, 128), jnp.int32),
        pltpu.SMEM((NP, 8, 128), jnp.int32),
        dma((2, 16)),
        dma((2, 16)),
        dma((2 * NZ,)),
        dma((2 * NZ,)),
        dma((NZ,)),
        dma((NZ,)),
        dma((2, 16)),
        dma((2, 16)),
        dma((3, NY - 1)),
        dma((3, NY - 1)),
        dma((NP - 1,)),
        dma((NP - 1,)),
        dma((1,)),
    ]
    out = jax.ShapeDtypeStruct(q_pre.shape, BF16)
    return pl.pallas_call(
        functools.partial(kernel, width_all),
        out_shape=(out, out, out),
        in_specs=[pl.BlockSpec(memory_space=pltpu.SMEM)] + [vmem] * 6,
        out_specs=(vmem, vmem, vmem),
        scratch_shapes=scratch,
        compiler_params=pltpu.CompilerParams(
            collective_id=0, has_side_effects=True, vmem_limit_bytes=62 * 2**20
        ),
        name="sparse_attention_backward",
    )(
        selected,
        q_pre,
        k_pre,
        values,
        out_grad,
        q_gain.reshape(1, -1),
        k_gain.reshape(1, -1),
    )


def solution(mesh):
    placed = (
        P("ctx", "head"),
        P("ctx", "head"),
        P("ctx", "head"),
        P("ctx", "head"),
        P("head"),
        P("head"),
        P("ctx", "head", None),
    )
    return jax.shard_map(
        on_device,
        mesh=mesh,
        in_specs=placed,
        out_specs=(P("ctx", "head"), P("ctx", "head"), P("ctx", "head")),
        check_vma=False,
    )
```

```python
import functools
import math

import jax
import jax.numpy as jnp
from jax import lax
from jax.experimental import pallas as pl
from jax.experimental.pallas import tpu as pltpu
from jax.sharding import PartitionSpec as P

HD = 128
TILE = 128
NH = 5
REM = 7
NT = 2 * NH
NZ = 8
NP = 8
NX = 4
NY = 4
TOK = 2 * TILE
EPS = 1e-6
FACTOR = 1.0 / math.sqrt(HD)
MESH = pl.DeviceIdType.MESH
F32 = jnp.float32
BF16 = jnp.bfloat16


def dot_nt(a, b):
    return lax.dot_general(a, b, (((1,), (1,)), ((), ())), preferred_element_type=F32)


def dot_nn(a, b):
    return lax.dot_general(a, b, (((1,), (0,)), ((), ())), preferred_element_type=F32)


def dot_tn(a, b):
    return lax.dot_general(a, b, (((0,), (0,)), ((), ())), preferred_element_type=F32)


def fold_rows(array, op):
    parts = [array[8 * i : 8 * i + 8] for i in range(array.shape[0] // 8)]
    while len(parts) > 1:
        parts = [op(parts[i], parts[i + 1]) for i in range(0, len(parts), 2)]
    return parts[0]


def kernel(width_all, *refs):
    sel, q_in, k_in, v_in, g_in, q_gain, k_gain, dq_out, dk_out, dv_out = refs[:10]
    scratch = list(refs[10:])
    g_bufs = [scratch.pop(0) for _ in range(NZ)]
    q_bufs = [scratch.pop(0) for _ in range(NZ)]
    moving = (g_bufs, q_bufs)
    (
        v_all,
        k_all,
        s_all,
        dp_all,
        back_z,
        core_out,
        core_in,
        x_out,
        x_in,
        s_near,
        dp_near,
        near_stats,
        stat_out,
        stat_in,
        reply_out,
        reply_in,
        lse_ref,
        delta_ref,
        dq_wide,
        dk_sum,
        dv_sum,
        q_scale_ref,
        k_scale_ref,
        y_out,
        y_in,
        req_v,
        req_s,
        zf_send,
        zf_recv,
        xg_send,
        xg_recv,
        cg_send,
        cg_recv,
        st_send,
        st_recv,
        rp_send,
        rp_recv,
        zb_send,
        zb_recv,
        cb_send,
        cb_recv,
        xb_send,
        xb_recv,
        y_send,
        y_recv,
        rq_send,
        rq_recv,
        here_sem,
    ) = scratch
    fixed = (v_all, k_all)

    me = lax.axis_index("ctx")
    group = lax.axis_index("head")
    z = me // NP
    x = lax.rem(me, NP) // 2
    core = lax.rem(me, 2)

    def along_z(o):
        return {"ctx": lax.rem(z + o, NZ) * NP + lax.rem(me, NP), "head": group}

    def along_x(o):
        return {"ctx": z * NP + lax.rem(x + o, NX) * 2 + core, "head": group}

    def along_y(o):
        return {"ctx": me, "head": lax.rem(group + o, NY)}

    other_core = {"ctx": z * NP + x * 2 + (1 - core), "head": group}
    z_next = (along_z(1), along_z(NZ - 1))
    x_next = (along_x(1), along_x(NX - 1))

    barrier = pltpu.get_barrier_semaphore()
    peers = [along_z(o) for o in range(1, NZ)] + [along_y(o) for o in range(1, NY)]
    peers += [x_next[0], x_next[1], other_core]
    for peer in peers:
        pl.semaphore_signal(barrier, inc=1, device_id=peer, device_id_type=MESH)

    def remote(src, dst, send, recv, to):
        return pltpu.make_async_remote_copy(
            src_ref=src,
            dst_ref=dst,
            send_sem=send,
            recv_sem=recv,
            device_id=to,
            device_id_type=MESH,
        )

    for h in range(NH):
        cols = slice(h * HD, (h + 1) * HD)
        g_bufs[0][h] = g_in[:, cols]
        for t in range(2):
            v_all[t * NH + h] = v_in[t * TILE : (t + 1) * TILE, cols]
    lane = lax.broadcasted_iota(jnp.int32, (8, 128), 1)
    wanted = jnp.full((8, 128), -1, jnp.int32)
    for h in range(NH):
        for c in range(REM):
            tile = sel[h, 0, c]
            wanted = jnp.where(lane == (tile >> 1), (tile & 1) * NH + h, wanted)
    req_v[0] = wanted

    def squares(ref):
        wide = ref[...].astype(F32)
        return jnp.sum(wide * wide, axis=1, keepdims=True)

    lanes_tok = lax.broadcasted_iota(jnp.int32, (TOK, 128), 1)

    def as_rows(first, second):
        both = jnp.where(lanes_tok == 0, first, jnp.where(lanes_tok == 1, second, 0.0))
        return jnp.transpose(both)[:8]

    def as_columns(rows):
        tall = jnp.transpose(jnp.concatenate([rows, jnp.zeros((120, TOK), F32)], axis=0))
        return tall[:, 0:1], tall[:, 1:2]

    def y_copy(n, p):
        return remote(
            y_out.at[n], y_in.at[n, p - 1], y_send.at[n, p - 1], y_recv.at[n, p - 1], along_y(p)
        )

    def y_start(n, first, second):
        y_out[n] = as_rows(first, second)
        for p in range(1, NY):
            y_copy(n, p).start()

    def y_total(n):
        for p in range(1, NY):
            y_copy(n, p).wait_recv()
        return (y_out[n] + y_in[n, 0]) + (y_in[n, 1] + y_in[n, 2])

    q_square, k_square = squares(q_in), squares(k_in)
    pl.semaphore_wait(barrier, len(peers))

    def req_copy(o):
        return remote(
            req_v.at[0], req_v.at[NZ - o], rq_send.at[o - 1], rq_recv.at[o - 1], along_z(o)
        )

    def zf_copy(d, hop, kind, t):
        source = (NZ + 1 - hop) % NZ if d == 0 else hop - 1
        target = NZ - hop if d == 0 else hop
        at = ((hop - 1) * 2 + kind) * 2 + t
        rows = pl.ds(t * TILE, TILE)
        return remote(
            moving[kind][source].at[:, rows],
            moving[kind][target].at[:, rows],
            zf_send.at[d, at],
            zf_recv.at[d, at],
            z_next[d],
        )

    def xg_copy(kind, d, n):
        if n < 2:
            src, dst = n * NH, (6 if d == 0 else 2) * NT + n * NH
        else:
            src = (6 if d == 0 else 2) * NT + d * NH
            dst = 4 * NT + d * NH
        return remote(
            fixed[kind].at[pl.ds(src, NH)],
            fixed[kind].at[pl.ds(dst, NH)],
            xg_send.at[kind, d, n],
            xg_recv.at[kind, d, n],
            x_next[d],
        )

    def cg_copy(kind, dx):
        return remote(
            fixed[kind].at[pl.ds(2 * dx * NT, NT)],
            fixed[kind].at[pl.ds((2 * dx + 1) * NT, NT)],
            cg_send.at[kind, dx],
            cg_recv.at[kind, dx],
            other_core,
        )

    y_start(0, q_square, k_square)
    for t in range(2):
        for d in range(2):
            zf_copy(d, 1, 0, t).start()
            xg_copy(0, d, t).start()
    for o in range(1, NZ):
        req_copy(o).start()
    cg_copy(0, 0).start()

    total = y_total(0)
    q_scale, k_scale = as_columns(lax.rsqrt(total / width_all + EPS))
    q_scale_ref[...] = jnp.broadcast_to(q_scale, (TOK, 128))
    k_scale_ref[...] = jnp.broadcast_to(k_scale, (TOK, 128))

    def gain(ref, h):
        return ref[h * HD : (h + 1) * HD].reshape(1, HD)

    for t in range(2):
        rows = slice(t * TILE, (t + 1) * TILE)
        for h in range(NH):
            cols = slice(h * HD, (h + 1) * HD)
            q_bufs[0][h, rows] = (
                q_in[rows, cols].astype(F32) * q_scale_ref[rows] * gain(q_gain, h)
            ).astype(BF16)
            k_all[t * NH + h] = (
                k_in[rows, cols].astype(F32) * k_scale_ref[rows] * gain(k_gain, h)
            ).astype(BF16)
        for d in range(2):
            zf_copy(d, 1, 1, t).start()
            xg_copy(1, d, t).start()
    cg_copy(1, 0).start()

    for o in range(1, NZ):
        req_copy(o).wait_recv()
    table = pltpu.make_async_copy(req_v, req_s, here_sem.at[0])
    table.start()
    table.wait()

    def code_of(r, place):
        dx, other = place // 2, lax.rem(place, 2)
        lane_at = z * NP + lax.rem(x + dx, NX) * 2 + lax.rem(core + other, 2)
        return req_s[r, 0, lane_at]

    def row_stats(s, dp, top):
        e = jnp.exp(s - top)
        return fold_rows(e, jnp.add), fold_rows(e * dp, jnp.add)

    def near_scores(h, carry):
        tops = []
        for t in range(2):
            s = dot_nt(k_all[t * NH + h], q_bufs[0][h]) * FACTOR
            s_near[h, t] = s
            dp_near[h, t] = dot_nt(v_all[t * NH + h], g_bufs[0][h])
            tops.append(fold_rows(s, jnp.maximum))
        top = jnp.max(jnp.maximum(tops[0], tops[1]), axis=0, keepdims=True)
        first = row_stats(s_near[h, 0], dp_near[h, 0], top)
        second = row_stats(s_near[h, 1], dp_near[h, 1], top)
        mass = jnp.sum(first[0] + second[0], axis=0, keepdims=True)
        drift = jnp.sum(first[1] + second[1], axis=0, keepdims=True)
        near_stats[h, 0] = jnp.broadcast_to(top + jnp.log(mass), (8, TOK))
        near_stats[h, 1] = jnp.broadcast_to(drift / mass, (8, TOK))
        return carry

    def st_copy(r):
        return remote(
            stat_out.at[r], stat_in.at[(NZ - r) % NZ], st_send.at[r], st_recv.at[r], along_z(r)
        )

    sub = lax.broadcasted_iota(jnp.int32, (8, TOK), 0)

    def scores(r):
        def one(i, carry):
            lse8, delta8 = carry
            for half in range(2):
                place = 2 * i + half
                code = jnp.maximum(code_of(r, place), 0)
                head = lax.rem(code, NH)
                s = dot_nt(k_all[place * NT + code], q_bufs[r][head]) * FACTOR
                dp = dot_nt(v_all[place * NT + code], g_bufs[r][head])
                s_all[r * NP + place] = s
                dp_all[r * NP + place] = dp
                top = jnp.max(fold_rows(s, jnp.maximum), axis=0, keepdims=True)
                mass, drift = row_stats(s, dp, top)
                mass = jnp.sum(mass, axis=0, keepdims=True)
                drift = jnp.sum(drift, axis=0, keepdims=True)
                lse8 = jnp.where(sub == place, top + jnp.log(mass), lse8)
                delta8 = jnp.where(sub == place, drift / mass, delta8)
            return lse8, delta8

        zero = jnp.zeros((8, TOK), F32)
        lse8, delta8 = lax.fori_loop(0, NP // 2, one, (zero, zero))
        if r == 0:
            stat_in[0, 0] = lse8
            stat_in[0, 1] = delta8
        else:
            stat_out[r, 0] = lse8
            stat_out[r, 1] = delta8
            st_copy(r).start()

    def forward(hop, kind):
        for t in range(2):
            for d in range(2):
                if hop < 4 or t == d:
                    zf_copy(d, hop, kind, t).wait_recv()
                if hop < 3 or (hop == 3 and t == d):
                    zf_copy(d, hop + 1, kind, t).start()

    def plane_first(kind):
        for t in range(2):
            for d in range(2):
                xg_copy(kind, d, t).wait_recv()
                if t == d:
                    xg_copy(kind, d, 2).start()
        cg_copy(kind, 1).start()
        cg_copy(kind, 3).start()

    def plane_second(kind):
        for d in range(2):
            xg_copy(kind, d, 2).wait_recv()
        cg_copy(kind, 2).start()

    forward(1, 0)
    plane_first(0)
    lax.fori_loop(0, NH, near_scores, 0)
    forward(1, 1)
    plane_first(1)
    plane_second(0)
    forward(2, 0)
    plane_second(1)
    for kind in range(2):
        for dx in range(NX):
            cg_copy(kind, dx).wait_recv()
    scores(0)
    forward(2, 1)
    scores(7)
    scores(1)
    forward(3, 0)
    scores(6)
    scores(2)
    forward(3, 1)
    scores(5)
    forward(4, 0)
    scores(3)
    forward(4, 1)
    scores(4)

    for o in range(1, NZ):
        req_copy(o).wait_send()
    for hop in range(1, 5):
        for kind in range(2):
            for t in range(2):
                for d in range(2):
                    if hop < 4 or t == d:
                        zf_copy(d, hop, kind, t).wait_send()
    for kind in range(2):
        for d in range(2):
            for n in range(3):
                xg_copy(kind, d, n).wait_send()
        for dx in range(NX):
            cg_copy(kind, dx).wait_send()

    row_at = lax.broadcasted_iota(jnp.int32, (NZ * NP, TOK), 0)
    head_at = jnp.full((NZ * NP, TOK), -1, jnp.int32)
    for h in range(NH):
        for c in range(REM):
            owner = sel[h, 0, c] >> 1
            dz = (owner // NP - z + NZ) & (NZ - 1)
            dx = ((owner & (NP - 1)) // 2 - x + NX) & (NX - 1)
            place = dx * 2 + ((owner + core) & 1)
            head_at = jnp.where(row_at == dz * NP + place, h, head_at)
    for r in range(1, NZ):
        st_copy(r).wait_recv()
    pair_lse = jnp.concatenate([stat_in[r, 0] for r in range(NZ)], axis=0)
    pair_delta = jnp.concatenate([stat_in[r, 1] for r in range(NZ)], axis=0)
    for h in range(NH):
        mine = head_at == h
        near_lse, near_delta = near_stats[h, 0, :1], near_stats[h, 1, :1]
        top = jnp.max(jnp.where(mine, pair_lse, -3e38), axis=0, keepdims=True)
        top = jnp.maximum(top, near_lse)
        weight = jnp.where(mine, jnp.exp(pair_lse - top), 0.0)
        near_weight = jnp.exp(near_lse - top)
        whole = jnp.sum(weight, axis=0, keepdims=True) + near_weight
        drift = jnp.where(mine, weight * pair_delta, 0.0)
        drift = jnp.sum(drift, axis=0, keepdims=True) + near_weight * near_delta
        reply_out[pl.ds(h, 1)] = top + jnp.log(whole)
        reply_out[pl.ds(8 + h, 1)] = drift / whole

    def rp_copy(o):
        return remote(
            reply_out, reply_in.at[NZ - o], rp_send.at[o - 1], rp_recv.at[o - 1], along_z(o)
        )

    for o in (4, 3, 5, 2, 6, 1, 7):
        rp_copy(o).start()
    reply_in[0] = reply_out[...]
    for o in range(1, NZ):
        rp_copy(o).wait_recv()
    for r in range(NZ):
        for h in range(NH):
            lse_ref[r * NH + h] = jnp.broadcast_to(reply_in[r, h : h + 1], (8, TOK))
            delta_ref[r * NH + h] = jnp.broadcast_to(reply_in[r, 8 + h : 9 + h], (8, TOK))

    def term(r, place):
        pair = r * NP + place
        asked = code_of(r, place)
        code = jnp.maximum(asked, 0)
        head = lax.rem(code, NH)
        probs = jnp.exp(s_all[pair] - lse_ref[r * NH + head][:1])
        probs = jnp.where(asked >= 0, probs, 0.0)
        ds = (probs * (dp_all[pair] - delta_ref[r * NH + head][:1]) * FACTOR).astype(BF16)
        dv = dot_nn(probs.astype(BF16), g_bufs[r][head])
        dk = dot_nn(ds, q_bufs[r][head])
        dq = dot_tn(ds, k_all[place * NT + code])
        s_all[pair, :, :HD] = dv
        s_all[pair, :, HD:] = dk
        dp_all[pair, :, :HD] = dq[:TILE]
        dp_all[pair, :, HD:] = dq[TILE:]

    def key_sum(place, kind, block):
        cols = slice(kind * HD, (kind + 1) * HD)
        acc = jnp.zeros((TILE, HD), F32)
        for r in range(NZ):
            acc += jnp.where(code_of(r, place) == block, s_all[r * NP + place, :, cols], 0.0)
        return acc

    def query_sum(r, t, h):
        cols = slice(t * TILE, (t + 1) * TILE)
        acc = jnp.zeros((TILE, HD), F32)
        for place in range(NP):
            head = lax.rem(jnp.maximum(code_of(r, place), 0), NH)
            acc += jnp.where(head == h, dp_all[r * NP + place, :, cols], 0.0)
        return acc

    def cb_copy(dx):
        part = pl.ds(dx * 2 * NT, 2 * NT)
        return remote(
            core_out.at[part], core_in.at[part], cb_send.at[dx], cb_recv.at[dx], other_core
        )

    def to_core(dx):
        def one(block, carry):
            for kind in range(2):
                acc = key_sum(2 * dx + 1, kind, block)
                core_out[dx * 2 * NT + kind * NT + block] = acc.astype(BF16)
            return carry

        lax.fori_loop(0, NT, one, 0)
        cb_copy(dx).start()

    def chip_sum(dx, kind, block):
        near = core_in[dx * 2 * NT + kind * NT + block].astype(F32)
        return key_sum(2 * dx, kind, block) + near

    def xb_copy(level, d, kind, t):
        dx = 2 if level == 2 else (1 if d == 0 else 3)
        part = pl.ds(kind * NT + t * NH, NH)
        return remote(
            x_out.at[dx - 1, part],
            x_in.at[level - 1, d, part],
            xb_send.at[level - 1, d, kind, t],
            xb_recv.at[level - 1, d, kind, t],
            x_next[d],
        )

    def x_pass(level, d, t):
        dx = 2 if level == 2 else (1 if d == 0 else 3)
        chained = level == 1 and t == d
        for kind in range(2):
            if chained:
                xb_copy(2, d, kind, t).wait_recv()

            def one(b, carry):
                block = t * NH + b
                acc = chip_sum(dx, kind, block)
                if chained:
                    acc += x_in[1, d, kind * NT + block].astype(F32)
                x_out[dx - 1, kind * NT + block] = acc.astype(BF16)
                return carry

            lax.fori_loop(0, NH, one, 0)
            xb_copy(level, d, kind, t).start()

    def zb_copy(d, level, t):
        r = level if d == 0 else NZ - level
        rows = pl.ds(t * TILE, TILE)
        return remote(
            q_bufs[r].at[:, rows],
            back_z.at[d, level - 1, :, rows],
            zb_send.at[d, level - 1, t],
            zb_recv.at[d, level - 1, t],
            z_next[d],
        )

    def z_pass(d, level):
        r = level if d == 0 else NZ - level
        for t in (1 - d, d) if level == 3 else ((d,) if level == 4 else (0, 1)):
            chained = level < 3 or (level == 3 and t == d)
            rows = slice(t * TILE, (t + 1) * TILE)
            if chained:
                zb_copy(d, level + 1, t).wait_recv()

            def one(h, carry):
                acc = query_sum(r, t, h)
                if chained:
                    acc += back_z[d, level, h, rows].astype(F32)
                q_bufs[r][h, rows] = acc.astype(BF16)
                return carry

            lax.fori_loop(0, NH, one, 0)
            zb_copy(d, level, t).start()

    def rest_terms(r):
        def one(i, carry):
            for half in range(2):
                place = 2 * i + half
                term(r, place + jnp.where(i >= 2, 2, 0))
            return carry

        lax.fori_loop(0, NP // 2 - 1, one, 0)

    for r in range(NZ):
        term(r, 5)
    to_core(2)
    for r in range(NZ):
        term(r, 4)
    rest_terms(4)
    z_pass(0, 4)
    z_pass(1, 4)
    cb_copy(2).wait_recv()
    x_pass(2, 0, 0)
    x_pass(2, 1, 1)
    rest_terms(5)
    z_pass(1, 3)
    rest_terms(3)
    z_pass(0, 3)
    for r in (6, 2, 7, 1, 0):
        rest_terms(r)
    to_core(1)
    to_core(3)
    cb_copy(1).wait_recv()
    x_pass(1, 0, 1)
    cb_copy(3).wait_recv()
    x_pass(1, 1, 0)
    z_pass(1, 2)
    z_pass(0, 2)
    x_pass(1, 0, 0)
    x_pass(1, 1, 1)
    to_core(0)
    z_pass(1, 1)
    z_pass(0, 1)

    def near_terms(h, carry):
        dq = jnp.zeros((TOK, HD), F32)
        lse, delta = lse_ref[h][:1], delta_ref[h][:1]
        for t in range(2):
            probs = jnp.exp(s_near[h, t] - lse)
            ds = (probs * (dp_near[h, t] - delta) * FACTOR).astype(BF16)
            dv_sum[t * NH + h] = dot_nn(probs.astype(BF16), g_bufs[0][h])
            dk_sum[t * NH + h] = dot_nn(ds, q_bufs[0][h])
            dq += dot_tn(ds, k_all[t * NH + h])
        dq_wide[h] = dq
        for t in range(2):
            dq_wide[h, t * TILE : (t + 1) * TILE] += query_sum(0, t, h)
        return carry

    lax.fori_loop(0, NH, near_terms, 0)
    cb_copy(0).wait_recv()

    def own_sum(block, carry):
        dv_sum[block] += chip_sum(0, 0, block)
        dk_sum[block] += chip_sum(0, 1, block)
        return carry

    lax.fori_loop(0, NT, own_sum, 0)

    for t in range(2):
        for d in range(2):
            zb_copy(d, 1, t).wait_recv()
    dots = jnp.zeros((TOK, HD), F32)
    for h in range(NH):
        cols = slice(h * HD, (h + 1) * HD)
        dq = dq_wide[h] + back_z[0, 0, h].astype(F32) + back_z[1, 0, h].astype(F32)
        dq_wide[h] = dq
        dots += gain(q_gain, h) * dq * q_in[:, cols].astype(F32)
    q_dot = jnp.sum(dots, axis=1, keepdims=True)

    for t in range(2):
        for d in range(2):
            for kind in range(2):
                xb_copy(1, d, kind, t).wait_recv()
    columns = []
    for t in range(2):
        rows = slice(t * TILE, (t + 1) * TILE)
        dots = jnp.zeros((TILE, HD), F32)
        for h in range(NH):
            cols = slice(h * HD, (h + 1) * HD)
            b = t * NH + h
            dv = dv_sum[b] + x_in[0, 0, b].astype(F32) + x_in[0, 1, b].astype(F32)
            dv_out[rows, cols] = dv.astype(BF16)
            dk = dk_sum[b] + x_in[0, 0, NT + b].astype(F32) + x_in[0, 1, NT + b].astype(F32)
            dk_sum[b] = dk
            dots += gain(k_gain, h) * dk * k_in[rows, cols].astype(F32)
        columns.append(jnp.sum(dots, axis=1, keepdims=True))
    y_start(1, q_dot, jnp.concatenate(columns, axis=0))

    def finish(wide, gains, grad, scale, dot_mean):
        return (scale * gains * grad - wide * (scale * scale * scale) * dot_mean).astype(BF16)

    q_dot, k_dot = as_columns(y_total(1) / width_all)
    for h in range(NH):
        cols = slice(h * HD, (h + 1) * HD)
        dq_out[:, cols] = finish(
            q_in[:, cols].astype(F32), gain(q_gain, h), dq_wide[h], q_scale_ref[...], q_dot
        )
        for t in range(2):
            rows = slice(t * TILE, (t + 1) * TILE)
            dk_out[rows, cols] = finish(
                k_in[rows, cols].astype(F32),
                gain(k_gain, h),
                dk_sum[t * NH + h],
                k_scale_ref[rows],
                k_dot[rows],
            )

    for n in range(2):
        for p in range(1, NY):
            y_copy(n, p).wait_send()
    for r in range(1, NZ):
        st_copy(r).wait_send()
        rp_copy(r).wait_send()
    for dx in range(NX):
        cb_copy(dx).wait_send()
    for t in range(2):
        for d in range(2):
            for level in range(1, 5):
                if level < 4 or t == d:
                    zb_copy(d, level, t).wait_send()
            for kind in range(2):
                xb_copy(1, d, kind, t).wait_send()
                if t == d:
                    xb_copy(2, d, kind, t).wait_send()


def on_device(q_pre, k_pre, values, out_grad, q_gain, k_gain, selected):
    width_dev = q_pre.shape[1]
    width_all = float(width_dev * lax.axis_size("head"))
    vmem = pl.BlockSpec(memory_space=pltpu.VMEM)
    dma = pltpu.SemaphoreType.DMA
    pairs = NZ * NP
    scratch = [pltpu.VMEM((NH, TOK, HD), BF16) for _ in range(2 * NZ)] + [
        pltpu.VMEM((NP * NT, TILE, HD), BF16),
        pltpu.VMEM((NP * NT, TILE, HD), BF16),
        pltpu.VMEM((pairs, TILE, TOK), F32),
        pltpu.VMEM((pairs, TILE, TOK), F32),
        pltpu.VMEM((2, 4, NH, TOK, HD), BF16),
        pltpu.VMEM((NX * 2 * NT, TILE, HD), BF16),
        pltpu.VMEM((NX * 2 * NT, TILE, HD), BF16),
        pltpu.VMEM((3, 2 * NT, TILE, HD), BF16),
        pltpu.VMEM((2, 2, 2 * NT, TILE, HD), BF16),
        pltpu.VMEM((NH, 2, TILE, TOK), F32),
        pltpu.VMEM((NH, 2, TILE, TOK), F32),
        pltpu.VMEM((NH, 2, 8, TOK), F32),
        pltpu.VMEM((NZ, 2, NP, TOK), F32),
        pltpu.VMEM((NZ, 2, NP, TOK), F32),
        pltpu.VMEM((16, TOK), F32),
        pltpu.VMEM((NZ, 16, TOK), F32),
        pltpu.VMEM((NZ * NH, 8, TOK), F32),
        pltpu.VMEM((NZ * NH, 8, TOK), F32),
        pltpu.VMEM((NH, TOK, HD), F32),
        pltpu.VMEM((NT, TILE, HD), F32),
        pltpu.VMEM((NT, TILE, HD), F32),
        pltpu.VMEM((TOK, 128), F32),
        pltpu.VMEM((TOK, 128), F32),
        pltpu.VMEM((2, 8, TOK), F32),
        pltpu.VMEM((2, NY - 1, 8, TOK), F32),
        pltpu.VMEM((NZ, 8, 128), jnp.int32),
        pltpu.SMEM((NZ, 8, 128), jnp.int32),
        dma((2, 16)),
        dma((2, 16)),
        dma((2, 2, 3)),
        dma((2, 2, 3)),
        dma((2, NX)),
        dma((2, NX)),
        dma((NZ,)),
        dma((NZ,)),
        dma((NZ - 1,)),
        dma((NZ - 1,)),
        dma((2, 4, 2)),
        dma((2, 4, 2)),
        dma((NX,)),
        dma((NX,)),
        dma((2, 2, 2, 2)),
        dma((2, 2, 2, 2)),
        dma((2, NY - 1)),
        dma((2, NY - 1)),
        dma((NZ - 1,)),
        dma((NZ - 1,)),
        dma((1,)),
    ]
    out = jax.ShapeDtypeStruct(q_pre.shape, BF16)
    return pl.pallas_call(
        functools.partial(kernel, width_all),
        out_shape=(out, out, out),
        in_specs=[pl.BlockSpec(memory_space=pltpu.SMEM)] + [vmem] * 6,
        out_specs=(vmem, vmem, vmem),
        scratch_shapes=scratch,
        compiler_params=pltpu.CompilerParams(
            collective_id=0, has_side_effects=True, vmem_limit_bytes=60 * 2**20
        ),
        name="sparse_attention_backward",
    )(
        jnp.transpose(selected, (1, 0, 2)), q_pre, k_pre, values, out_grad, q_gain, k_gain
    )


def solution(mesh):
    placed = (
        P("ctx", "head"),
        P("ctx", "head"),
        P("ctx", "head"),
        P("ctx", "head"),
        P("head"),
        P("head"),
        P("ctx", "head", None),
    )
    return jax.shard_map(
        on_device,
        mesh=mesh,
        in_specs=placed,
        out_specs=(P("ctx", "head"), P("ctx", "head"), P("ctx", "head")),
        check_vma=False,
    )
```

```python
import functools
import math

import jax
import jax.numpy as jnp
from jax import lax
from jax.experimental import pallas as pl
from jax.experimental.pallas import tpu as pltpu
from jax.sharding import PartitionSpec as P

HD = 128
TILE = 128
NH = 5
REM = 7
NT = 2 * NH
NZ = 8
NP = 8
NX = 4
NY = 4
TOK = 2 * TILE
EPS = 1e-6
FACTOR = 1.0 / math.sqrt(HD)
MESH = pl.DeviceIdType.MESH
F32 = jnp.float32
BF16 = jnp.bfloat16


def dot_nt(a, b):
    return lax.dot_general(a, b, (((1,), (1,)), ((), ())), preferred_element_type=F32)


def dot_nn(a, b):
    return lax.dot_general(a, b, (((1,), (0,)), ((), ())), preferred_element_type=F32)


def dot_tn(a, b):
    return lax.dot_general(a, b, (((0,), (0,)), ((), ())), preferred_element_type=F32)


def fold_rows(array, op):
    parts = [array[8 * i : 8 * i + 8] for i in range(array.shape[0] // 8)]
    while len(parts) > 1:
        parts = [op(parts[i], parts[i + 1]) for i in range(0, len(parts), 2)]
    return parts[0]


def kernel(width_all, *refs):
    sel, q_in, k_in, v_in, g_in, q_gain, k_gain, dq_out, dk_out, dv_out = refs[:10]
    scratch = list(refs[10:])
    g_bufs = [scratch.pop(0) for _ in range(NZ)]
    q_bufs = [scratch.pop(0) for _ in range(NZ)]
    moving = (g_bufs, q_bufs)
    (
        v_all,
        k_all,
        s_all,
        dp_all,
        kv_terms,
        q_terms,
        back_z,
        core_out,
        core_in,
        x_out,
        x_in,
        s_near,
        dp_near,
        near_stats,
        stat_out,
        stat_in,
        reply_out,
        reply_in,
        lse_ref,
        delta_ref,
        dq_wide,
        dk_sum,
        dv_sum,
        q_scale_ref,
        k_scale_ref,
        y_out,
        y_in,
        req_v,
        req_s,
        zf_send,
        zf_recv,
        xg_send,
        xg_recv,
        cg_send,
        cg_recv,
        st_send,
        st_recv,
        rp_send,
        rp_recv,
        zb_send,
        zb_recv,
        cb_send,
        cb_recv,
        xb_send,
        xb_recv,
        y_send,
        y_recv,
        rq_send,
        rq_recv,
        here_sem,
    ) = scratch
    fixed = (v_all, k_all)

    me = lax.axis_index("ctx")
    group = lax.axis_index("head")
    z = me // NP
    x = lax.rem(me, NP) // 2
    core = lax.rem(me, 2)

    def along_z(o):
        return {"ctx": lax.rem(z + o, NZ) * NP + lax.rem(me, NP), "head": group}

    def along_x(o):
        return {"ctx": z * NP + lax.rem(x + o, NX) * 2 + core, "head": group}

    def along_y(o):
        return {"ctx": me, "head": lax.rem(group + o, NY)}

    other_core = {"ctx": z * NP + x * 2 + (1 - core), "head": group}
    z_next = (along_z(1), along_z(NZ - 1))
    x_next = (along_x(1), along_x(NX - 1))

    barrier = pltpu.get_barrier_semaphore()
    peers = [along_z(o) for o in range(1, NZ)] + [along_y(o) for o in range(1, NY)]
    peers += [x_next[0], x_next[1], other_core]
    for peer in peers:
        pl.semaphore_signal(barrier, inc=1, device_id=peer, device_id_type=MESH)

    def remote(src, dst, send, recv, to):
        return pltpu.make_async_remote_copy(
            src_ref=src,
            dst_ref=dst,
            send_sem=send,
            recv_sem=recv,
            device_id=to,
            device_id_type=MESH,
        )

    for h in range(NH):
        cols = slice(h * HD, (h + 1) * HD)
        g_bufs[0][h] = g_in[:, cols]
        for t in range(2):
            v_all[t * NH + h] = v_in[t * TILE : (t + 1) * TILE, cols]
    lane = lax.broadcasted_iota(jnp.int32, (8, 128), 1)
    wanted = jnp.full((8, 128), -1, jnp.int32)
    for h in range(NH):
        for c in range(REM):
            tile = sel[h, 0, c]
            wanted = jnp.where(lane == (tile >> 1), (tile & 1) * NH + h, wanted)
    req_v[0] = wanted

    def squares(ref):
        wide = ref[...].astype(F32)
        return jnp.sum(wide * wide, axis=1, keepdims=True)

    lanes_tok = lax.broadcasted_iota(jnp.int32, (TOK, 128), 1)

    def as_rows(first, second):
        both = jnp.where(lanes_tok == 0, first, jnp.where(lanes_tok == 1, second, 0.0))
        return jnp.transpose(both)[:8]

    def as_columns(rows):
        tall = jnp.transpose(jnp.concatenate([rows, jnp.zeros((120, TOK), F32)], axis=0))
        return tall[:, 0:1], tall[:, 1:2]

    def y_copy(n, p):
        return remote(
            y_out.at[n], y_in.at[n, p - 1], y_send.at[n, p - 1], y_recv.at[n, p - 1], along_y(p)
        )

    def y_start(n):
        for p in range(1, NY):
            y_copy(n, p).start()

    def y_total(n):
        for p in range(1, NY):
            y_copy(n, p).wait_recv()
        return (y_out[n] + y_in[n, 0]) + (y_in[n, 1] + y_in[n, 2])

    y_out[0] = as_rows(squares(q_in), squares(k_in))
    pl.semaphore_wait(barrier, len(peers))

    def req_copy(o):
        return remote(
            req_v.at[0], req_v.at[NZ - o], rq_send.at[o - 1], rq_recv.at[o - 1], along_z(o)
        )

    def zf_copy(d, hop, kind, t):
        source = (NZ + 1 - hop) % NZ if d == 0 else hop - 1
        target = NZ - hop if d == 0 else hop
        at = ((hop - 1) * 2 + kind) * 2 + t
        rows = pl.ds(t * TILE, TILE)
        return remote(
            moving[kind][source].at[:, rows],
            moving[kind][target].at[:, rows],
            zf_send.at[d, at],
            zf_recv.at[d, at],
            z_next[d],
        )

    def xg_copy(kind, d, n):
        if n < 2:
            src, dst = n * NH, (6 if d == 0 else 2) * NT + n * NH
        else:
            src = (6 if d == 0 else 2) * NT + d * NH
            dst = 4 * NT + d * NH
        return remote(
            fixed[kind].at[pl.ds(src, NH)],
            fixed[kind].at[pl.ds(dst, NH)],
            xg_send.at[kind, d, n],
            xg_recv.at[kind, d, n],
            x_next[d],
        )

    def cg_copy(kind, dx):
        return remote(
            fixed[kind].at[pl.ds(2 * dx * NT, NT)],
            fixed[kind].at[pl.ds((2 * dx + 1) * NT, NT)],
            cg_send.at[kind, dx],
            cg_recv.at[kind, dx],
            other_core,
        )

    y_start(0)
    for t in range(2):
        for d in range(2):
            zf_copy(d, 1, 0, t).start()
            xg_copy(0, d, t).start()
    for o in range(1, NZ):
        req_copy(o).start()
    cg_copy(0, 0).start()

    total = y_total(0)
    q_scale, k_scale = as_columns(lax.rsqrt(total / width_all + EPS))
    q_scale_ref[...] = jnp.broadcast_to(q_scale, (TOK, 128))
    k_scale_ref[...] = jnp.broadcast_to(k_scale, (TOK, 128))

    def gain(ref, h):
        return ref[h * HD : (h + 1) * HD].reshape(1, HD)

    for t in range(2):
        rows = slice(t * TILE, (t + 1) * TILE)
        for h in range(NH):
            cols = slice(h * HD, (h + 1) * HD)
            q_bufs[0][h, rows] = (
                q_in[rows, cols].astype(F32) * q_scale_ref[rows] * gain(q_gain, h)
            ).astype(BF16)
            k_all[t * NH + h] = (
                k_in[rows, cols].astype(F32) * k_scale_ref[rows] * gain(k_gain, h)
            ).astype(BF16)
        for d in range(2):
            zf_copy(d, 1, 1, t).start()
            xg_copy(1, d, t).start()
    cg_copy(1, 0).start()

    for o in range(1, NZ):
        req_copy(o).wait_recv()
    table = pltpu.make_async_copy(req_v, req_s, here_sem.at[0])
    table.start()
    table.wait()

    def code_of(r, place):
        dx, other = place // 2, lax.rem(place, 2)
        lane_at = z * NP + lax.rem(x + dx, NX) * 2 + lax.rem(core + other, 2)
        return req_s[r, 0, lane_at]

    def row_stats(s, dp, top):
        e = jnp.exp(s - top)
        return fold_rows(e, jnp.add), fold_rows(e * dp, jnp.add)

    def near_scores(h, carry):
        tops = []
        for t in range(2):
            s = dot_nt(k_all[t * NH + h], q_bufs[0][h]) * FACTOR
            s_near[h, t] = s
            dp_near[h, t] = dot_nt(v_all[t * NH + h], g_bufs[0][h])
            tops.append(fold_rows(s, jnp.maximum))
        top = jnp.max(jnp.maximum(tops[0], tops[1]), axis=0, keepdims=True)
        first = row_stats(s_near[h, 0], dp_near[h, 0], top)
        second = row_stats(s_near[h, 1], dp_near[h, 1], top)
        mass = jnp.sum(first[0] + second[0], axis=0, keepdims=True)
        drift = jnp.sum(first[1] + second[1], axis=0, keepdims=True)
        near_stats[h, 0] = jnp.broadcast_to(top + jnp.log(mass), (8, TOK))
        near_stats[h, 1] = jnp.broadcast_to(drift / mass, (8, TOK))
        return carry

    def st_copy(r):
        return remote(
            stat_out.at[r], stat_in.at[(NZ - r) % NZ], st_send.at[r], st_recv.at[r], along_z(r)
        )

    sub = lax.broadcasted_iota(jnp.int32, (8, TOK), 0)

    def gradient_scores(r):
        def one(i, carry):
            for half in range(2):
                place = 2 * i + half
                code = jnp.maximum(code_of(r, place), 0)
                dp_all[r * NP + place] = dot_nt(
                    v_all[place * NT + code], g_bufs[r][lax.rem(code, NH)]
                )
            return carry

        lax.fori_loop(0, NP // 2, one, 0)

    def scores(r, with_dp=True):
        def one(i, carry):
            lse8, delta8 = carry
            for half in range(2):
                place = 2 * i + half
                code = jnp.maximum(code_of(r, place), 0)
                head = lax.rem(code, NH)
                s = dot_nt(k_all[place * NT + code], q_bufs[r][head]) * FACTOR
                if with_dp:
                    dp = dot_nt(v_all[place * NT + code], g_bufs[r][head])
                    dp_all[r * NP + place] = dp
                else:
                    dp = dp_all[r * NP + place]
                s_all[r * NP + place] = s
                top = jnp.max(fold_rows(s, jnp.maximum), axis=0, keepdims=True)
                mass, drift = row_stats(s, dp, top)
                mass = jnp.sum(mass, axis=0, keepdims=True)
                drift = jnp.sum(drift, axis=0, keepdims=True)
                lse8 = jnp.where(sub == place, top + jnp.log(mass), lse8)
                delta8 = jnp.where(sub == place, drift / mass, delta8)
            return lse8, delta8

        zero = jnp.zeros((8, TOK), F32)
        lse8, delta8 = lax.fori_loop(0, NP // 2, one, (zero, zero))
        if r == 0:
            stat_in[0, 0] = lse8
            stat_in[0, 1] = delta8
        else:
            stat_out[r, 0] = lse8
            stat_out[r, 1] = delta8
            st_copy(r).start()

    def forward(hop, kind):
        for t in range(2):
            for d in range(2):
                if hop < 4 or t == d:
                    zf_copy(d, hop, kind, t).wait_recv()
                if hop < 3 or (hop == 3 and t == d):
                    zf_copy(d, hop + 1, kind, t).start()

    def plane_first(kind):
        for t in range(2):
            for d in range(2):
                xg_copy(kind, d, t).wait_recv()
                if t == d:
                    xg_copy(kind, d, 2).start()
        cg_copy(kind, 1).start()
        cg_copy(kind, 3).start()

    def plane_second(kind):
        for d in range(2):
            xg_copy(kind, d, 2).wait_recv()
        cg_copy(kind, 2).start()

    forward(1, 0)
    plane_first(0)
    lax.fori_loop(0, NH, near_scores, 0)
    forward(1, 1)
    plane_first(1)
    plane_second(0)
    forward(2, 0)
    plane_second(1)
    for kind in range(2):
        for dx in range(NX):
            cg_copy(kind, dx).wait_recv()
    scores(0)
    forward(2, 1)
    scores(7)
    scores(1)
    forward(3, 0)
    scores(6)
    scores(2)
    forward(3, 1)
    scores(5)
    forward(4, 0)
    scores(3)
    gradient_scores(4)
    forward(4, 1)
    scores(4, with_dp=False)

    for o in range(1, NZ):
        req_copy(o).wait_send()
    for hop in range(1, 5):
        for kind in range(2):
            for t in range(2):
                for d in range(2):
                    if hop < 4 or t == d:
                        zf_copy(d, hop, kind, t).wait_send()
    for kind in range(2):
        for d in range(2):
            for n in range(3):
                xg_copy(kind, d, n).wait_send()
        for dx in range(NX):
            cg_copy(kind, dx).wait_send()

    row_at = lax.broadcasted_iota(jnp.int32, (NZ * NP, TOK), 0)
    head_at = jnp.full((NZ * NP, TOK), -1, jnp.int32)
    for h in range(NH):
        for c in range(REM):
            owner = sel[h, 0, c] >> 1
            dz = (owner // NP - z + NZ) & (NZ - 1)
            dx = ((owner & (NP - 1)) // 2 - x + NX) & (NX - 1)
            place = dx * 2 + ((owner + core) & 1)
            head_at = jnp.where(row_at == dz * NP + place, h, head_at)
    for r in range(1, NZ):
        st_copy(r).wait_recv()
    pair_lse = jnp.concatenate([stat_in[r, 0] for r in range(NZ)], axis=0)
    pair_delta = jnp.concatenate([stat_in[r, 1] for r in range(NZ)], axis=0)
    for h in range(NH):
        mine = head_at == h
        near_lse, near_delta = near_stats[h, 0, :1], near_stats[h, 1, :1]
        top = jnp.max(jnp.where(mine, pair_lse, -3e38), axis=0, keepdims=True)
        top = jnp.maximum(top, near_lse)
        weight = jnp.where(mine, jnp.exp(pair_lse - top), 0.0)
        near_weight = jnp.exp(near_lse - top)
        whole = jnp.sum(weight, axis=0, keepdims=True) + near_weight
        drift = jnp.where(mine, weight * pair_delta, 0.0)
        drift = jnp.sum(drift, axis=0, keepdims=True) + near_weight * near_delta
        reply_out[pl.ds(h, 1)] = top + jnp.log(whole)
        reply_out[pl.ds(8 + h, 1)] = drift / whole

    def rp_copy(o):
        return remote(
            reply_out, reply_in.at[NZ - o], rp_send.at[o - 1], rp_recv.at[o - 1], along_z(o)
        )

    for o in (4, 3, 5, 2, 6, 1, 7):
        rp_copy(o).start()
    reply_in[0] = reply_out[...]
    for o in range(1, NZ):
        rp_copy(o).wait_recv()
    for r in range(NZ):
        for h in range(NH):
            lse_ref[r * NH + h] = jnp.broadcast_to(reply_in[r, h : h + 1], (8, TOK))
            delta_ref[r * NH + h] = jnp.broadcast_to(reply_in[r, 8 + h : 9 + h], (8, TOK))

    def term(r, place):
        pair = r * NP + place
        asked = code_of(r, place)
        code = jnp.maximum(asked, 0)
        head = lax.rem(code, NH)
        probs = jnp.exp(s_all[pair] - lse_ref[r * NH + head][:1])
        probs = jnp.where(asked >= 0, probs, 0.0)
        ds = (probs * (dp_all[pair] - delta_ref[r * NH + head][:1]) * FACTOR).astype(BF16)
        dv = dot_nn(probs.astype(BF16), g_bufs[r][head])
        dk = dot_nn(ds, q_bufs[r][head])
        dq = dot_tn(ds, k_all[place * NT + code])
        kv_terms[2 * pair] = dv.astype(BF16)
        kv_terms[2 * pair + 1] = dk.astype(BF16)
        q_terms[pair] = dq.astype(BF16)

    zero_tile = jnp.zeros((TILE, HD), BF16)

    def tree(parts):
        while len(parts) > 1:
            parts = [parts[i] + parts[i + 1] for i in range(0, len(parts), 2)]
        return parts[0].astype(F32)

    def key_sum(place, kind, block):
        return tree(
            [
                jnp.where(
                    code_of(r, place) == block, kv_terms[2 * (r * NP + place) + kind], zero_tile
                )
                for r in range(NZ)
            ]
        )

    def query_sum(r, t, h):
        rows = slice(t * TILE, (t + 1) * TILE)
        return tree(
            [
                jnp.where(
                    lax.rem(jnp.maximum(code_of(r, place), 0), NH) == h,
                    q_terms[r * NP + place, rows],
                    zero_tile,
                )
                for place in range(NP)
            ]
        )

    def cb_copy(dx):
        part = pl.ds(dx * 2 * NT, 2 * NT)
        return remote(
            core_out.at[part], core_in.at[part], cb_send.at[dx], cb_recv.at[dx], other_core
        )

    def to_core(dx):
        def one(block, carry):
            for kind in range(2):
                acc = key_sum(2 * dx + 1, kind, block)
                core_out[dx * 2 * NT + kind * NT + block] = acc.astype(BF16)
            return carry

        lax.fori_loop(0, NT, one, 0)
        cb_copy(dx).start()

    def chip_sum(dx, kind, block):
        near = core_in[dx * 2 * NT + kind * NT + block].astype(F32)
        return key_sum(2 * dx, kind, block) + near

    def xb_copy(level, d, kind, t):
        dx = 2 if level == 2 else (1 if d == 0 else 3)
        part = pl.ds(kind * NT + t * NH, NH)
        return remote(
            x_out.at[dx - 1, part],
            x_in.at[level - 1, d, part],
            xb_send.at[level - 1, d, kind, t],
            xb_recv.at[level - 1, d, kind, t],
            x_next[d],
        )

    def x_pass(level, d, t):
        dx = 2 if level == 2 else (1 if d == 0 else 3)
        chained = level == 1 and t == d
        for kind in range(2):
            if chained:
                xb_copy(2, d, kind, t).wait_recv()

            def one(b, carry):
                block = t * NH + b
                acc = chip_sum(dx, kind, block)
                if chained:
                    acc += x_in[1, d, kind * NT + block].astype(F32)
                x_out[dx - 1, kind * NT + block] = acc.astype(BF16)
                return carry

            lax.fori_loop(0, NH, one, 0)
            xb_copy(level, d, kind, t).start()

    def zb_copy(d, level, t):
        r = level if d == 0 else NZ - level
        rows = pl.ds(t * TILE, TILE)
        return remote(
            q_bufs[r].at[:, rows],
            back_z.at[d, level - 1, :, rows],
            zb_send.at[d, level - 1, t],
            zb_recv.at[d, level - 1, t],
            z_next[d],
        )

    def z_pass(d, level):
        r = level if d == 0 else NZ - level
        for t in (1 - d, d) if level == 3 else ((d,) if level == 4 else (0, 1)):
            chained = level < 3 or (level == 3 and t == d)
            rows = slice(t * TILE, (t + 1) * TILE)
            if chained:
                zb_copy(d, level + 1, t).wait_recv()

            def one(h, carry):
                acc = query_sum(r, t, h)
                if chained:
                    acc += back_z[d, level, h, rows].astype(F32)
                q_bufs[r][h, rows] = acc.astype(BF16)
                return carry

            lax.fori_loop(0, NH, one, 0)
            zb_copy(d, level, t).start()

    def rest_terms(r):
        def one(i, carry):
            for half in range(2):
                place = 2 * i + half
                term(r, place + jnp.where(i >= 2, 2, 0))
            return carry

        lax.fori_loop(0, NP // 2 - 1, one, 0)

    def opposite_terms(r):
        term(r, 4)
        term(r, 5)

    opposite_terms(4)
    rest_terms(4)
    z_pass(0, 4)
    z_pass(1, 4)
    for r in (5, 3, 6, 2, 7, 1, 0):
        opposite_terms(r)
    to_core(2)
    rest_terms(5)
    z_pass(1, 3)
    rest_terms(3)
    z_pass(0, 3)
    cb_copy(2).wait_recv()
    x_pass(2, 0, 0)
    x_pass(2, 1, 1)
    for r in (6, 2, 7, 1, 0):
        rest_terms(r)
    to_core(1)
    to_core(3)
    z_pass(1, 2)
    z_pass(0, 2)
    cb_copy(1).wait_recv()
    x_pass(1, 0, 1)
    cb_copy(3).wait_recv()
    x_pass(1, 1, 0)
    x_pass(1, 0, 0)
    x_pass(1, 1, 1)
    to_core(0)

    def near_terms(h, carry):
        dq = jnp.zeros((TOK, HD), F32)
        lse, delta = lse_ref[h][:1], delta_ref[h][:1]
        for t in range(2):
            probs = jnp.exp(s_near[h, t] - lse)
            ds = (probs * (dp_near[h, t] - delta) * FACTOR).astype(BF16)
            dv_sum[t * NH + h] = dot_nn(probs.astype(BF16), g_bufs[0][h])
            dk_sum[t * NH + h] = dot_nn(ds, q_bufs[0][h])
            dq += dot_tn(ds, k_all[t * NH + h])
        dq_wide[h] = dq
        for t in range(2):
            dq_wide[h, t * TILE : (t + 1) * TILE] += query_sum(0, t, h)
        return carry

    lax.fori_loop(0, NH, near_terms, 0)
    z_pass(1, 1)
    z_pass(0, 1)
    cb_copy(0).wait_recv()

    def own_sum(block, carry):
        dv_sum[block] += chip_sum(0, 0, block)
        dk_sum[block] += chip_sum(0, 1, block)
        return carry

    lax.fori_loop(0, NT, own_sum, 0)

    for t in range(2):
        for d in range(2):
            zb_copy(d, 1, t).wait_recv()
    dots = jnp.zeros((TOK, HD), F32)
    for h in range(NH):
        cols = slice(h * HD, (h + 1) * HD)
        dq = dq_wide[h] + back_z[0, 0, h].astype(F32) + back_z[1, 0, h].astype(F32)
        dq_wide[h] = dq
        dots += gain(q_gain, h) * dq * q_in[:, cols].astype(F32)
    q_dot = jnp.sum(dots, axis=1, keepdims=True)

    for t in range(2):
        for d in range(2):
            for kind in range(2):
                xb_copy(1, d, kind, t).wait_recv()
    columns = []
    for t in range(2):
        rows = slice(t * TILE, (t + 1) * TILE)
        dots = jnp.zeros((TILE, HD), F32)
        for h in range(NH):
            cols = slice(h * HD, (h + 1) * HD)
            b = t * NH + h
            dv = dv_sum[b] + x_in[0, 0, b].astype(F32) + x_in[0, 1, b].astype(F32)
            dv_out[rows, cols] = dv.astype(BF16)
            dk = dk_sum[b] + x_in[0, 0, NT + b].astype(F32) + x_in[0, 1, NT + b].astype(F32)
            dk_sum[b] = dk
            dots += gain(k_gain, h) * dk * k_in[rows, cols].astype(F32)
        columns.append(jnp.sum(dots, axis=1, keepdims=True))
    y_out[1] = as_rows(q_dot, jnp.concatenate(columns, axis=0))
    y_start(1)

    def finish(wide, gains, grad, scale, dot_mean):
        return (scale * gains * grad - wide * (scale * scale * scale) * dot_mean).astype(BF16)

    q_dot, k_dot = as_columns(y_total(1) / width_all)
    for h in range(NH):
        cols = slice(h * HD, (h + 1) * HD)
        dq_out[:, cols] = finish(
            q_in[:, cols].astype(F32), gain(q_gain, h), dq_wide[h], q_scale_ref[...], q_dot
        )
        for t in range(2):
            rows = slice(t * TILE, (t + 1) * TILE)
            dk_out[rows, cols] = finish(
                k_in[rows, cols].astype(F32),
                gain(k_gain, h),
                dk_sum[t * NH + h],
                k_scale_ref[rows],
                k_dot[rows],
            )

    for n in range(2):
        for p in range(1, NY):
            y_copy(n, p).wait_send()
    for r in range(1, NZ):
        st_copy(r).wait_send()
        rp_copy(r).wait_send()
    for dx in range(NX):
        cb_copy(dx).wait_send()
    for t in range(2):
        for d in range(2):
            for level in range(1, 5):
                if level < 4 or t == d:
                    zb_copy(d, level, t).wait_send()
            for kind in range(2):
                xb_copy(1, d, kind, t).wait_send()
                if t == d:
                    xb_copy(2, d, kind, t).wait_send()


def place_results(a, b, c, a_out, b_out, c_out, sems):
    copies = [
        pltpu.make_async_copy(src, dst, sems.at[i])
        for i, (src, dst) in enumerate(((a, a_out), (b, b_out), (c, c_out)))
    ]
    for copy in copies:
        copy.start()
    for copy in copies:
        copy.wait()


def on_device(q_pre, k_pre, values, out_grad, q_gain, k_gain, selected):
    width_dev = q_pre.shape[1]
    width_all = float(width_dev * lax.axis_size("head"))
    vmem = pl.BlockSpec(memory_space=pltpu.VMEM)
    dma = pltpu.SemaphoreType.DMA
    pairs = NZ * NP
    scratch = [pltpu.VMEM((NH, TOK, HD), BF16) for _ in range(2 * NZ)] + [
        pltpu.VMEM((NP * NT, TILE, HD), BF16),
        pltpu.VMEM((NP * NT, TILE, HD), BF16),
        pltpu.VMEM((pairs, TILE, TOK), F32),
        pltpu.VMEM((pairs, TILE, TOK), F32),
        pltpu.VMEM((2 * pairs, TILE, HD), BF16),
        pltpu.VMEM((pairs, TOK, HD), BF16),
        pltpu.VMEM((2, 4, NH, TOK, HD), BF16),
        pltpu.VMEM((NX * 2 * NT, TILE, HD), BF16),
        pltpu.VMEM((NX * 2 * NT, TILE, HD), BF16),
        pltpu.VMEM((3, 2 * NT, TILE, HD), BF16),
        pltpu.VMEM((2, 2, 2 * NT, TILE, HD), BF16),
        pltpu.VMEM((NH, 2, TILE, TOK), F32),
        pltpu.VMEM((NH, 2, TILE, TOK), F32),
        pltpu.VMEM((NH, 2, 8, TOK), F32),
        pltpu.VMEM((NZ, 2, NP, TOK), F32),
        pltpu.VMEM((NZ, 2, NP, TOK), F32),
        pltpu.VMEM((16, TOK), F32),
        pltpu.VMEM((NZ, 16, TOK), F32),
        pltpu.VMEM((NZ * NH, 8, TOK), F32),
        pltpu.VMEM((NZ * NH, 8, TOK), F32),
        pltpu.VMEM((NH, TOK, HD), F32),
        pltpu.VMEM((NT, TILE, HD), F32),
        pltpu.VMEM((NT, TILE, HD), F32),
        pltpu.VMEM((TOK, 128), F32),
        pltpu.VMEM((TOK, 128), F32),
        pltpu.VMEM((2, 8, TOK), F32),
        pltpu.VMEM((2, NY - 1, 8, TOK), F32),
        pltpu.VMEM((NZ, 8, 128), jnp.int32),
        pltpu.SMEM((NZ, 8, 128), jnp.int32),
        dma((2, 16)),
        dma((2, 16)),
        dma((2, 2, 3)),
        dma((2, 2, 3)),
        dma((2, NX)),
        dma((2, NX)),
        dma((NZ,)),
        dma((NZ,)),
        dma((NZ - 1,)),
        dma((NZ - 1,)),
        dma((2, 4, 2)),
        dma((2, 4, 2)),
        dma((NX,)),
        dma((NX,)),
        dma((2, 2, 2, 2)),
        dma((2, 2, 2, 2)),
        dma((2, NY - 1)),
        dma((2, NY - 1)),
        dma((NZ - 1,)),
        dma((NZ - 1,)),
        dma((1,)),
    ]
    out = jax.ShapeDtypeStruct(q_pre.shape, BF16)
    results = pl.pallas_call(
        functools.partial(kernel, width_all),
        out_shape=(out, out, out),
        in_specs=[pl.BlockSpec(memory_space=pltpu.SMEM)] + [vmem] * 6,
        out_specs=(vmem, vmem, vmem),
        scratch_shapes=scratch,
        compiler_params=pltpu.CompilerParams(
            collective_id=0, has_side_effects=True, vmem_limit_bytes=60 * 2**20
        ),
        name="sparse_attention_backward",
    )(
        jnp.transpose(selected, (1, 0, 2)), q_pre, k_pre, values, out_grad, q_gain, k_gain
    )
    anywhere = pl.BlockSpec(memory_space=pl.ANY)
    return pl.pallas_call(
        place_results,
        out_shape=(out, out, out),
        in_specs=[anywhere] * 3,
        out_specs=(anywhere,) * 3,
        scratch_shapes=[dma((3,))],
        name="place_results",
    )(*results)


def solution(mesh):
    placed = (
        P("ctx", "head"),
        P("ctx", "head"),
        P("ctx", "head"),
        P("ctx", "head"),
        P("head"),
        P("head"),
        P("ctx", "head", None),
    )
    return jax.shard_map(
        on_device,
        mesh=mesh,
        in_specs=placed,
        out_specs=(P("ctx", "head"), P("ctx", "head"), P("ctx", "head")),
        check_vma=False,
    )
```

```python
import functools
import math

import jax
import jax.numpy as jnp
from jax import lax
from jax.experimental import pallas as pl
from jax.experimental.pallas import tpu as pltpu
from jax.sharding import PartitionSpec as P

HD = 128
TILE = 128
NH = 5
REM = 7
NT = 2 * NH
NZ = 8
NP = 8
NX = 4
NY = 4
TOK = 2 * TILE
EPS = 1e-6
FACTOR = 1.0 / math.sqrt(HD)
MESH = pl.DeviceIdType.MESH
F32 = jnp.float32
BF16 = jnp.bfloat16


def dot_nt(a, b):
    return lax.dot_general(a, b, (((1,), (1,)), ((), ())), preferred_element_type=F32)


def dot_nn(a, b):
    return lax.dot_general(a, b, (((1,), (0,)), ((), ())), preferred_element_type=F32)


def dot_tn(a, b):
    return lax.dot_general(a, b, (((0,), (0,)), ((), ())), preferred_element_type=F32)


def fold_rows(array, op):
    parts = [array[8 * i : 8 * i + 8] for i in range(array.shape[0] // 8)]
    while len(parts) > 1:
        parts = [op(parts[i], parts[i + 1]) for i in range(0, len(parts), 2)]
    return parts[0]


def kernel(width_all, *refs):
    sel, q_in, k_in, v_in, g_in, q_gain, k_gain, dq_out, dk_out, dv_out = refs[:10]
    scratch = list(refs[10:])
    g_bufs = [scratch.pop(0) for _ in range(NZ)]
    q_bufs = [scratch.pop(0) for _ in range(NZ)]
    moving = (g_bufs, q_bufs)
    (
        v_all,
        k_all,
        s_all,
        dp_all,
        kv_terms,
        q_terms,
        back_z,
        core_out,
        core_in,
        x_out,
        x_in,
        s_near,
        dp_near,
        near_stats,
        stat_out,
        stat_in,
        reply_out,
        reply_in,
        lse_ref,
        delta_ref,
        dq_wide,
        dk_sum,
        dv_sum,
        q_scale_ref,
        k_scale_ref,
        y_out,
        y_in,
        req_v,
        req_s,
        zf_send,
        zf_recv,
        xg_send,
        xg_recv,
        cg_send,
        cg_recv,
        st_send,
        st_recv,
        rp_send,
        rp_recv,
        zb_send,
        zb_recv,
        cb_send,
        cb_recv,
        xb_send,
        xb_recv,
        y_send,
        y_recv,
        rq_send,
        rq_recv,
        here_sem,
    ) = scratch
    fixed = (v_all, k_all)

    me = lax.axis_index("ctx")
    group = lax.axis_index("head")
    z = me // NP
    x = lax.rem(me, NP) // 2
    core = lax.rem(me, 2)

    def along_z(o):
        return {"ctx": lax.rem(z + o, NZ) * NP + lax.rem(me, NP), "head": group}

    def along_x(o):
        return {"ctx": z * NP + lax.rem(x + o, NX) * 2 + core, "head": group}

    def along_y(o):
        return {"ctx": me, "head": lax.rem(group + o, NY)}

    other_core = {"ctx": z * NP + x * 2 + (1 - core), "head": group}
    z_next = (along_z(1), along_z(NZ - 1))
    x_next = (along_x(1), along_x(NX - 1))

    barrier = pltpu.get_barrier_semaphore()
    peers = [along_z(o) for o in range(1, NZ)] + [along_y(o) for o in range(1, NY)]
    peers += [x_next[0], x_next[1], other_core]
    for peer in peers:
        pl.semaphore_signal(barrier, inc=1, device_id=peer, device_id_type=MESH)

    def remote(src, dst, send, recv, to):
        return pltpu.make_async_remote_copy(
            src_ref=src,
            dst_ref=dst,
            send_sem=send,
            recv_sem=recv,
            device_id=to,
            device_id_type=MESH,
        )

    for h in range(NH):
        g_bufs[0][h] = g_in[:, h * HD : (h + 1) * HD]
    pl.semaphore_wait(barrier, len(peers))

    def squares(ref):
        wide = ref[...].astype(F32)
        return jnp.sum(wide * wide, axis=1, keepdims=True)

    lanes_tok = lax.broadcasted_iota(jnp.int32, (TOK, 128), 1)

    def as_rows(first, second):
        both = jnp.where(lanes_tok == 0, first, jnp.where(lanes_tok == 1, second, 0.0))
        return jnp.transpose(both)[:8]

    def as_columns(rows):
        tall = jnp.transpose(jnp.concatenate([rows, jnp.zeros((120, TOK), F32)], axis=0))
        return tall[:, 0:1], tall[:, 1:2]

    def y_copy(n, p):
        return remote(
            y_out.at[n], y_in.at[n, p - 1], y_send.at[n, p - 1], y_recv.at[n, p - 1], along_y(p)
        )

    def y_start(n):
        for p in range(1, NY):
            y_copy(n, p).start()

    def y_total(n):
        for p in range(1, NY):
            y_copy(n, p).wait_recv()
        return (y_out[n] + y_in[n, 0]) + (y_in[n, 1] + y_in[n, 2])

    def req_copy(o):
        return remote(
            req_v.at[0], req_v.at[NZ - o], rq_send.at[o - 1], rq_recv.at[o - 1], along_z(o)
        )

    def zf_copy(d, hop, kind, t):
        source = (NZ + 1 - hop) % NZ if d == 0 else hop - 1
        target = NZ - hop if d == 0 else hop
        at = ((hop - 1) * 2 + kind) * 2 + t
        rows = pl.ds(t * TILE, TILE)
        return remote(
            moving[kind][source].at[:, rows],
            moving[kind][target].at[:, rows],
            zf_send.at[d, at],
            zf_recv.at[d, at],
            z_next[d],
        )

    def xg_copy(kind, d, n):
        if n < 2:
            src, dst = n * NH, (6 if d == 0 else 2) * NT + n * NH
        else:
            src = (6 if d == 0 else 2) * NT + d * NH
            dst = 4 * NT + d * NH
        return remote(
            fixed[kind].at[pl.ds(src, NH)],
            fixed[kind].at[pl.ds(dst, NH)],
            xg_send.at[kind, d, n],
            xg_recv.at[kind, d, n],
            x_next[d],
        )

    def cg_copy(kind, dx):
        return remote(
            fixed[kind].at[pl.ds(2 * dx * NT, NT)],
            fixed[kind].at[pl.ds((2 * dx + 1) * NT, NT)],
            cg_send.at[kind, dx],
            cg_recv.at[kind, dx],
            other_core,
        )

    for t in range(2):
        for d in range(2):
            zf_copy(d, 1, 0, t).start()
    y_out[0] = as_rows(squares(q_in), squares(k_in))
    y_start(0)
    for t in range(2):
        for h in range(NH):
            v_all[t * NH + h] = v_in[t * TILE : (t + 1) * TILE, h * HD : (h + 1) * HD]
        for d in range(2):
            xg_copy(0, d, t).start()
    cg_copy(0, 0).start()
    lane = lax.broadcasted_iota(jnp.int32, (8, 128), 1)
    wanted = jnp.full((8, 128), -1, jnp.int32)
    for h in range(NH):
        for c in range(REM):
            tile = sel[h, 0, c]
            wanted = jnp.where(lane == (tile >> 1), (tile & 1) * NH + h, wanted)
    req_v[0] = wanted
    for o in range(1, NZ):
        req_copy(o).start()

    total = y_total(0)
    q_scale, k_scale = as_columns(lax.rsqrt(total / width_all + EPS))
    q_scale_ref[...] = jnp.broadcast_to(q_scale, (TOK, 128))
    k_scale_ref[...] = jnp.broadcast_to(k_scale, (TOK, 128))

    def gain(ref, h):
        return ref[h * HD : (h + 1) * HD].reshape(1, HD)

    for t in range(2):
        rows = slice(t * TILE, (t + 1) * TILE)
        for h in range(NH):
            cols = slice(h * HD, (h + 1) * HD)
            q_bufs[0][h, rows] = (
                q_in[rows, cols].astype(F32) * q_scale_ref[rows] * gain(q_gain, h)
            ).astype(BF16)
            k_all[t * NH + h] = (
                k_in[rows, cols].astype(F32) * k_scale_ref[rows] * gain(k_gain, h)
            ).astype(BF16)
        for d in range(2):
            zf_copy(d, 1, 1, t).start()
            xg_copy(1, d, t).start()
    cg_copy(1, 0).start()

    for o in range(1, NZ):
        req_copy(o).wait_recv()
    table = pltpu.make_async_copy(req_v, req_s, here_sem.at[0])
    table.start()
    table.wait()

    def code_of(r, place):
        dx, other = place // 2, lax.rem(place, 2)
        lane_at = z * NP + lax.rem(x + dx, NX) * 2 + lax.rem(core + other, 2)
        return req_s[r, 0, lane_at]

    def row_stats(s, dp, top):
        e = jnp.exp(s - top)
        return fold_rows(e, jnp.add), fold_rows(e * dp, jnp.add)

    def near_scores(h, carry):
        tops = []
        for t in range(2):
            s = dot_nt(k_all[t * NH + h], q_bufs[0][h]) * FACTOR
            s_near[h, t] = s
            dp_near[h, t] = dot_nt(v_all[t * NH + h], g_bufs[0][h])
            tops.append(fold_rows(s, jnp.maximum))
        top = jnp.max(jnp.maximum(tops[0], tops[1]), axis=0, keepdims=True)
        first = row_stats(s_near[h, 0], dp_near[h, 0], top)
        second = row_stats(s_near[h, 1], dp_near[h, 1], top)
        mass = jnp.sum(first[0] + second[0], axis=0, keepdims=True)
        drift = jnp.sum(first[1] + second[1], axis=0, keepdims=True)
        near_stats[h, 0] = jnp.broadcast_to(top + jnp.log(mass), (8, TOK))
        near_stats[h, 1] = jnp.broadcast_to(drift / mass, (8, TOK))
        return carry

    def st_copy(r):
        return remote(
            stat_out.at[r], stat_in.at[(NZ - r) % NZ], st_send.at[r], st_recv.at[r], along_z(r)
        )

    sub = lax.broadcasted_iota(jnp.int32, (8, TOK), 0)

    def gradient_scores(r):
        def one(i, carry):
            for half in range(2):
                place = 2 * i + half
                code = jnp.maximum(code_of(r, place), 0)
                dp_all[r * NP + place] = dot_nt(
                    v_all[place * NT + code], g_bufs[r][lax.rem(code, NH)]
                )
            return carry

        lax.fori_loop(0, NP // 2, one, 0)

    def scores(r, with_dp=True):
        def one(i, carry):
            lse8, delta8 = carry
            for half in range(2):
                place = 2 * i + half
                code = jnp.maximum(code_of(r, place), 0)
                head = lax.rem(code, NH)
                s = dot_nt(k_all[place * NT + code], q_bufs[r][head]) * FACTOR
                if with_dp:
                    dp = dot_nt(v_all[place * NT + code], g_bufs[r][head])
                    dp_all[r * NP + place] = dp
                else:
                    dp = dp_all[r * NP + place]
                s_all[r * NP + place] = s
                top = jnp.max(fold_rows(s, jnp.maximum), axis=0, keepdims=True)
                mass, drift = row_stats(s, dp, top)
                mass = jnp.sum(mass, axis=0, keepdims=True)
                drift = jnp.sum(drift, axis=0, keepdims=True)
                lse8 = jnp.where(sub == place, top + jnp.log(mass), lse8)
                delta8 = jnp.where(sub == place, drift / mass, delta8)
            return lse8, delta8

        zero = jnp.zeros((8, TOK), F32)
        lse8, delta8 = lax.fori_loop(0, NP // 2, one, (zero, zero))
        if r == 0:
            stat_in[0, 0] = lse8
            stat_in[0, 1] = delta8
        else:
            stat_out[r, 0] = lse8
            stat_out[r, 1] = delta8
            st_copy(r).start()

    def forward(hop, kind):
        for t in range(2):
            for d in range(2):
                if hop < 4 or t == d:
                    zf_copy(d, hop, kind, t).wait_recv()
                if hop < 3 or (hop == 3 and t == d):
                    zf_copy(d, hop + 1, kind, t).start()

    def plane_first(kind):
        for t in range(2):
            for d in range(2):
                xg_copy(kind, d, t).wait_recv()
                if t == d:
                    xg_copy(kind, d, 2).start()
        cg_copy(kind, 1).start()
        cg_copy(kind, 3).start()

    def plane_second(kind):
        for d in range(2):
            xg_copy(kind, d, 2).wait_recv()
        cg_copy(kind, 2).start()

    forward(1, 0)
    plane_first(0)
    lax.fori_loop(0, NH, near_scores, 0)
    forward(1, 1)
    plane_first(1)
    plane_second(0)
    forward(2, 0)
    plane_second(1)
    for kind in range(2):
        for dx in range(NX):
            cg_copy(kind, dx).wait_recv()
    scores(0)
    forward(2, 1)
    scores(7)
    scores(1)
    forward(3, 0)
    scores(6)
    scores(2)
    forward(3, 1)
    scores(5)
    forward(4, 0)
    scores(3)
    gradient_scores(4)
    forward(4, 1)
    scores(4, with_dp=False)

    for o in range(1, NZ):
        req_copy(o).wait_send()
    for hop in range(1, 5):
        for kind in range(2):
            for t in range(2):
                for d in range(2):
                    if hop < 4 or t == d:
                        zf_copy(d, hop, kind, t).wait_send()
    for kind in range(2):
        for d in range(2):
            for n in range(3):
                xg_copy(kind, d, n).wait_send()
        for dx in range(NX):
            cg_copy(kind, dx).wait_send()

    row_at = lax.broadcasted_iota(jnp.int32, (NZ * NP, TOK), 0)
    head_at = jnp.full((NZ * NP, TOK), -1, jnp.int32)
    for h in range(NH):
        for c in range(REM):
            owner = sel[h, 0, c] >> 1
            dz = (owner // NP - z + NZ) & (NZ - 1)
            dx = ((owner & (NP - 1)) // 2 - x + NX) & (NX - 1)
            place = dx * 2 + ((owner + core) & 1)
            head_at = jnp.where(row_at == dz * NP + place, h, head_at)
    for r in range(1, NZ):
        st_copy(r).wait_recv()
    pair_lse = jnp.concatenate([stat_in[r, 0] for r in range(NZ)], axis=0)
    pair_delta = jnp.concatenate([stat_in[r, 1] for r in range(NZ)], axis=0)
    for h in range(NH):
        mine = head_at == h
        near_lse, near_delta = near_stats[h, 0, :1], near_stats[h, 1, :1]
        top = jnp.max(jnp.where(mine, pair_lse, -3e38), axis=0, keepdims=True)
        top = jnp.maximum(top, near_lse)
        weight = jnp.where(mine, jnp.exp(pair_lse - top), 0.0)
        near_weight = jnp.exp(near_lse - top)
        whole = jnp.sum(weight, axis=0, keepdims=True) + near_weight
        drift = jnp.where(mine, weight * pair_delta, 0.0)
        drift = jnp.sum(drift, axis=0, keepdims=True) + near_weight * near_delta
        reply_out[pl.ds(h, 1)] = top + jnp.log(whole)
        reply_out[pl.ds(8 + h, 1)] = drift / whole

    def rp_copy(o):
        return remote(
            reply_out, reply_in.at[NZ - o], rp_send.at[o - 1], rp_recv.at[o - 1], along_z(o)
        )

    for o in (4, 3, 5, 2, 6, 1, 7):
        rp_copy(o).start()
    reply_in[0] = reply_out[...]
    for o in range(1, NZ):
        rp_copy(o).wait_recv()
    for r in range(NZ):
        for h in range(NH):
            lse_ref[r * NH + h] = jnp.broadcast_to(reply_in[r, h : h + 1], (8, TOK))
            delta_ref[r * NH + h] = jnp.broadcast_to(reply_in[r, 8 + h : 9 + h], (8, TOK))

    def term(r, place):
        pair = r * NP + place
        asked = code_of(r, place)
        code = jnp.maximum(asked, 0)
        head = lax.rem(code, NH)
        probs = jnp.exp(s_all[pair] - lse_ref[r * NH + head][:1])
        probs = jnp.where(asked >= 0, probs, 0.0)
        ds = (probs * (dp_all[pair] - delta_ref[r * NH + head][:1]) * FACTOR).astype(BF16)
        dv = dot_nn(probs.astype(BF16), g_bufs[r][head])
        dk = dot_nn(ds, q_bufs[r][head])
        dq = dot_tn(ds, k_all[place * NT + code])
        kv_terms[2 * pair] = dv.astype(BF16)
        kv_terms[2 * pair + 1] = dk.astype(BF16)
        q_terms[pair] = dq.astype(BF16)

    zero_tile = jnp.zeros((TILE, HD), BF16)

    def tree(parts):
        while len(parts) > 1:
            parts = [parts[i] + parts[i + 1] for i in range(0, len(parts), 2)]
        return parts[0].astype(F32)

    def key_sum(place, kind, block):
        return tree(
            [
                jnp.where(
                    code_of(r, place) == block, kv_terms[2 * (r * NP + place) + kind], zero_tile
                )
                for r in range(NZ)
            ]
        )

    def query_sum(r, t, h):
        rows = slice(t * TILE, (t + 1) * TILE)
        return tree(
            [
                jnp.where(
                    lax.rem(jnp.maximum(code_of(r, place), 0), NH) == h,
                    q_terms[r * NP + place, rows],
                    zero_tile,
                )
                for place in range(NP)
            ]
        )

    def cb_copy(dx):
        part = pl.ds(dx * 2 * NT, 2 * NT)
        return remote(
            core_out.at[part], core_in.at[part], cb_send.at[dx], cb_recv.at[dx], other_core
        )

    def to_core(dx):
        def one(block, carry):
            for kind in range(2):
                acc = key_sum(2 * dx + 1, kind, block)
                core_out[dx * 2 * NT + kind * NT + block] = acc.astype(BF16)
            return carry

        lax.fori_loop(0, NT, one, 0)
        cb_copy(dx).start()

    def chip_sum(dx, kind, block):
        near = core_in[dx * 2 * NT + kind * NT + block].astype(F32)
        return key_sum(2 * dx, kind, block) + near

    def xb_copy(level, d, kind, t):
        dx = 2 if level == 2 else (1 if d == 0 else 3)
        part = pl.ds(kind * NT + t * NH, NH)
        return remote(
            x_out.at[dx - 1, part],
            x_in.at[level - 1, d, part],
            xb_send.at[level - 1, d, kind, t],
            xb_recv.at[level - 1, d, kind, t],
            x_next[d],
        )

    def x_pass(level, d, t):
        dx = 2 if level == 2 else (1 if d == 0 else 3)
        chained = level == 1 and t == d
        for kind in range(2):
            if chained:
                xb_copy(2, d, kind, t).wait_recv()

            def one(b, carry):
                block = t * NH + b
                acc = chip_sum(dx, kind, block)
                if chained:
                    acc += x_in[1, d, kind * NT + block].astype(F32)
                x_out[dx - 1, kind * NT + block] = acc.astype(BF16)
                return carry

            lax.fori_loop(0, NH, one, 0)
            xb_copy(level, d, kind, t).start()

    def zb_copy(d, level, t):
        r = level if d == 0 else NZ - level
        rows = pl.ds(t * TILE, TILE)
        return remote(
            q_bufs[r].at[:, rows],
            back_z.at[d, level - 1, :, rows],
            zb_send.at[d, level - 1, t],
            zb_recv.at[d, level - 1, t],
            z_next[d],
        )

    def z_pass(d, level):
        r = level if d == 0 else NZ - level
        for t in (1 - d, d) if level == 3 else ((d,) if level == 4 else (0, 1)):
            chained = level < 3 or (level == 3 and t == d)
            rows = slice(t * TILE, (t + 1) * TILE)
            if chained:
                zb_copy(d, level + 1, t).wait_recv()

            def one(h, carry):
                acc = query_sum(r, t, h)
                if chained:
                    acc += back_z[d, level, h, rows].astype(F32)
                q_bufs[r][h, rows] = acc.astype(BF16)
                return carry

            lax.fori_loop(0, NH, one, 0)
            zb_copy(d, level, t).start()

    def opposite_terms(r):
        term(r, 4)
        term(r, 5)

    def own_terms(r):
        term(r, 0)
        term(r, 1)

    def side_terms(r):
        def one(i, carry):
            for half in range(2):
                term(r, 4 * i + 2 + half)
            return carry

        lax.fori_loop(0, 2, one, 0)

    opposite_terms(4)
    own_terms(4)
    side_terms(4)
    z_pass(0, 4)
    z_pass(1, 4)
    for r in (5, 3, 6, 2, 7, 1, 0):
        opposite_terms(r)
    to_core(2)
    own_terms(5)
    side_terms(5)
    z_pass(1, 3)
    own_terms(3)
    side_terms(3)
    z_pass(0, 3)
    cb_copy(2).wait_recv()
    x_pass(2, 0, 0)
    x_pass(2, 1, 1)
    for r in (6, 2, 7, 1, 0):
        side_terms(r)
    to_core(1)
    to_core(3)
    for r in (6, 2):
        own_terms(r)
    cb_copy(1).wait_recv()
    x_pass(1, 0, 1)
    cb_copy(3).wait_recv()
    x_pass(1, 1, 0)
    z_pass(1, 2)
    z_pass(0, 2)
    for r in (7, 1, 0):
        own_terms(r)
    x_pass(1, 0, 0)
    x_pass(1, 1, 1)
    to_core(0)

    def near_terms(h, carry):
        dq = jnp.zeros((TOK, HD), F32)
        lse, delta = lse_ref[h][:1], delta_ref[h][:1]
        for t in range(2):
            probs = jnp.exp(s_near[h, t] - lse)
            ds = (probs * (dp_near[h, t] - delta) * FACTOR).astype(BF16)
            dv_sum[t * NH + h] = dot_nn(probs.astype(BF16), g_bufs[0][h])
            dk_sum[t * NH + h] = dot_nn(ds, q_bufs[0][h])
            dq += dot_tn(ds, k_all[t * NH + h])
        dq_wide[h] = dq
        for t in range(2):
            dq_wide[h, t * TILE : (t + 1) * TILE] += query_sum(0, t, h)
        return carry

    lax.fori_loop(0, NH, near_terms, 0)
    z_pass(1, 1)
    z_pass(0, 1)
    cb_copy(0).wait_recv()

    def own_sum(block, carry):
        dv_sum[block] += chip_sum(0, 0, block)
        dk_sum[block] += chip_sum(0, 1, block)
        return carry

    lax.fori_loop(0, NT, own_sum, 0)

    for t in range(2):
        for d in range(2):
            zb_copy(d, 1, t).wait_recv()
    dots = jnp.zeros((TOK, HD), F32)
    for h in range(NH):
        cols = slice(h * HD, (h + 1) * HD)
        dq = dq_wide[h] + back_z[0, 0, h].astype(F32) + back_z[1, 0, h].astype(F32)
        dq_wide[h] = dq
        dots += gain(q_gain, h) * dq * q_in[:, cols].astype(F32)
    q_dot = jnp.sum(dots, axis=1, keepdims=True)

    for t in range(2):
        for d in range(2):
            for kind in range(2):
                xb_copy(1, d, kind, t).wait_recv()
    columns = []
    for t in range(2):
        rows = slice(t * TILE, (t + 1) * TILE)
        dots = jnp.zeros((TILE, HD), F32)
        for h in range(NH):
            cols = slice(h * HD, (h + 1) * HD)
            b = t * NH + h
            dv = dv_sum[b] + x_in[0, 0, b].astype(F32) + x_in[0, 1, b].astype(F32)
            dv_out[rows, cols] = dv.astype(BF16)
            dk = dk_sum[b] + x_in[0, 0, NT + b].astype(F32) + x_in[0, 1, NT + b].astype(F32)
            dk_sum[b] = dk
            dots += gain(k_gain, h) * dk * k_in[rows, cols].astype(F32)
        columns.append(jnp.sum(dots, axis=1, keepdims=True))
    y_out[1] = as_rows(q_dot, jnp.concatenate(columns, axis=0))
    y_start(1)

    def finish(wide, gains, grad, scale, dot_mean):
        return (scale * gains * grad - wide * (scale * scale * scale) * dot_mean).astype(BF16)

    q_dot, k_dot = as_columns(y_total(1) / width_all)
    for h in range(NH):
        cols = slice(h * HD, (h + 1) * HD)
        dq_out[:, cols] = finish(
            q_in[:, cols].astype(F32), gain(q_gain, h), dq_wide[h], q_scale_ref[...], q_dot
        )
        for t in range(2):
            rows = slice(t * TILE, (t + 1) * TILE)
            dk_out[rows, cols] = finish(
                k_in[rows, cols].astype(F32),
                gain(k_gain, h),
                dk_sum[t * NH + h],
                k_scale_ref[rows],
                k_dot[rows],
            )

    for n in range(2):
        for p in range(1, NY):
            y_copy(n, p).wait_send()
    for r in range(1, NZ):
        st_copy(r).wait_send()
        rp_copy(r).wait_send()
    for dx in range(NX):
        cb_copy(dx).wait_send()
    for t in range(2):
        for d in range(2):
            for level in range(1, 5):
                if level < 4 or t == d:
                    zb_copy(d, level, t).wait_send()
            for kind in range(2):
                xb_copy(1, d, kind, t).wait_send()
                if t == d:
                    xb_copy(2, d, kind, t).wait_send()


def place_results(a, b, c, a_out, b_out, c_out, held, sems):
    coming = [
        pltpu.make_async_copy(src, held.at[i], sems.at[0, i]) for i, src in enumerate((a, b, c))
    ]
    going = [
        pltpu.make_async_copy(held.at[i], dst, sems.at[1, i])
        for i, dst in enumerate((a_out, b_out, c_out))
    ]
    for copy in coming:
        copy.start()
    for came, goes in zip(coming, going):
        came.wait()
        goes.start()
    for copy in going:
        copy.wait()


def on_device(q_pre, k_pre, values, out_grad, q_gain, k_gain, selected):
    width_dev = q_pre.shape[1]
    width_all = float(width_dev * lax.axis_size("head"))
    vmem = pl.BlockSpec(memory_space=pltpu.VMEM)
    dma = pltpu.SemaphoreType.DMA
    pairs = NZ * NP
    scratch = [pltpu.VMEM((NH, TOK, HD), BF16) for _ in range(2 * NZ)] + [
        pltpu.VMEM((NP * NT, TILE, HD), BF16),
        pltpu.VMEM((NP * NT, TILE, HD), BF16),
        pltpu.VMEM((pairs, TILE, TOK), F32),
        pltpu.VMEM((pairs, TILE, TOK), F32),
        pltpu.VMEM((2 * pairs, TILE, HD), BF16),
        pltpu.VMEM((pairs, TOK, HD), BF16),
        pltpu.VMEM((2, 4, NH, TOK, HD), BF16),
        pltpu.VMEM((NX * 2 * NT, TILE, HD), BF16),
        pltpu.VMEM((NX * 2 * NT, TILE, HD), BF16),
        pltpu.VMEM((3, 2 * NT, TILE, HD), BF16),
        pltpu.VMEM((2, 2, 2 * NT, TILE, HD), BF16),
        pltpu.VMEM((NH, 2, TILE, TOK), F32),
        pltpu.VMEM((NH, 2, TILE, TOK), F32),
        pltpu.VMEM((NH, 2, 8, TOK), F32),
        pltpu.VMEM((NZ, 2, NP, TOK), F32),
        pltpu.VMEM((NZ, 2, NP, TOK), F32),
        pltpu.VMEM((16, TOK), F32),
        pltpu.VMEM((NZ, 16, TOK), F32),
        pltpu.VMEM((NZ * NH, 8, TOK), F32),
        pltpu.VMEM((NZ * NH, 8, TOK), F32),
        pltpu.VMEM((NH, TOK, HD), F32),
        pltpu.VMEM((NT, TILE, HD), F32),
        pltpu.VMEM((NT, TILE, HD), F32),
        pltpu.VMEM((TOK, 128), F32),
        pltpu.VMEM((TOK, 128), F32),
        pltpu.VMEM((2, 8, TOK), F32),
        pltpu.VMEM((2, NY - 1, 8, TOK), F32),
        pltpu.VMEM((NZ, 8, 128), jnp.int32),
        pltpu.SMEM((NZ, 8, 128), jnp.int32),
        dma((2, 16)),
        dma((2, 16)),
        dma((2, 2, 3)),
        dma((2, 2, 3)),
        dma((2, NX)),
        dma((2, NX)),
        dma((NZ,)),
        dma((NZ,)),
        dma((NZ - 1,)),
        dma((NZ - 1,)),
        dma((2, 4, 2)),
        dma((2, 4, 2)),
        dma((NX,)),
        dma((NX,)),
        dma((2, 2, 2, 2)),
        dma((2, 2, 2, 2)),
        dma((2, NY - 1)),
        dma((2, NY - 1)),
        dma((NZ - 1,)),
        dma((NZ - 1,)),
        dma((1,)),
    ]
    out = jax.ShapeDtypeStruct(q_pre.shape, BF16)
    results = pl.pallas_call(
        functools.partial(kernel, width_all),
        out_shape=(out, out, out),
        in_specs=[pl.BlockSpec(memory_space=pltpu.SMEM)] + [vmem] * 6,
        out_specs=(vmem, vmem, vmem),
        scratch_shapes=scratch,
        compiler_params=pltpu.CompilerParams(
            collective_id=0, has_side_effects=True, vmem_limit_bytes=60 * 2**20
        ),
        name="sparse_attention_backward",
    )(
        jnp.transpose(selected, (1, 0, 2)), q_pre, k_pre, values, out_grad, q_gain, k_gain
    )
    anywhere = pl.BlockSpec(memory_space=pl.ANY)
    return pl.pallas_call(
        place_results,
        out_shape=(out, out, out),
        in_specs=[anywhere] * 3,
        out_specs=(anywhere,) * 3,
        scratch_shapes=[pltpu.VMEM((3,) + q_pre.shape, BF16), dma((2, 3))],
        name="place_results",
    )(*results)


def solution(mesh):
    placed = (
        P("ctx", "head"),
        P("ctx", "head"),
        P("ctx", "head"),
        P("ctx", "head"),
        P("head"),
        P("head"),
        P("ctx", "head", None),
    )
    return jax.shard_map(
        on_device,
        mesh=mesh,
        in_specs=placed,
        out_specs=(P("ctx", "head"), P("ctx", "head"), P("ctx", "head")),
        check_vma=False,
    )
```

```python
import functools
import math

import jax
import jax.numpy as jnp
from jax import lax
from jax.experimental import pallas as pl
from jax.experimental.pallas import tpu as pltpu
from jax.sharding import PartitionSpec as P

HD = 128
TILE = 128
NH = 5
REM = 7
NT = 2 * NH
NZ = 8
NP = 8
NX = 4
NY = 4
TOK = 2 * TILE
EPS = 1e-6
FACTOR = 1.0 / math.sqrt(HD)
MESH = pl.DeviceIdType.MESH
F32 = jnp.float32
BF16 = jnp.bfloat16


def dot_nt(a, b):
    return lax.dot_general(a, b, (((1,), (1,)), ((), ())), preferred_element_type=F32)


def dot_nn(a, b):
    return lax.dot_general(a, b, (((1,), (0,)), ((), ())), preferred_element_type=F32)


def dot_tn(a, b):
    return lax.dot_general(a, b, (((0,), (0,)), ((), ())), preferred_element_type=F32)


def fold_rows(array, op):
    parts = [array[8 * i : 8 * i + 8] for i in range(array.shape[0] // 8)]
    while len(parts) > 1:
        parts = [op(parts[i], parts[i + 1]) for i in range(0, len(parts), 2)]
    return parts[0]


def kernel(width_all, *refs):
    sel, q_in, k_in, v_in, g_in, q_gain, k_gain, dq_out, dk_out, dv_out = refs[:10]
    scratch = list(refs[10:])
    g_bufs = [scratch.pop(0) for _ in range(NZ)]
    q_bufs = [scratch.pop(0) for _ in range(NZ)]
    moving = (g_bufs, q_bufs)
    (
        v_all,
        k_all,
        s_all,
        dp_all,
        kv_terms,
        q_terms,
        back_z,
        core_out,
        core_in,
        x_out,
        x_in,
        s_near,
        dp_near,
        near_stats,
        stat_out,
        stat_in,
        reply_out,
        reply_in,
        lse_ref,
        delta_ref,
        dq_wide,
        dk_sum,
        dv_sum,
        q_scale_ref,
        k_scale_ref,
        y_out,
        y_in,
        req_v,
        req_s,
        zf_send,
        zf_recv,
        xg_send,
        xg_recv,
        cg_send,
        cg_recv,
        st_send,
        st_recv,
        rp_send,
        rp_recv,
        zb_send,
        zb_recv,
        cb_send,
        cb_recv,
        xb_send,
        xb_recv,
        y_send,
        y_recv,
        rq_send,
        rq_recv,
        here_sem,
    ) = scratch
    fixed = (v_all, k_all)

    me = lax.axis_index("ctx")
    group = lax.axis_index("head")
    z = me // NP
    x = lax.rem(me, NP) // 2
    core = lax.rem(me, 2)

    def along_z(o):
        return {"ctx": lax.rem(z + o, NZ) * NP + lax.rem(me, NP), "head": group}

    def along_x(o):
        return {"ctx": z * NP + lax.rem(x + o, NX) * 2 + core, "head": group}

    def along_y(o):
        return {"ctx": me, "head": lax.rem(group + o, NY)}

    other_core = {"ctx": z * NP + x * 2 + (1 - core), "head": group}
    z_next = (along_z(1), along_z(NZ - 1))
    x_next = (along_x(1), along_x(NX - 1))

    barrier = pltpu.get_barrier_semaphore()
    peers = [along_z(o) for o in range(1, NZ)] + [along_y(o) for o in range(1, NY)]
    peers += [x_next[0], x_next[1], other_core]
    for peer in peers:
        pl.semaphore_signal(barrier, inc=1, device_id=peer, device_id_type=MESH)

    def remote(src, dst, send, recv, to):
        return pltpu.make_async_remote_copy(
            src_ref=src,
            dst_ref=dst,
            send_sem=send,
            recv_sem=recv,
            device_id=to,
            device_id_type=MESH,
        )

    for h in range(NH):
        cols = slice(h * HD, (h + 1) * HD)
        g_bufs[0][h] = g_in[:, cols]
        for t in range(2):
            v_all[t * NH + h] = v_in[t * TILE : (t + 1) * TILE, cols]
    lane = lax.broadcasted_iota(jnp.int32, (8, 128), 1)
    wanted = jnp.full((8, 128), -1, jnp.int32)
    for h in range(NH):
        for c in range(REM):
            tile = sel[h, 0, c]
            wanted = jnp.where(lane == (tile >> 1), (tile & 1) * NH + h, wanted)
    req_v[0] = wanted

    def squares(ref):
        wide = ref[...].astype(F32)
        return jnp.sum(wide * wide, axis=1, keepdims=True)

    lanes_tok = lax.broadcasted_iota(jnp.int32, (TOK, 128), 1)

    def as_rows(first, second):
        both = jnp.where(lanes_tok == 0, first, jnp.where(lanes_tok == 1, second, 0.0))
        return jnp.transpose(both)[:8]

    def as_columns(rows):
        tall = jnp.transpose(jnp.concatenate([rows, jnp.zeros((120, TOK), F32)], axis=0))
        return tall[:, 0:1], tall[:, 1:2]

    def y_copy(n, p):
        return remote(
            y_out.at[n], y_in.at[n, p - 1], y_send.at[n, p - 1], y_recv.at[n, p - 1], along_y(p)
        )

    def y_start(n):
        for p in range(1, NY):
            y_copy(n, p).start()

    def y_total(n):
        for p in range(1, NY):
            y_copy(n, p).wait_recv()
        return (y_out[n] + y_in[n, 0]) + (y_in[n, 1] + y_in[n, 2])

    y_out[0] = as_rows(squares(q_in), squares(k_in))
    pl.semaphore_wait(barrier, len(peers))

    def req_copy(o):
        return remote(
            req_v.at[0], req_v.at[NZ - o], rq_send.at[o - 1], rq_recv.at[o - 1], along_z(o)
        )

    def zf_copy(d, hop, kind, t):
        source = (NZ + 1 - hop) % NZ if d == 0 else hop - 1
        target = NZ - hop if d == 0 else hop
        at = ((hop - 1) * 2 + kind) * 2 + t
        rows = pl.ds(t * TILE, TILE)
        return remote(
            moving[kind][source].at[:, rows],
            moving[kind][target].at[:, rows],
            zf_send.at[d, at],
            zf_recv.at[d, at],
            z_next[d],
        )

    def xg_copy(kind, d, n):
        if n < 2:
            src, dst = n * NH, (6 if d == 0 else 2) * NT + n * NH
        else:
            src = (6 if d == 0 else 2) * NT + d * NH
            dst = 4 * NT + d * NH
        return remote(
            fixed[kind].at[pl.ds(src, NH)],
            fixed[kind].at[pl.ds(dst, NH)],
            xg_send.at[kind, d, n],
            xg_recv.at[kind, d, n],
            x_next[d],
        )

    def cg_copy(kind, dx):
        return remote(
            fixed[kind].at[pl.ds(2 * dx * NT, NT)],
            fixed[kind].at[pl.ds((2 * dx + 1) * NT, NT)],
            cg_send.at[kind, dx],
            cg_recv.at[kind, dx],
            other_core,
        )

    for t in range(2):
        for d in range(2):
            zf_copy(d, 1, 0, t).start()
    y_start(0)
    for t in range(2):
        for d in range(2):
            xg_copy(0, d, t).start()
    for o in range(1, NZ):
        req_copy(o).start()
    cg_copy(0, 0).start()

    total = y_total(0)
    q_scale, k_scale = as_columns(lax.rsqrt(total / width_all + EPS))
    q_scale_ref[...] = jnp.broadcast_to(q_scale, (TOK, 128))
    k_scale_ref[...] = jnp.broadcast_to(k_scale, (TOK, 128))

    def gain(ref, h):
        return ref[h * HD : (h + 1) * HD].reshape(1, HD)

    for t in range(2):
        rows = slice(t * TILE, (t + 1) * TILE)
        for h in range(NH):
            cols = slice(h * HD, (h + 1) * HD)
            q_bufs[0][h, rows] = (
                q_in[rows, cols].astype(F32) * q_scale_ref[rows] * gain(q_gain, h)
            ).astype(BF16)
            k_all[t * NH + h] = (
                k_in[rows, cols].astype(F32) * k_scale_ref[rows] * gain(k_gain, h)
            ).astype(BF16)
        for d in range(2):
            zf_copy(d, 1, 1, t).start()
            xg_copy(1, d, t).start()
    cg_copy(1, 0).start()

    for o in range(1, NZ):
        req_copy(o).wait_recv()
    table = pltpu.make_async_copy(req_v, req_s, here_sem.at[0])
    table.start()
    table.wait()

    def code_of(r, place):
        dx, other = place // 2, lax.rem(place, 2)
        lane_at = z * NP + lax.rem(x + dx, NX) * 2 + lax.rem(core + other, 2)
        return req_s[r, 0, lane_at]

    def row_stats(s, dp, top):
        e = jnp.exp(s - top)
        return fold_rows(e, jnp.add), fold_rows(e * dp, jnp.add)

    def near_scores(h, carry):
        tops = []
        for t in range(2):
            s = dot_nt(k_all[t * NH + h], q_bufs[0][h]) * FACTOR
            s_near[h, t] = s
            dp_near[h, t] = dot_nt(v_all[t * NH + h], g_bufs[0][h])
            tops.append(fold_rows(s, jnp.maximum))
        top = jnp.max(jnp.maximum(tops[0], tops[1]), axis=0, keepdims=True)
        first = row_stats(s_near[h, 0], dp_near[h, 0], top)
        second = row_stats(s_near[h, 1], dp_near[h, 1], top)
        mass = jnp.sum(first[0] + second[0], axis=0, keepdims=True)
        drift = jnp.sum(first[1] + second[1], axis=0, keepdims=True)
        near_stats[h, 0] = jnp.broadcast_to(top + jnp.log(mass), (8, TOK))
        near_stats[h, 1] = jnp.broadcast_to(drift / mass, (8, TOK))
        return carry

    def st_copy(r):
        return remote(
            stat_out.at[r], stat_in.at[(NZ - r) % NZ], st_send.at[r], st_recv.at[r], along_z(r)
        )

    sub = lax.broadcasted_iota(jnp.int32, (8, TOK), 0)

    def gradient_scores(r):
        def one(i, carry):
            for half in range(2):
                place = 2 * i + half
                code = jnp.maximum(code_of(r, place), 0)
                dp_all[r * NP + place] = dot_nt(
                    v_all[place * NT + code], g_bufs[r][lax.rem(code, NH)]
                )
            return carry

        lax.fori_loop(0, NP // 2, one, 0)

    def scores(r, with_dp=True):
        def one(i, carry):
            lse8, delta8 = carry
            for half in range(2):
                place = 2 * i + half
                code = jnp.maximum(code_of(r, place), 0)
                head = lax.rem(code, NH)
                s = dot_nt(k_all[place * NT + code], q_bufs[r][head]) * FACTOR
                if with_dp:
                    dp = dot_nt(v_all[place * NT + code], g_bufs[r][head])
                    dp_all[r * NP + place] = dp
                else:
                    dp = dp_all[r * NP + place]
                s_all[r * NP + place] = s
                top = jnp.max(fold_rows(s, jnp.maximum), axis=0, keepdims=True)
                mass, drift = row_stats(s, dp, top)
                mass = jnp.sum(mass, axis=0, keepdims=True)
                drift = jnp.sum(drift, axis=0, keepdims=True)
                lse8 = jnp.where(sub == place, top + jnp.log(mass), lse8)
                delta8 = jnp.where(sub == place, drift / mass, delta8)
            return lse8, delta8

        zero = jnp.zeros((8, TOK), F32)
        lse8, delta8 = lax.fori_loop(0, NP // 2, one, (zero, zero))
        if r == 0:
            stat_in[0, 0] = lse8
            stat_in[0, 1] = delta8
        else:
            stat_out[r, 0] = lse8
            stat_out[r, 1] = delta8
            st_copy(r).start()

    def forward(hop, kind):
        for t in range(2):
            for d in range(2):
                if hop < 4 or t == d:
                    zf_copy(d, hop, kind, t).wait_recv()
                if hop < 3 or (hop == 3 and t == d):
                    zf_copy(d, hop + 1, kind, t).start()

    def plane_first(kind):
        for t in range(2):
            for d in range(2):
                xg_copy(kind, d, t).wait_recv()
                if t == d:
                    xg_copy(kind, d, 2).start()
        cg_copy(kind, 1).start()
        cg_copy(kind, 3).start()

    def plane_second(kind):
        for d in range(2):
            xg_copy(kind, d, 2).wait_recv()
        cg_copy(kind, 2).start()

    forward(1, 0)
    plane_first(0)
    lax.fori_loop(0, NH, near_scores, 0)
    forward(1, 1)
    plane_first(1)
    plane_second(0)
    forward(2, 0)
    plane_second(1)
    for kind in range(2):
        for dx in range(NX):
            cg_copy(kind, dx).wait_recv()
    scores(0)
    forward(2, 1)
    scores(7)
    scores(1)
    forward(3, 0)
    scores(6)
    scores(2)
    row_at = lax.broadcasted_iota(jnp.int32, (NZ * NP, TOK), 0)
    head_at = jnp.full((NZ * NP, TOK), -1, jnp.int32)
    for h in range(NH):
        for c in range(REM):
            owner = sel[h, 0, c] >> 1
            dz = (owner // NP - z + NZ) & (NZ - 1)
            dx = ((owner & (NP - 1)) // 2 - x + NX) & (NX - 1)
            place = dx * 2 + ((owner + core) & 1)
            head_at = jnp.where(row_at == dz * NP + place, h, head_at)
    forward(3, 1)
    scores(5)
    forward(4, 0)
    scores(3)
    gradient_scores(4)
    forward(4, 1)
    scores(4, with_dp=False)

    for r in range(1, NZ):
        st_copy(r).wait_recv()
    pair_lse = jnp.concatenate([stat_in[r, 0] for r in range(NZ)], axis=0)
    pair_delta = jnp.concatenate([stat_in[r, 1] for r in range(NZ)], axis=0)
    for h in range(NH):
        mine = head_at == h
        near_lse, near_delta = near_stats[h, 0, :1], near_stats[h, 1, :1]
        top = jnp.max(jnp.where(mine, pair_lse, -3e38), axis=0, keepdims=True)
        top = jnp.maximum(top, near_lse)
        weight = jnp.where(mine, jnp.exp(pair_lse - top), 0.0)
        near_weight = jnp.exp(near_lse - top)
        whole = jnp.sum(weight, axis=0, keepdims=True) + near_weight
        drift = jnp.where(mine, weight * pair_delta, 0.0)
        drift = jnp.sum(drift, axis=0, keepdims=True) + near_weight * near_delta
        reply_out[pl.ds(h, 1)] = top + jnp.log(whole)
        reply_out[pl.ds(8 + h, 1)] = drift / whole

    def rp_copy(o):
        return remote(
            reply_out, reply_in.at[NZ - o], rp_send.at[o - 1], rp_recv.at[o - 1], along_z(o)
        )

    for o in (4, 3, 5, 2, 6, 1, 7):
        rp_copy(o).start()
    reply_in[0] = reply_out[...]

    for o in range(1, NZ):
        req_copy(o).wait_send()
    for hop in range(1, 5):
        for kind in range(2):
            for t in range(2):
                for d in range(2):
                    if hop < 4 or t == d:
                        zf_copy(d, hop, kind, t).wait_send()
    for kind in range(2):
        for d in range(2):
            for n in range(3):
                xg_copy(kind, d, n).wait_send()
        for dx in range(NX):
            cg_copy(kind, dx).wait_send()

    for o in range(1, NZ):
        rp_copy(o).wait_recv()
    for r in range(NZ):
        for h in range(NH):
            lse_ref[r * NH + h] = jnp.broadcast_to(reply_in[r, h : h + 1], (8, TOK))
            delta_ref[r * NH + h] = jnp.broadcast_to(reply_in[r, 8 + h : 9 + h], (8, TOK))

    def term(r, place):
        pair = r * NP + place
        asked = code_of(r, place)
        code = jnp.maximum(asked, 0)
        head = lax.rem(code, NH)
        probs = jnp.exp(s_all[pair] - lse_ref[r * NH + head][:1])
        probs = jnp.where(asked >= 0, probs, 0.0)
        ds = (probs * (dp_all[pair] - delta_ref[r * NH + head][:1]) * FACTOR).astype(BF16)
        dv = dot_nn(probs.astype(BF16), g_bufs[r][head])
        dk = dot_nn(ds, q_bufs[r][head])
        dq = dot_tn(ds, k_all[place * NT + code])
        kv_terms[2 * pair] = dv.astype(BF16)
        kv_terms[2 * pair + 1] = dk.astype(BF16)
        q_terms[pair] = dq.astype(BF16)

    zero_tile = jnp.zeros((TILE, HD), BF16)

    def tree(parts):
        while len(parts) > 1:
            parts = [parts[i] + parts[i + 1] for i in range(0, len(parts), 2)]
        return parts[0].astype(F32)

    def key_sum(place, kind, block):
        return tree(
            [
                jnp.where(
                    code_of(r, place) == block, kv_terms[2 * (r * NP + place) + kind], zero_tile
                )
                for r in range(NZ)
            ]
        )

    def query_sum(r, t, h):
        rows = slice(t * TILE, (t + 1) * TILE)
        return tree(
            [
                jnp.where(
                    lax.rem(jnp.maximum(code_of(r, place), 0), NH) == h,
                    q_terms[r * NP + place, rows],
                    zero_tile,
                )
                for place in range(NP)
            ]
        )

    def cb_copy(dx):
        part = pl.ds(dx * 2 * NT, 2 * NT)
        return remote(
            core_out.at[part], core_in.at[part], cb_send.at[dx], cb_recv.at[dx], other_core
        )

    def to_core(dx):
        def one(block, carry):
            for kind in range(2):
                acc = key_sum(2 * dx + 1, kind, block)
                core_out[dx * 2 * NT + kind * NT + block] = acc.astype(BF16)
            return carry

        lax.fori_loop(0, NT, one, 0)
        cb_copy(dx).start()

    def chip_sum(dx, kind, block):
        near = core_in[dx * 2 * NT + kind * NT + block].astype(F32)
        return key_sum(2 * dx, kind, block) + near

    def xb_copy(level, d, kind, t):
        dx = 2 if level == 2 else (1 if d == 0 else 3)
        part = pl.ds(kind * NT + t * NH, NH)
        return remote(
            x_out.at[dx - 1, part],
            x_in.at[level - 1, d, part],
            xb_send.at[level - 1, d, kind, t],
            xb_recv.at[level - 1, d, kind, t],
            x_next[d],
        )

    def x_pass(level, d, t):
        dx = 2 if level == 2 else (1 if d == 0 else 3)
        chained = level == 1 and t == d
        for kind in range(2):
            if chained:
                xb_copy(2, d, kind, t).wait_recv()

            def one(b, carry):
                block = t * NH + b
                acc = chip_sum(dx, kind, block)
                if chained:
                    acc += x_in[1, d, kind * NT + block].astype(F32)
                x_out[dx - 1, kind * NT + block] = acc.astype(BF16)
                return carry

            lax.fori_loop(0, NH, one, 0)
            xb_copy(level, d, kind, t).start()

    def zb_copy(d, level, t):
        r = level if d == 0 else NZ - level
        rows = pl.ds(t * TILE, TILE)
        return remote(
            q_bufs[r].at[:, rows],
            back_z.at[d, level - 1, :, rows],
            zb_send.at[d, level - 1, t],
            zb_recv.at[d, level - 1, t],
            z_next[d],
        )

    def z_pass(d, level):
        r = level if d == 0 else NZ - level
        for t in (1 - d, d) if level == 3 else ((d,) if level == 4 else (0, 1)):
            chained = level < 3 or (level == 3 and t == d)
            rows = slice(t * TILE, (t + 1) * TILE)
            if chained:
                zb_copy(d, level + 1, t).wait_recv()

            def one(h, carry):
                acc = query_sum(r, t, h)
                if chained:
                    acc += back_z[d, level, h, rows].astype(F32)
                q_bufs[r][h, rows] = acc.astype(BF16)
                return carry

            lax.fori_loop(0, NH, one, 0)
            zb_copy(d, level, t).start()

    def rest_terms(r):
        def one(i, carry):
            for half in range(2):
                place = 2 * i + half
                term(r, place + jnp.where(i >= 2, 2, 0))
            return carry

        lax.fori_loop(0, NP // 2 - 1, one, 0)

    def opposite_terms(r):
        term(r, 4)
        term(r, 5)

    opposite_terms(4)
    rest_terms(4)
    z_pass(0, 4)
    z_pass(1, 4)
    for r in (5, 3, 6, 2, 7, 1, 0):
        opposite_terms(r)
    to_core(2)
    rest_terms(5)
    z_pass(1, 3)
    rest_terms(3)
    z_pass(0, 3)
    cb_copy(2).wait_recv()
    x_pass(2, 0, 0)
    x_pass(2, 1, 1)
    for r in (6, 2, 7, 1, 0):
        rest_terms(r)
    to_core(1)
    to_core(3)
    z_pass(1, 2)
    z_pass(0, 2)
    cb_copy(1).wait_recv()
    x_pass(1, 0, 1)
    cb_copy(3).wait_recv()
    x_pass(1, 1, 0)
    x_pass(1, 0, 0)
    x_pass(1, 1, 1)
    to_core(0)

    def near_terms(h, carry):
        dq = jnp.zeros((TOK, HD), F32)
        lse, delta = lse_ref[h][:1], delta_ref[h][:1]
        for t in range(2):
            probs = jnp.exp(s_near[h, t] - lse)
            ds = (probs * (dp_near[h, t] - delta) * FACTOR).astype(BF16)
            dv_sum[t * NH + h] = dot_nn(probs.astype(BF16), g_bufs[0][h])
            dk_sum[t * NH + h] = dot_nn(ds, q_bufs[0][h])
            dq += dot_tn(ds, k_all[t * NH + h])
        dq_wide[h] = dq
        for t in range(2):
            dq_wide[h, t * TILE : (t + 1) * TILE] += query_sum(0, t, h)
        return carry

    lax.fori_loop(0, NH, near_terms, 0)
    z_pass(1, 1)
    z_pass(0, 1)
    cb_copy(0).wait_recv()

    def own_sum(block, carry):
        dv_sum[block] += chip_sum(0, 0, block)
        dk_sum[block] += chip_sum(0, 1, block)
        return carry

    lax.fori_loop(0, NT, own_sum, 0)

    for t in range(2):
        for d in range(2):
            zb_copy(d, 1, t).wait_recv()
    dots = jnp.zeros((TOK, HD), F32)
    for h in range(NH):
        cols = slice(h * HD, (h + 1) * HD)
        dq = dq_wide[h] + back_z[0, 0, h].astype(F32) + back_z[1, 0, h].astype(F32)
        dq_wide[h] = dq
        dots += gain(q_gain, h) * dq * q_in[:, cols].astype(F32)
    y_out[1] = as_rows(jnp.sum(dots, axis=1, keepdims=True), 0.0)
    y_start(1)

    for t in range(2):
        for d in range(2):
            for kind in range(2):
                xb_copy(1, d, kind, t).wait_recv()
    columns = []
    for t in range(2):
        rows = slice(t * TILE, (t + 1) * TILE)
        dots = jnp.zeros((TILE, HD), F32)
        for h in range(NH):
            cols = slice(h * HD, (h + 1) * HD)
            b = t * NH + h
            dk = dk_sum[b] + x_in[0, 0, NT + b].astype(F32) + x_in[0, 1, NT + b].astype(F32)
            dk_sum[b] = dk
            dots += gain(k_gain, h) * dk * k_in[rows, cols].astype(F32)
        columns.append(jnp.sum(dots, axis=1, keepdims=True))
    y_out[2] = as_rows(jnp.concatenate(columns, axis=0), 0.0)
    y_start(2)

    def finish(wide, gains, grad, scale, dot_mean):
        return (scale * gains * grad - wide * (scale * scale * scale) * dot_mean).astype(BF16)

    for t in range(2):
        rows = slice(t * TILE, (t + 1) * TILE)
        for h in range(NH):
            b = t * NH + h
            dv = dv_sum[b] + x_in[0, 0, b].astype(F32) + x_in[0, 1, b].astype(F32)
            dv_out[rows, h * HD : (h + 1) * HD] = dv.astype(BF16)
    q_dot, _ = as_columns(y_total(1) / width_all)
    for h in range(NH):
        cols = slice(h * HD, (h + 1) * HD)
        dq_out[:, cols] = finish(
            q_in[:, cols].astype(F32), gain(q_gain, h), dq_wide[h], q_scale_ref[...], q_dot
        )
    k_dot, _ = as_columns(y_total(2) / width_all)
    for t in range(2):
        rows = slice(t * TILE, (t + 1) * TILE)
        for h in range(NH):
            cols = slice(h * HD, (h + 1) * HD)
            dk_out[rows, cols] = finish(
                k_in[rows, cols].astype(F32),
                gain(k_gain, h),
                dk_sum[t * NH + h],
                k_scale_ref[rows],
                k_dot[rows],
            )

    for n in range(3):
        for p in range(1, NY):
            y_copy(n, p).wait_send()
    for r in range(1, NZ):
        st_copy(r).wait_send()
        rp_copy(r).wait_send()
    for dx in range(NX):
        cb_copy(dx).wait_send()
    for t in range(2):
        for d in range(2):
            for level in range(1, 5):
                if level < 4 or t == d:
                    zb_copy(d, level, t).wait_send()
            for kind in range(2):
                xb_copy(1, d, kind, t).wait_send()
                if t == d:
                    xb_copy(2, d, kind, t).wait_send()


def place_results(a, b, c, a_out, b_out, c_out, held, sems):
    coming = [
        pltpu.make_async_copy(src, held.at[i], sems.at[0, i]) for i, src in enumerate((a, b, c))
    ]
    going = [
        pltpu.make_async_copy(held.at[i], dst, sems.at[1, i])
        for i, dst in enumerate((a_out, b_out, c_out))
    ]
    for copy in coming:
        copy.start()
    for came, goes in zip(coming, going):
        came.wait()
        goes.start()
    for copy in going:
        copy.wait()


def on_device(q_pre, k_pre, values, out_grad, q_gain, k_gain, selected):
    width_dev = q_pre.shape[1]
    width_all = float(width_dev * lax.axis_size("head"))
    vmem = pl.BlockSpec(memory_space=pltpu.VMEM)
    dma = pltpu.SemaphoreType.DMA
    pairs = NZ * NP
    scratch = [pltpu.VMEM((NH, TOK, HD), BF16) for _ in range(2 * NZ)] + [
        pltpu.VMEM((NP * NT, TILE, HD), BF16),
        pltpu.VMEM((NP * NT, TILE, HD), BF16),
        pltpu.VMEM((pairs, TILE, TOK), F32),
        pltpu.VMEM((pairs, TILE, TOK), F32),
        pltpu.VMEM((2 * pairs, TILE, HD), BF16),
        pltpu.VMEM((pairs, TOK, HD), BF16),
        pltpu.VMEM((2, 4, NH, TOK, HD), BF16),
        pltpu.VMEM((NX * 2 * NT, TILE, HD), BF16),
        pltpu.VMEM((NX * 2 * NT, TILE, HD), BF16),
        pltpu.VMEM((3, 2 * NT, TILE, HD), BF16),
        pltpu.VMEM((2, 2, 2 * NT, TILE, HD), BF16),
        pltpu.VMEM((NH, 2, TILE, TOK), F32),
        pltpu.VMEM((NH, 2, TILE, TOK), F32),
        pltpu.VMEM((NH, 2, 8, TOK), F32),
        pltpu.VMEM((NZ, 2, NP, TOK), F32),
        pltpu.VMEM((NZ, 2, NP, TOK), F32),
        pltpu.VMEM((16, TOK), F32),
        pltpu.VMEM((NZ, 16, TOK), F32),
        pltpu.VMEM((NZ * NH, 8, TOK), F32),
        pltpu.VMEM((NZ * NH, 8, TOK), F32),
        pltpu.VMEM((NH, TOK, HD), F32),
        pltpu.VMEM((NT, TILE, HD), F32),
        pltpu.VMEM((NT, TILE, HD), F32),
        pltpu.VMEM((TOK, 128), F32),
        pltpu.VMEM((TOK, 128), F32),
        pltpu.VMEM((3, 8, TOK), F32),
        pltpu.VMEM((3, NY - 1, 8, TOK), F32),
        pltpu.VMEM((NZ, 8, 128), jnp.int32),
        pltpu.SMEM((NZ, 8, 128), jnp.int32),
        dma((2, 16)),
        dma((2, 16)),
        dma((2, 2, 3)),
        dma((2, 2, 3)),
        dma((2, NX)),
        dma((2, NX)),
        dma((NZ,)),
        dma((NZ,)),
        dma((NZ - 1,)),
        dma((NZ - 1,)),
        dma((2, 4, 2)),
        dma((2, 4, 2)),
        dma((NX,)),
        dma((NX,)),
        dma((2, 2, 2, 2)),
        dma((2, 2, 2, 2)),
        dma((3, NY - 1)),
        dma((3, NY - 1)),
        dma((NZ - 1,)),
        dma((NZ - 1,)),
        dma((1,)),
    ]
    out = jax.ShapeDtypeStruct(q_pre.shape, BF16)
    results = pl.pallas_call(
        functools.partial(kernel, width_all),
        out_shape=(out, out, out),
        in_specs=[pl.BlockSpec(memory_space=pltpu.SMEM)] + [vmem] * 6,
        out_specs=(vmem, vmem, vmem),
        scratch_shapes=scratch,
        compiler_params=pltpu.CompilerParams(
            collective_id=0, has_side_effects=True, vmem_limit_bytes=60 * 2**20
        ),
        name="sparse_attention_backward",
    )(
        jnp.transpose(selected, (1, 0, 2)), q_pre, k_pre, values, out_grad, q_gain, k_gain
    )
    anywhere = pl.BlockSpec(memory_space=pl.ANY)
    return pl.pallas_call(
        place_results,
        out_shape=(out, out, out),
        in_specs=[anywhere] * 3,
        out_specs=(anywhere,) * 3,
        scratch_shapes=[pltpu.VMEM((3,) + q_pre.shape, BF16), dma((2, 3))],
        name="place_results",
    )(*results)


def solution(mesh):
    placed = (
        P("ctx", "head"),
        P("ctx", "head"),
        P("ctx", "head"),
        P("ctx", "head"),
        P("head"),
        P("head"),
        P("ctx", "head", None),
    )
    return jax.shard_map(
        on_device,
        mesh=mesh,
        in_specs=placed,
        out_specs=(P("ctx", "head"), P("ctx", "head"), P("ctx", "head")),
        check_vma=False,
    )
```

```python
import functools
import math

import jax
import jax.numpy as jnp
from jax import lax
from jax.experimental import pallas as pl
from jax.experimental.pallas import tpu as pltpu
from jax.sharding import PartitionSpec as P

HD = 128
TILE = 128
NH = 5
REM = 7
NT = 2 * NH
NZ = 8
NP = 8
NX = 4
NY = 4
TOK = 2 * TILE
EPS = 1e-6
FACTOR = 1.0 / math.sqrt(HD)
MESH = pl.DeviceIdType.MESH
F32 = jnp.float32
BF16 = jnp.bfloat16


def dot_nt(a, b):
    return lax.dot_general(a, b, (((1,), (1,)), ((), ())), preferred_element_type=F32)


def dot_nn(a, b):
    return lax.dot_general(a, b, (((1,), (0,)), ((), ())), preferred_element_type=F32)


def dot_tn(a, b):
    return lax.dot_general(a, b, (((0,), (0,)), ((), ())), preferred_element_type=F32)


def fold_rows(array, op):
    parts = [array[8 * i : 8 * i + 8] for i in range(array.shape[0] // 8)]
    while len(parts) > 1:
        parts = [op(parts[i], parts[i + 1]) for i in range(0, len(parts), 2)]
    return parts[0]


def kernel(width_all, *refs):
    sel, q_in, k_in, v_in, g_in, q_gain, k_gain, dq_out, dk_out, dv_out = refs[:10]
    scratch = list(refs[10:])
    g_bufs = [scratch.pop(0) for _ in range(NZ)]
    q_bufs = [scratch.pop(0) for _ in range(NZ)]
    moving = (g_bufs, q_bufs)
    (
        v_all,
        k_all,
        s_all,
        dp_all,
        kv_terms,
        q_terms,
        back_z,
        core_out,
        core_in,
        x_out,
        x_in,
        s_near,
        dp_near,
        near_stats,
        stat_out,
        stat_in,
        reply_out,
        reply_in,
        lse_ref,
        delta_ref,
        dq_wide,
        dq_rows,
        dk_sum,
        dv_sum,
        q_scale_ref,
        k_scale_ref,
        y_out,
        y_in,
        req_v,
        req_s,
        zf_send,
        zf_recv,
        xg_send,
        xg_recv,
        cg_send,
        cg_recv,
        st_send,
        st_recv,
        rp_send,
        rp_recv,
        zb_send,
        zb_recv,
        cb_send,
        cb_recv,
        xb_send,
        xb_recv,
        y_send,
        y_recv,
        rq_send,
        rq_recv,
        here_sem,
    ) = scratch
    fixed = (v_all, k_all)

    me = lax.axis_index("ctx")
    group = lax.axis_index("head")
    z = me // NP
    x = lax.rem(me, NP) // 2
    core = lax.rem(me, 2)

    def along_z(o):
        return {"ctx": lax.rem(z + o, NZ) * NP + lax.rem(me, NP), "head": group}

    def along_x(o):
        return {"ctx": z * NP + lax.rem(x + o, NX) * 2 + core, "head": group}

    def along_y(o):
        return {"ctx": me, "head": lax.rem(group + o, NY)}

    other_core = {"ctx": z * NP + x * 2 + (1 - core), "head": group}
    z_next = (along_z(1), along_z(NZ - 1))
    x_next = (along_x(1), along_x(NX - 1))

    barrier = pltpu.get_barrier_semaphore()
    peers = [along_z(o) for o in range(1, NZ)] + [along_y(o) for o in range(1, NY)]
    peers += [x_next[0], x_next[1], other_core]
    for peer in peers:
        pl.semaphore_signal(barrier, inc=1, device_id=peer, device_id_type=MESH)

    def remote(src, dst, send, recv, to):
        return pltpu.make_async_remote_copy(
            src_ref=src,
            dst_ref=dst,
            send_sem=send,
            recv_sem=recv,
            device_id=to,
            device_id_type=MESH,
        )

    for h in range(NH):
        cols = slice(h * HD, (h + 1) * HD)
        g_bufs[0][h] = g_in[:, cols]
        for t in range(2):
            v_all[t * NH + h] = v_in[t * TILE : (t + 1) * TILE, cols]
    lane = lax.broadcasted_iota(jnp.int32, (8, 128), 1)
    wanted = jnp.full((8, 128), -1, jnp.int32)
    for h in range(NH):
        for c in range(REM):
            tile = sel[h, 0, c]
            wanted = jnp.where(lane == (tile >> 1), (tile & 1) * NH + h, wanted)
    req_v[0] = wanted

    def squares(ref):
        wide = ref[...].astype(F32)
        return jnp.sum(wide * wide, axis=1, keepdims=True)

    lanes_tok = lax.broadcasted_iota(jnp.int32, (TOK, 128), 1)

    def as_rows(first, second):
        both = jnp.where(lanes_tok == 0, first, jnp.where(lanes_tok == 1, second, 0.0))
        return jnp.transpose(both)[:8]

    def as_columns(rows):
        tall = jnp.transpose(jnp.concatenate([rows, jnp.zeros((120, TOK), F32)], axis=0))
        return tall[:, 0:1], tall[:, 1:2]

    def y_copy(n, p):
        return remote(
            y_out.at[n], y_in.at[n, p - 1], y_send.at[n, p - 1], y_recv.at[n, p - 1], along_y(p)
        )

    def y_start(n):
        for p in range(1, NY):
            y_copy(n, p).start()

    def y_total(n):
        for p in range(1, NY):
            y_copy(n, p).wait_recv()
        return (y_out[n] + y_in[n, 0]) + (y_in[n, 1] + y_in[n, 2])

    y_out[0] = as_rows(squares(q_in), squares(k_in))
    pl.semaphore_wait(barrier, len(peers))

    def req_copy(o):
        return remote(
            req_v.at[0], req_v.at[NZ - o], rq_send.at[o - 1], rq_recv.at[o - 1], along_z(o)
        )

    def zf_copy(d, hop, kind, t):
        source = (NZ + 1 - hop) % NZ if d == 0 else hop - 1
        target = NZ - hop if d == 0 else hop
        at = ((hop - 1) * 2 + kind) * 2 + t
        rows = pl.ds(t * TILE, TILE)
        return remote(
            moving[kind][source].at[:, rows],
            moving[kind][target].at[:, rows],
            zf_send.at[d, at],
            zf_recv.at[d, at],
            z_next[d],
        )

    def xg_copy(kind, d, n):
        if n < 2:
            src, dst = n * NH, (6 if d == 0 else 2) * NT + n * NH
        else:
            src = (6 if d == 0 else 2) * NT + d * NH
            dst = 4 * NT + d * NH
        return remote(
            fixed[kind].at[pl.ds(src, NH)],
            fixed[kind].at[pl.ds(dst, NH)],
            xg_send.at[kind, d, n],
            xg_recv.at[kind, d, n],
            x_next[d],
        )

    def cg_copy(kind, dx):
        return remote(
            fixed[kind].at[pl.ds(2 * dx * NT, NT)],
            fixed[kind].at[pl.ds((2 * dx + 1) * NT, NT)],
            cg_send.at[kind, dx],
            cg_recv.at[kind, dx],
            other_core,
        )

    for t in range(2):
        for d in range(2):
            zf_copy(d, 1, 0, t).start()
    y_start(0)
    for t in range(2):
        for d in range(2):
            xg_copy(0, d, t).start()
    for o in range(1, NZ):
        req_copy(o).start()
    cg_copy(0, 0).start()

    total = y_total(0)
    q_scale, k_scale = as_columns(lax.rsqrt(total / width_all + EPS))
    q_scale_ref[...] = jnp.broadcast_to(q_scale, (TOK, 128))
    k_scale_ref[...] = jnp.broadcast_to(k_scale, (TOK, 128))

    def gain(ref, h):
        return ref[h * HD : (h + 1) * HD].reshape(1, HD)

    for t in range(2):
        rows = slice(t * TILE, (t + 1) * TILE)
        for h in range(NH):
            cols = slice(h * HD, (h + 1) * HD)
            q_bufs[0][h, rows] = (
                q_in[rows, cols].astype(F32) * q_scale_ref[rows] * gain(q_gain, h)
            ).astype(BF16)
            k_all[t * NH + h] = (
                k_in[rows, cols].astype(F32) * k_scale_ref[rows] * gain(k_gain, h)
            ).astype(BF16)
        for d in range(2):
            zf_copy(d, 1, 1, t).start()
            xg_copy(1, d, t).start()
    cg_copy(1, 0).start()

    for o in range(1, NZ):
        req_copy(o).wait_recv()
    table = pltpu.make_async_copy(req_v, req_s, here_sem.at[0])
    table.start()
    table.wait()

    def code_of(r, place):
        dx, other = place // 2, lax.rem(place, 2)
        lane_at = z * NP + lax.rem(x + dx, NX) * 2 + lax.rem(core + other, 2)
        return req_s[r, 0, lane_at]

    def row_stats(s, dp, top):
        e = jnp.exp(s - top)
        return fold_rows(e, jnp.add), fold_rows(e * dp, jnp.add)

    def near_scores(h, carry):
        tops = []
        for t in range(2):
            s = dot_nt(k_all[t * NH + h], q_bufs[0][h]) * FACTOR
            s_near[h, t] = s
            dp_near[h, t] = dot_nt(v_all[t * NH + h], g_bufs[0][h])
            tops.append(fold_rows(s, jnp.maximum))
        top = jnp.max(jnp.maximum(tops[0], tops[1]), axis=0, keepdims=True)
        first = row_stats(s_near[h, 0], dp_near[h, 0], top)
        second = row_stats(s_near[h, 1], dp_near[h, 1], top)
        mass = jnp.sum(first[0] + second[0], axis=0, keepdims=True)
        drift = jnp.sum(first[1] + second[1], axis=0, keepdims=True)
        near_stats[h, 0] = jnp.broadcast_to(top + jnp.log(mass), (8, TOK))
        near_stats[h, 1] = jnp.broadcast_to(drift / mass, (8, TOK))
        return carry

    def st_copy(r):
        return remote(
            stat_out.at[r], stat_in.at[(NZ - r) % NZ], st_send.at[r], st_recv.at[r], along_z(r)
        )

    sub = lax.broadcasted_iota(jnp.int32, (8, TOK), 0)

    def gradient_scores(r):
        def one(i, carry):
            for half in range(2):
                place = 2 * i + half
                code = jnp.maximum(code_of(r, place), 0)
                dp_all[r * NP + place] = dot_nt(
                    v_all[place * NT + code], g_bufs[r][lax.rem(code, NH)]
                )
            return carry

        lax.fori_loop(0, NP // 2, one, 0)

    def scores(r, with_dp=True):
        def one(i, carry):
            lse8, delta8 = carry
            for half in range(2):
                place = 2 * i + half
                code = jnp.maximum(code_of(r, place), 0)
                head = lax.rem(code, NH)
                s = dot_nt(k_all[place * NT + code], q_bufs[r][head]) * FACTOR
                if with_dp:
                    dp = dot_nt(v_all[place * NT + code], g_bufs[r][head])
                    dp_all[r * NP + place] = dp
                else:
                    dp = dp_all[r * NP + place]
                s_all[r * NP + place] = s
                top = jnp.max(fold_rows(s, jnp.maximum), axis=0, keepdims=True)
                mass, drift = row_stats(s, dp, top)
                mass = jnp.sum(mass, axis=0, keepdims=True)
                drift = jnp.sum(drift, axis=0, keepdims=True)
                lse8 = jnp.where(sub == place, top + jnp.log(mass), lse8)
                delta8 = jnp.where(sub == place, drift / mass, delta8)
            return lse8, delta8

        zero = jnp.zeros((8, TOK), F32)
        lse8, delta8 = lax.fori_loop(0, NP // 2, one, (zero, zero))
        if r == 0:
            stat_in[0, 0] = lse8
            stat_in[0, 1] = delta8
        else:
            stat_out[r, 0] = lse8
            stat_out[r, 1] = delta8
            st_copy(r).start()

    def forward(hop, kind):
        for t in range(2):
            for d in range(2):
                if hop < 4 or t == d:
                    zf_copy(d, hop, kind, t).wait_recv()
                if hop < 3 or (hop == 3 and t == d):
                    zf_copy(d, hop + 1, kind, t).start()

    def plane_first(kind):
        for t in range(2):
            for d in range(2):
                xg_copy(kind, d, t).wait_recv()
                if t == d:
                    xg_copy(kind, d, 2).start()
        cg_copy(kind, 1).start()
        cg_copy(kind, 3).start()

    def plane_second(kind):
        for d in range(2):
            xg_copy(kind, d, 2).wait_recv()
        cg_copy(kind, 2).start()

    forward(1, 0)
    plane_first(0)
    lax.fori_loop(0, NH, near_scores, 0)
    forward(1, 1)
    plane_first(1)
    plane_second(0)
    forward(2, 0)
    plane_second(1)
    for kind in range(2):
        for dx in range(NX):
            cg_copy(kind, dx).wait_recv()
    scores(0)
    forward(2, 1)
    scores(7)
    scores(1)
    forward(3, 0)
    scores(6)
    scores(2)
    row_at = lax.broadcasted_iota(jnp.int32, (NZ * NP, TOK), 0)
    head_at = jnp.full((NZ * NP, TOK), -1, jnp.int32)
    for h in range(NH):
        for c in range(REM):
            owner = sel[h, 0, c] >> 1
            dz = (owner // NP - z + NZ) & (NZ - 1)
            dx = ((owner & (NP - 1)) // 2 - x + NX) & (NX - 1)
            place = dx * 2 + ((owner + core) & 1)
            head_at = jnp.where(row_at == dz * NP + place, h, head_at)
    forward(3, 1)
    scores(5)
    forward(4, 0)
    scores(3)
    gradient_scores(4)
    forward(4, 1)
    scores(4, with_dp=False)

    for r in range(1, NZ):
        st_copy(r).wait_recv()
    pair_lse = jnp.concatenate([stat_in[r, 0] for r in range(NZ)], axis=0)
    pair_delta = jnp.concatenate([stat_in[r, 1] for r in range(NZ)], axis=0)
    for h in range(NH):
        mine = head_at == h
        near_lse, near_delta = near_stats[h, 0, :1], near_stats[h, 1, :1]
        top = jnp.max(jnp.where(mine, pair_lse, -3e38), axis=0, keepdims=True)
        top = jnp.maximum(top, near_lse)
        weight = jnp.where(mine, jnp.exp(pair_lse - top), 0.0)
        near_weight = jnp.exp(near_lse - top)
        whole = jnp.sum(weight, axis=0, keepdims=True) + near_weight
        drift = jnp.where(mine, weight * pair_delta, 0.0)
        drift = jnp.sum(drift, axis=0, keepdims=True) + near_weight * near_delta
        reply_out[pl.ds(h, 1)] = top + jnp.log(whole)
        reply_out[pl.ds(8 + h, 1)] = drift / whole

    def rp_copy(o):
        return remote(
            reply_out, reply_in.at[NZ - o], rp_send.at[o - 1], rp_recv.at[o - 1], along_z(o)
        )

    for o in (4, 3, 5, 2, 6, 1, 7):
        rp_copy(o).start()
    reply_in[0] = reply_out[...]

    for o in range(1, NZ):
        req_copy(o).wait_send()
    for hop in range(1, 5):
        for kind in range(2):
            for t in range(2):
                for d in range(2):
                    if hop < 4 or t == d:
                        zf_copy(d, hop, kind, t).wait_send()
    for kind in range(2):
        for d in range(2):
            for n in range(3):
                xg_copy(kind, d, n).wait_send()
        for dx in range(NX):
            cg_copy(kind, dx).wait_send()

    for o in range(1, NZ):
        rp_copy(o).wait_recv()
    for r in range(NZ):
        for h in range(NH):
            lse_ref[r * NH + h] = jnp.broadcast_to(reply_in[r, h : h + 1], (8, TOK))
            delta_ref[r * NH + h] = jnp.broadcast_to(reply_in[r, 8 + h : 9 + h], (8, TOK))

    def term(r, place):
        pair = r * NP + place
        asked = code_of(r, place)
        code = jnp.maximum(asked, 0)
        head = lax.rem(code, NH)
        probs = jnp.exp(s_all[pair] - lse_ref[r * NH + head][:1])
        probs = jnp.where(asked >= 0, probs, 0.0)
        ds = (probs * (dp_all[pair] - delta_ref[r * NH + head][:1]) * FACTOR).astype(BF16)
        dv = dot_nn(probs.astype(BF16), g_bufs[r][head])
        dk = dot_nn(ds, q_bufs[r][head])
        dq = dot_tn(k_all[place * NT + code], ds)
        kv_terms[2 * pair] = dv.astype(BF16)
        kv_terms[2 * pair + 1] = dk.astype(BF16)
        q_terms[pair] = dq.astype(BF16)

    zero_tile = jnp.zeros((TILE, HD), BF16)

    def tree(parts):
        while len(parts) > 1:
            parts = [parts[i] + parts[i + 1] for i in range(0, len(parts), 2)]
        return parts[0].astype(F32)

    def key_sum(place, kind, block):
        return tree(
            [
                jnp.where(
                    code_of(r, place) == block, kv_terms[2 * (r * NP + place) + kind], zero_tile
                )
                for r in range(NZ)
            ]
        )

    def query_sum(r, t, h):
        cols = slice(t * TILE, (t + 1) * TILE)
        return tree(
            [
                jnp.where(
                    lax.rem(jnp.maximum(code_of(r, place), 0), NH) == h,
                    q_terms[r * NP + place, :, cols],
                    zero_tile,
                )
                for place in range(NP)
            ]
        )

    def cb_copy(dx):
        part = pl.ds(dx * 2 * NT, 2 * NT)
        return remote(
            core_out.at[part], core_in.at[part], cb_send.at[dx], cb_recv.at[dx], other_core
        )

    def to_core(dx):
        def one(block, carry):
            for kind in range(2):
                acc = key_sum(2 * dx + 1, kind, block)
                core_out[dx * 2 * NT + kind * NT + block] = acc.astype(BF16)
            return carry

        lax.fori_loop(0, NT, one, 0)
        cb_copy(dx).start()

    def chip_sum(dx, kind, block):
        near = core_in[dx * 2 * NT + kind * NT + block].astype(F32)
        return key_sum(2 * dx, kind, block) + near

    def xb_copy(level, d, kind, t):
        dx = 2 if level == 2 else (1 if d == 0 else 3)
        part = pl.ds(kind * NT + t * NH, NH)
        return remote(
            x_out.at[dx - 1, part],
            x_in.at[level - 1, d, part],
            xb_send.at[level - 1, d, kind, t],
            xb_recv.at[level - 1, d, kind, t],
            x_next[d],
        )

    def x_pass(level, d, t):
        dx = 2 if level == 2 else (1 if d == 0 else 3)
        chained = level == 1 and t == d
        for kind in range(2):
            if chained:
                xb_copy(2, d, kind, t).wait_recv()

            def one(b, carry):
                block = t * NH + b
                acc = chip_sum(dx, kind, block)
                if chained:
                    acc += x_in[1, d, kind * NT + block].astype(F32)
                x_out[dx - 1, kind * NT + block] = acc.astype(BF16)
                return carry

            lax.fori_loop(0, NH, one, 0)
            xb_copy(level, d, kind, t).start()

    def zb_copy(d, level, t):
        r = level if d == 0 else NZ - level
        rows = pl.ds(t * TILE, TILE)
        return remote(
            q_bufs[r].at[:, rows],
            back_z.at[d, level - 1, :, rows],
            zb_send.at[d, level - 1, t],
            zb_recv.at[d, level - 1, t],
            z_next[d],
        )

    def z_pass(d, level):
        r = level if d == 0 else NZ - level
        for t in (1 - d, d) if level == 3 else ((d,) if level == 4 else (0, 1)):
            chained = level < 3 or (level == 3 and t == d)
            rows = slice(t * TILE, (t + 1) * TILE)
            if chained:
                zb_copy(d, level + 1, t).wait_recv()

            def one(h, carry):
                acc = query_sum(r, t, h)
                if chained:
                    acc += back_z[d, level, h, rows].astype(F32)
                q_bufs[r][h, rows] = acc.astype(BF16)
                return carry

            lax.fori_loop(0, NH, one, 0)
            zb_copy(d, level, t).start()

    def rest_terms(r):
        def one(i, carry):
            for half in range(2):
                place = 2 * i + half
                term(r, place + jnp.where(i >= 2, 2, 0))
            return carry

        lax.fori_loop(0, NP // 2 - 1, one, 0)

    def opposite_terms(r):
        term(r, 4)
        term(r, 5)

    opposite_terms(4)
    rest_terms(4)
    z_pass(0, 4)
    z_pass(1, 4)
    for r in (5, 3, 6, 2, 7, 1, 0):
        opposite_terms(r)
    to_core(2)
    rest_terms(5)
    z_pass(1, 3)
    rest_terms(3)
    z_pass(0, 3)
    cb_copy(2).wait_recv()
    x_pass(2, 0, 0)
    x_pass(2, 1, 1)
    for r in (6, 2, 7, 1, 0):
        rest_terms(r)
    to_core(1)
    to_core(3)
    z_pass(1, 2)
    z_pass(0, 2)
    cb_copy(1).wait_recv()
    x_pass(1, 0, 1)
    cb_copy(3).wait_recv()
    x_pass(1, 1, 0)
    x_pass(1, 0, 0)
    x_pass(1, 1, 1)
    z_pass(1, 1)
    z_pass(0, 1)
    to_core(0)

    def near_terms(h, carry):
        dq = jnp.zeros((HD, TOK), F32)
        lse, delta = lse_ref[h][:1], delta_ref[h][:1]
        for t in range(2):
            probs = jnp.exp(s_near[h, t] - lse)
            ds = (probs * (dp_near[h, t] - delta) * FACTOR).astype(BF16)
            dv_sum[t * NH + h] = dot_nn(probs.astype(BF16), g_bufs[0][h])
            dk_sum[t * NH + h] = dot_nn(ds, q_bufs[0][h])
            dq += dot_tn(k_all[t * NH + h], ds)
        dq_wide[h] = dq
        for t in range(2):
            dq_wide[h, :, t * TILE : (t + 1) * TILE] += query_sum(0, t, h)
        return carry

    lax.fori_loop(0, NH, near_terms, 0)
    cb_copy(0).wait_recv()

    def own_sum(block, carry):
        dv_sum[block] += chip_sum(0, 0, block)
        dk_sum[block] += chip_sum(0, 1, block)
        return carry

    lax.fori_loop(0, NT, own_sum, 0)

    for t in range(2):
        for d in range(2):
            zb_copy(d, 1, t).wait_recv()
    dots = jnp.zeros((TOK, HD), F32)
    for h in range(NH):
        cols = slice(h * HD, (h + 1) * HD)
        for t in range(2):
            rows = slice(t * TILE, (t + 1) * TILE)
            came = back_z[0, 0, h, rows].astype(F32) + back_z[1, 0, h, rows].astype(F32)
            dq_rows[h, rows] = jnp.transpose(dq_wide[h, :, rows] + came)
        dots += gain(q_gain, h) * dq_rows[h] * q_in[:, cols].astype(F32)
    y_out[1] = as_rows(jnp.sum(dots, axis=1, keepdims=True), 0.0)
    y_start(1)

    for t in range(2):
        for d in range(2):
            for kind in range(2):
                xb_copy(1, d, kind, t).wait_recv()
    columns = []
    for t in range(2):
        rows = slice(t * TILE, (t + 1) * TILE)
        dots = jnp.zeros((TILE, HD), F32)
        for h in range(NH):
            cols = slice(h * HD, (h + 1) * HD)
            b = t * NH + h
            dk = dk_sum[b] + x_in[0, 0, NT + b].astype(F32) + x_in[0, 1, NT + b].astype(F32)
            dk_sum[b] = dk
            dots += gain(k_gain, h) * dk * k_in[rows, cols].astype(F32)
        columns.append(jnp.sum(dots, axis=1, keepdims=True))
    y_out[2] = as_rows(jnp.concatenate(columns, axis=0), 0.0)
    y_start(2)

    def finish(wide, gains, grad, scale, dot_mean):
        return (scale * gains * grad - wide * (scale * scale * scale) * dot_mean).astype(BF16)

    for t in range(2):
        rows = slice(t * TILE, (t + 1) * TILE)
        for h in range(NH):
            b = t * NH + h
            dv = dv_sum[b] + x_in[0, 0, b].astype(F32) + x_in[0, 1, b].astype(F32)
            dv_out[rows, h * HD : (h + 1) * HD] = dv.astype(BF16)
    q_dot, _ = as_columns(y_total(1) / width_all)
    for h in range(NH):
        cols = slice(h * HD, (h + 1) * HD)
        dq_out[:, cols] = finish(
            q_in[:, cols].astype(F32), gain(q_gain, h), dq_rows[h], q_scale_ref[...], q_dot
        )
    k_dot, _ = as_columns(y_total(2) / width_all)
    for t in range(2):
        rows = slice(t * TILE, (t + 1) * TILE)
        for h in range(NH):
            cols = slice(h * HD, (h + 1) * HD)
            dk_out[rows, cols] = finish(
                k_in[rows, cols].astype(F32),
                gain(k_gain, h),
                dk_sum[t * NH + h],
                k_scale_ref[rows],
                k_dot[rows],
            )

    for n in range(3):
        for p in range(1, NY):
            y_copy(n, p).wait_send()
    for r in range(1, NZ):
        st_copy(r).wait_send()
        rp_copy(r).wait_send()
    for dx in range(NX):
        cb_copy(dx).wait_send()
    for t in range(2):
        for d in range(2):
            for level in range(1, 5):
                if level < 4 or t == d:
                    zb_copy(d, level, t).wait_send()
            for kind in range(2):
                xb_copy(1, d, kind, t).wait_send()
                if t == d:
                    xb_copy(2, d, kind, t).wait_send()


def place_results(a, b, c, a_out, b_out, c_out, held, sems):
    coming = [
        pltpu.make_async_copy(src, held.at[i], sems.at[0, i]) for i, src in enumerate((a, b, c))
    ]
    going = [
        pltpu.make_async_copy(held.at[i], dst, sems.at[1, i])
        for i, dst in enumerate((a_out, b_out, c_out))
    ]
    for copy in coming:
        copy.start()
    for came, goes in zip(coming, going):
        came.wait()
        goes.start()
    for copy in going:
        copy.wait()


def on_device(q_pre, k_pre, values, out_grad, q_gain, k_gain, selected):
    width_dev = q_pre.shape[1]
    width_all = float(width_dev * lax.axis_size("head"))
    vmem = pl.BlockSpec(memory_space=pltpu.VMEM)
    dma = pltpu.SemaphoreType.DMA
    pairs = NZ * NP
    scratch = [pltpu.VMEM((NH, TOK, HD), BF16) for _ in range(2 * NZ)] + [
        pltpu.VMEM((NP * NT, TILE, HD), BF16),
        pltpu.VMEM((NP * NT, TILE, HD), BF16),
        pltpu.VMEM((pairs, TILE, TOK), F32),
        pltpu.VMEM((pairs, TILE, TOK), F32),
        pltpu.VMEM((2 * pairs, TILE, HD), BF16),
        pltpu.VMEM((pairs, HD, TOK), BF16),
        pltpu.VMEM((2, 4, NH, TOK, HD), BF16),
        pltpu.VMEM((NX * 2 * NT, TILE, HD), BF16),
        pltpu.VMEM((NX * 2 * NT, TILE, HD), BF16),
        pltpu.VMEM((3, 2 * NT, TILE, HD), BF16),
        pltpu.VMEM((2, 2, 2 * NT, TILE, HD), BF16),
        pltpu.VMEM((NH, 2, TILE, TOK), F32),
        pltpu.VMEM((NH, 2, TILE, TOK), F32),
        pltpu.VMEM((NH, 2, 8, TOK), F32),
        pltpu.VMEM((NZ, 2, NP, TOK), F32),
        pltpu.VMEM((NZ, 2, NP, TOK), F32),
        pltpu.VMEM((16, TOK), F32),
        pltpu.VMEM((NZ, 16, TOK), F32),
        pltpu.VMEM((NZ * NH, 8, TOK), F32),
        pltpu.VMEM((NZ * NH, 8, TOK), F32),
        pltpu.VMEM((NH, HD, TOK), F32),
        pltpu.VMEM((NH, TOK, HD), F32),
        pltpu.VMEM((NT, TILE, HD), F32),
        pltpu.VMEM((NT, TILE, HD), F32),
        pltpu.VMEM((TOK, 128), F32),
        pltpu.VMEM((TOK, 128), F32),
        pltpu.VMEM((3, 8, TOK), F32),
        pltpu.VMEM((3, NY - 1, 8, TOK), F32),
        pltpu.VMEM((NZ, 8, 128), jnp.int32),
        pltpu.SMEM((NZ, 8, 128), jnp.int32),
        dma((2, 16)),
        dma((2, 16)),
        dma((2, 2, 3)),
        dma((2, 2, 3)),
        dma((2, NX)),
        dma((2, NX)),
        dma((NZ,)),
        dma((NZ,)),
        dma((NZ - 1,)),
        dma((NZ - 1,)),
        dma((2, 4, 2)),
        dma((2, 4, 2)),
        dma((NX,)),
        dma((NX,)),
        dma((2, 2, 2, 2)),
        dma((2, 2, 2, 2)),
        dma((3, NY - 1)),
        dma((3, NY - 1)),
        dma((NZ - 1,)),
        dma((NZ - 1,)),
        dma((1,)),
    ]
    out = jax.ShapeDtypeStruct(q_pre.shape, BF16)
    results = pl.pallas_call(
        functools.partial(kernel, width_all),
        out_shape=(out, out, out),
        in_specs=[pl.BlockSpec(memory_space=pltpu.SMEM)] + [vmem] * 6,
        out_specs=(vmem, vmem, vmem),
        scratch_shapes=scratch,
        compiler_params=pltpu.CompilerParams(
            collective_id=0, has_side_effects=True, vmem_limit_bytes=60 * 2**20
        ),
        name="sparse_attention_backward",
    )(
        jnp.transpose(selected, (1, 0, 2)), q_pre, k_pre, values, out_grad, q_gain, k_gain
    )
    anywhere = pl.BlockSpec(memory_space=pl.ANY)
    return pl.pallas_call(
        place_results,
        out_shape=(out, out, out),
        in_specs=[anywhere] * 3,
        out_specs=(anywhere,) * 3,
        scratch_shapes=[pltpu.VMEM((3,) + q_pre.shape, BF16), dma((2, 3))],
        name="place_results",
    )(*results)


def solution(mesh):
    placed = (
        P("ctx", "head"),
        P("ctx", "head"),
        P("ctx", "head"),
        P("ctx", "head"),
        P("head"),
        P("head"),
        P("ctx", "head", None),
    )
    return jax.shard_map(
        on_device,
        mesh=mesh,
        in_specs=placed,
        out_specs=(P("ctx", "head"), P("ctx", "head"), P("ctx", "head")),
        check_vma=False,
    )
```

```python
import functools
import math

import jax
import jax.numpy as jnp
from jax import lax
from jax.experimental import pallas as pl
from jax.experimental.pallas import tpu as pltpu
from jax.sharding import PartitionSpec as P

HD = 128
TILE = 128
NH = 5
REM = 7
NT = 2 * NH
NZ = 8
NP = 8
NX = 4
NY = 4
TOK = 2 * TILE
EPS = 1e-6
FACTOR = 1.0 / math.sqrt(HD)
MESH = pl.DeviceIdType.MESH
Z_ORDER = ((0, 0), (1, 1), (0, 1), (1, 0))
F32 = jnp.float32
BF16 = jnp.bfloat16


def dot_nt(a, b):
    return lax.dot_general(a, b, (((1,), (1,)), ((), ())), preferred_element_type=F32)


def dot_nn(a, b):
    return lax.dot_general(a, b, (((1,), (0,)), ((), ())), preferred_element_type=F32)


def dot_tn(a, b):
    return lax.dot_general(a, b, (((0,), (0,)), ((), ())), preferred_element_type=F32)


def fold_rows(array, op):
    parts = [array[8 * i : 8 * i + 8] for i in range(array.shape[0] // 8)]
    while len(parts) > 1:
        parts = [op(parts[i], parts[i + 1]) for i in range(0, len(parts), 2)]
    return parts[0]


def kernel(width_all, *refs):
    sel, q_in, k_in, v_in, g_in, q_gain, k_gain, dq_out, dk_out, dv_out = refs[:10]
    scratch = list(refs[10:])
    g_bufs = [scratch.pop(0) for _ in range(NZ)]
    q_bufs = [scratch.pop(0) for _ in range(NZ)]
    moving = (g_bufs, q_bufs)
    (
        v_all,
        k_all,
        s_all,
        dp_all,
        kv_terms,
        q_terms,
        back_z,
        core_out,
        core_in,
        x_out,
        x_in,
        s_near,
        dp_near,
        near_stats,
        stat_out,
        stat_in,
        reply_out,
        reply_in,
        lse_ref,
        delta_ref,
        dq_wide,
        dk_sum,
        dv_sum,
        q_scale_ref,
        k_scale_ref,
        y_out,
        y_in,
        req_v,
        req_s,
        zf_send,
        zf_recv,
        xg_send,
        xg_recv,
        cg_send,
        cg_recv,
        st_send,
        st_recv,
        rp_send,
        rp_recv,
        zb_send,
        zb_recv,
        cb_send,
        cb_recv,
        xb_send,
        xb_recv,
        y_send,
        y_recv,
        rq_send,
        rq_recv,
        here_sem,
    ) = scratch
    fixed = (v_all, k_all)

    me = lax.axis_index("ctx")
    group = lax.axis_index("head")
    z = me // NP
    x = lax.rem(me, NP) // 2
    core = lax.rem(me, 2)

    def along_z(o):
        return {"ctx": lax.rem(z + o, NZ) * NP + lax.rem(me, NP), "head": group}

    def along_x(o):
        return {"ctx": z * NP + lax.rem(x + o, NX) * 2 + core, "head": group}

    def along_y(o):
        return {"ctx": me, "head": lax.rem(group + o, NY)}

    other_core = {"ctx": z * NP + x * 2 + (1 - core), "head": group}
    z_next = (along_z(1), along_z(NZ - 1))
    x_next = (along_x(1), along_x(NX - 1))

    barrier = pltpu.get_barrier_semaphore()
    peers = [along_z(o) for o in range(1, NZ)] + [along_y(o) for o in range(1, NY)]
    peers += [x_next[0], x_next[1], other_core]
    for peer in peers:
        pl.semaphore_signal(barrier, inc=1, device_id=peer, device_id_type=MESH)

    def remote(src, dst, send, recv, to):
        return pltpu.make_async_remote_copy(
            src_ref=src,
            dst_ref=dst,
            send_sem=send,
            recv_sem=recv,
            device_id=to,
            device_id_type=MESH,
        )

    for h in range(NH):
        cols = slice(h * HD, (h + 1) * HD)
        g_bufs[0][h] = g_in[:, cols]
        for t in range(2):
            v_all[t * NH + h] = v_in[t * TILE : (t + 1) * TILE, cols]
    lane = lax.broadcasted_iota(jnp.int32, (8, 128), 1)
    wanted = jnp.full((8, 128), -1, jnp.int32)
    for h in range(NH):
        for c in range(REM):
            tile = sel[h, 0, c]
            wanted = jnp.where(lane == (tile >> 1), (tile & 1) * NH + h, wanted)
    req_v[0] = wanted

    def squares(ref):
        wide = ref[...].astype(F32)
        return jnp.sum(wide * wide, axis=1, keepdims=True)

    lanes_tok = lax.broadcasted_iota(jnp.int32, (TOK, 128), 1)

    def as_rows(first, second):
        both = jnp.where(lanes_tok == 0, first, jnp.where(lanes_tok == 1, second, 0.0))
        return jnp.transpose(both)[:8]

    def as_columns(rows):
        tall = jnp.transpose(jnp.concatenate([rows, jnp.zeros((120, TOK), F32)], axis=0))
        return tall[:, 0:1], tall[:, 1:2]

    def y_copy(n, p):
        return remote(
            y_out.at[n], y_in.at[n, p - 1], y_send.at[n, p - 1], y_recv.at[n, p - 1], along_y(p)
        )

    def y_start(n):
        for p in range(1, NY):
            y_copy(n, p).start()

    def y_total(n):
        for p in range(1, NY):
            y_copy(n, p).wait_recv()
        return (y_out[n] + y_in[n, 0]) + (y_in[n, 1] + y_in[n, 2])

    y_out[0] = as_rows(squares(q_in), squares(k_in))
    pl.semaphore_wait(barrier, len(peers))

    def req_copy(o):
        return remote(
            req_v.at[0], req_v.at[NZ - o], rq_send.at[o - 1], rq_recv.at[o - 1], along_z(o)
        )

    def zf_copy(d, hop, kind, t):
        source = (NZ + 1 - hop) % NZ if d == 0 else hop - 1
        target = NZ - hop if d == 0 else hop
        at = ((hop - 1) * 2 + kind) * 2 + t
        rows = pl.ds(t * TILE, TILE)
        return remote(
            moving[kind][source].at[:, rows],
            moving[kind][target].at[:, rows],
            zf_send.at[d, at],
            zf_recv.at[d, at],
            z_next[d],
        )

    def xg_copy(kind, d, n):
        if n < 2:
            src, dst = n * NH, (6 if d == 0 else 2) * NT + n * NH
        else:
            src = (6 if d == 0 else 2) * NT + d * NH
            dst = 4 * NT + d * NH
        return remote(
            fixed[kind].at[pl.ds(src, NH)],
            fixed[kind].at[pl.ds(dst, NH)],
            xg_send.at[kind, d, n],
            xg_recv.at[kind, d, n],
            x_next[d],
        )

    def cg_copy(kind, dx):
        return remote(
            fixed[kind].at[pl.ds(2 * dx * NT, NT)],
            fixed[kind].at[pl.ds((2 * dx + 1) * NT, NT)],
            cg_send.at[kind, dx],
            cg_recv.at[kind, dx],
            other_core,
        )

    for d, t in Z_ORDER:
        zf_copy(d, 1, 0, t).start()
    y_start(0)
    for t in range(2):
        for d in range(2):
            xg_copy(0, d, t).start()
    for o in range(1, NZ):
        req_copy(o).start()
    cg_copy(0, 0).start()

    total = y_total(0)
    q_scale, k_scale = as_columns(lax.rsqrt(total / width_all + EPS))
    q_scale_ref[...] = jnp.broadcast_to(q_scale, (TOK, 128))
    k_scale_ref[...] = jnp.broadcast_to(k_scale, (TOK, 128))

    def gain(ref, h):
        return ref[h * HD : (h + 1) * HD].reshape(1, HD)

    for t in range(2):
        rows = slice(t * TILE, (t + 1) * TILE)
        for h in range(NH):
            cols = slice(h * HD, (h + 1) * HD)
            q_bufs[0][h, rows] = (
                q_in[rows, cols].astype(F32) * q_scale_ref[rows] * gain(q_gain, h)
            ).astype(BF16)
            k_all[t * NH + h] = (
                k_in[rows, cols].astype(F32) * k_scale_ref[rows] * gain(k_gain, h)
            ).astype(BF16)
        for d in range(2):
            xg_copy(1, d, t).start()
            if t == 1:
                zf_copy(d, 1, 1, d).start()
    for d in range(2):
        zf_copy(d, 1, 1, 1 - d).start()
    cg_copy(1, 0).start()

    for o in range(1, NZ):
        req_copy(o).wait_recv()
    table = pltpu.make_async_copy(req_v, req_s, here_sem.at[0])
    table.start()
    table.wait()

    def code_of(r, place):
        dx, other = place // 2, lax.rem(place, 2)
        lane_at = z * NP + lax.rem(x + dx, NX) * 2 + lax.rem(core + other, 2)
        return req_s[r, 0, lane_at]

    def row_stats(s, dp, top):
        e = jnp.exp(s - top)
        return fold_rows(e, jnp.add), fold_rows(e * dp, jnp.add)

    def near_scores(h, carry):
        tops = []
        for t in range(2):
            s = dot_nt(k_all[t * NH + h], q_bufs[0][h]) * FACTOR
            s_near[h, t] = s
            dp_near[h, t] = dot_nt(v_all[t * NH + h], g_bufs[0][h])
            tops.append(fold_rows(s, jnp.maximum))
        top = jnp.max(jnp.maximum(tops[0], tops[1]), axis=0, keepdims=True)
        first = row_stats(s_near[h, 0], dp_near[h, 0], top)
        second = row_stats(s_near[h, 1], dp_near[h, 1], top)
        mass = jnp.sum(first[0] + second[0], axis=0, keepdims=True)
        drift = jnp.sum(first[1] + second[1], axis=0, keepdims=True)
        near_stats[h, 0] = jnp.broadcast_to(top + jnp.log(mass), (8, TOK))
        near_stats[h, 1] = jnp.broadcast_to(drift / mass, (8, TOK))
        return carry

    def st_copy(r):
        return remote(
            stat_out.at[r], stat_in.at[(NZ - r) % NZ], st_send.at[r], st_recv.at[r], along_z(r)
        )

    sub = lax.broadcasted_iota(jnp.int32, (8, TOK), 0)

    def gradient_scores(r):
        def one(i, carry):
            for half in range(2):
                place = 2 * i + half
                code = jnp.maximum(code_of(r, place), 0)
                dp_all[r * NP + place] = dot_nt(
                    v_all[place * NT + code], g_bufs[r][lax.rem(code, NH)]
                )
            return carry

        lax.fori_loop(0, NP // 2, one, 0)

    def scores(r, with_dp=True):
        def one(i, carry):
            lse8, delta8 = carry
            for half in range(2):
                place = 2 * i + half
                code = jnp.maximum(code_of(r, place), 0)
                head = lax.rem(code, NH)
                s = dot_nt(k_all[place * NT + code], q_bufs[r][head]) * FACTOR
                if with_dp:
                    dp = dot_nt(v_all[place * NT + code], g_bufs[r][head])
                    dp_all[r * NP + place] = dp
                else:
                    dp = dp_all[r * NP + place]
                s_all[r * NP + place] = s
                top = jnp.max(fold_rows(s, jnp.maximum), axis=0, keepdims=True)
                mass, drift = row_stats(s, dp, top)
                mass = jnp.sum(mass, axis=0, keepdims=True)
                drift = jnp.sum(drift, axis=0, keepdims=True)
                lse8 = jnp.where(sub == place, top + jnp.log(mass), lse8)
                delta8 = jnp.where(sub == place, drift / mass, delta8)
            return lse8, delta8

        zero = jnp.zeros((8, TOK), F32)
        lse8, delta8 = lax.fori_loop(0, NP // 2, one, (zero, zero))
        if r == 0:
            stat_in[0, 0] = lse8
            stat_in[0, 1] = delta8
        else:
            stat_out[r, 0] = lse8
            stat_out[r, 1] = delta8
            st_copy(r).start()

    def forward(hop, kind):
        for d, t in Z_ORDER:
            if hop < 4 or t == d:
                zf_copy(d, hop, kind, t).wait_recv()
            if hop < 3 or (hop == 3 and t == d):
                zf_copy(d, hop + 1, kind, t).start()

    def plane_first(kind):
        for t in range(2):
            for d in range(2):
                xg_copy(kind, d, t).wait_recv()
                if t == d:
                    xg_copy(kind, d, 2).start()
        cg_copy(kind, 1).start()
        cg_copy(kind, 3).start()

    def plane_second(kind):
        for d in range(2):
            xg_copy(kind, d, 2).wait_recv()
        cg_copy(kind, 2).start()

    forward(1, 0)
    plane_first(0)
    lax.fori_loop(0, NH, near_scores, 0)
    forward(1, 1)
    plane_first(1)
    plane_second(0)
    forward(2, 0)
    plane_second(1)
    for kind in range(2):
        for dx in range(NX):
            cg_copy(kind, dx).wait_recv()
    scores(0)
    forward(2, 1)
    scores(7)
    scores(1)
    forward(3, 0)
    scores(6)
    row_at = lax.broadcasted_iota(jnp.int32, (NZ * NP, TOK), 0)
    head_at = jnp.full((NZ * NP, TOK), -1, jnp.int32)
    for h in range(NH):
        for c in range(REM):
            owner = sel[h, 0, c] >> 1
            dz = (owner // NP - z + NZ) & (NZ - 1)
            dx = ((owner & (NP - 1)) // 2 - x + NX) & (NX - 1)
            place = dx * 2 + ((owner + core) & 1)
            head_at = jnp.where(row_at == dz * NP + place, h, head_at)
    forward(3, 1)
    scores(2)
    scores(5)
    forward(4, 0)
    scores(3)
    gradient_scores(4)
    forward(4, 1)
    scores(4, with_dp=False)

    for r in range(1, NZ):
        st_copy(r).wait_recv()
    pair_lse = jnp.concatenate([stat_in[r, 0] for r in range(NZ)], axis=0)
    pair_delta = jnp.concatenate([stat_in[r, 1] for r in range(NZ)], axis=0)
    for h in range(NH):
        mine = head_at == h
        near_lse, near_delta = near_stats[h, 0, :1], near_stats[h, 1, :1]
        top = jnp.max(jnp.where(mine, pair_lse, -3e38), axis=0, keepdims=True)
        top = jnp.maximum(top, near_lse)
        weight = jnp.where(mine, jnp.exp(pair_lse - top), 0.0)
        near_weight = jnp.exp(near_lse - top)
        whole = jnp.sum(weight, axis=0, keepdims=True) + near_weight
        drift = jnp.where(mine, weight * pair_delta, 0.0)
        drift = jnp.sum(drift, axis=0, keepdims=True) + near_weight * near_delta
        reply_out[pl.ds(h, 1)] = top + jnp.log(whole)
        reply_out[pl.ds(8 + h, 1)] = drift / whole

    def rp_copy(o):
        return remote(
            reply_out, reply_in.at[NZ - o], rp_send.at[o - 1], rp_recv.at[o - 1], along_z(o)
        )

    for o in (4, 3, 5, 2, 6, 1, 7):
        rp_copy(o).start()
    reply_in[0] = reply_out[...]

    for o in range(1, NZ):
        req_copy(o).wait_send()
    for hop in range(1, 5):
        for kind in range(2):
            for t in range(2):
                for d in range(2):
                    if hop < 4 or t == d:
                        zf_copy(d, hop, kind, t).wait_send()
    for kind in range(2):
        for d in range(2):
            for n in range(3):
                xg_copy(kind, d, n).wait_send()
        for dx in range(NX):
            cg_copy(kind, dx).wait_send()

    for o in range(1, NZ):
        rp_copy(o).wait_recv()
    for r in range(NZ):
        for h in range(NH):
            lse_ref[r * NH + h] = jnp.broadcast_to(reply_in[r, h : h + 1], (8, TOK))
            delta_ref[r * NH + h] = jnp.broadcast_to(reply_in[r, 8 + h : 9 + h], (8, TOK))

    def term(r, place):
        pair = r * NP + place
        asked = code_of(r, place)
        code = jnp.maximum(asked, 0)
        head = lax.rem(code, NH)
        probs = jnp.exp(s_all[pair] - lse_ref[r * NH + head][:1])
        probs = jnp.where(asked >= 0, probs, 0.0)
        ds = (probs * (dp_all[pair] - delta_ref[r * NH + head][:1]) * FACTOR).astype(BF16)
        dv = dot_nn(probs.astype(BF16), g_bufs[r][head])
        dk = dot_nn(ds, q_bufs[r][head])
        dq = dot_tn(ds, k_all[place * NT + code])
        kv_terms[2 * pair] = dv.astype(BF16)
        kv_terms[2 * pair + 1] = dk.astype(BF16)
        q_terms[pair] = dq.astype(BF16)

    zero_tile = jnp.zeros((TILE, HD), BF16)

    def tree(parts):
        while len(parts) > 1:
            parts = [parts[i] + parts[i + 1] for i in range(0, len(parts), 2)]
        return parts[0].astype(F32)

    def key_sum(place, kind, block):
        return tree(
            [
                jnp.where(
                    code_of(r, place) == block, kv_terms[2 * (r * NP + place) + kind], zero_tile
                )
                for r in range(NZ)
            ]
        )

    def query_sum(r, t, h):
        rows = slice(t * TILE, (t + 1) * TILE)
        return tree(
            [
                jnp.where(
                    lax.rem(jnp.maximum(code_of(r, place), 0), NH) == h,
                    q_terms[r * NP + place, rows],
                    zero_tile,
                )
                for place in range(NP)
            ]
        )

    def cb_copy(dx):
        part = pl.ds(dx * 2 * NT, 2 * NT)
        return remote(
            core_out.at[part], core_in.at[part], cb_send.at[dx], cb_recv.at[dx], other_core
        )

    def to_core(dx):
        def one(block, carry):
            for kind in range(2):
                acc = key_sum(2 * dx + 1, kind, block)
                core_out[dx * 2 * NT + kind * NT + block] = acc.astype(BF16)
            return carry

        lax.fori_loop(0, NT, one, 0)
        cb_copy(dx).start()

    def chip_sum(dx, kind, block):
        near = core_in[dx * 2 * NT + kind * NT + block].astype(F32)
        return key_sum(2 * dx, kind, block) + near

    def xb_copy(level, d, kind, t):
        dx = 2 if level == 2 else (1 if d == 0 else 3)
        part = pl.ds(kind * NT + t * NH, NH)
        return remote(
            x_out.at[dx - 1, part],
            x_in.at[level - 1, d, part],
            xb_send.at[level - 1, d, kind, t],
            xb_recv.at[level - 1, d, kind, t],
            x_next[d],
        )

    def x_pass(level, d, t):
        dx = 2 if level == 2 else (1 if d == 0 else 3)
        chained = level == 1 and t == d
        for kind in range(2):
            if chained:
                xb_copy(2, d, kind, t).wait_recv()

            def one(b, carry):
                block = t * NH + b
                acc = chip_sum(dx, kind, block)
                if chained:
                    acc += x_in[1, d, kind * NT + block].astype(F32)
                x_out[dx - 1, kind * NT + block] = acc.astype(BF16)
                return carry

            lax.fori_loop(0, NH, one, 0)
            xb_copy(level, d, kind, t).start()

    def zb_copy(d, level, t):
        r = level if d == 0 else NZ - level
        rows = pl.ds(t * TILE, TILE)
        return remote(
            q_bufs[r].at[:, rows],
            back_z.at[d, level - 1, :, rows],
            zb_send.at[d, level - 1, t],
            zb_recv.at[d, level - 1, t],
            z_next[d],
        )

    def z_pass(d, level):
        r = level if d == 0 else NZ - level
        for t in (d,) if level == 4 else (1 - d, d):
            chained = level < 3 or (level == 3 and t == d)
            rows = slice(t * TILE, (t + 1) * TILE)
            if chained:
                zb_copy(d, level + 1, t).wait_recv()

            def one(h, carry):
                acc = query_sum(r, t, h)
                if chained:
                    acc += back_z[d, level, h, rows].astype(F32)
                q_bufs[r][h, rows] = acc.astype(BF16)
                return carry

            lax.fori_loop(0, NH, one, 0)
            zb_copy(d, level, t).start()

    def rest_terms(r):
        def one(i, carry):
            for half in range(2):
                place = 2 * i + half
                term(r, place + jnp.where(i >= 2, 2, 0))
            return carry

        lax.fori_loop(0, NP // 2 - 1, one, 0)

    def opposite_terms(r):
        term(r, 4)
        term(r, 5)

    opposite_terms(4)
    rest_terms(4)
    z_pass(0, 4)
    z_pass(1, 4)
    for r in (5, 3, 6, 2, 7, 1, 0):
        opposite_terms(r)
    to_core(2)
    rest_terms(5)
    z_pass(1, 3)
    rest_terms(3)
    z_pass(0, 3)
    cb_copy(2).wait_recv()
    x_pass(2, 0, 0)
    x_pass(2, 1, 1)
    for r in (6, 2, 7, 1, 0):
        rest_terms(r)
    to_core(1)
    to_core(3)
    z_pass(1, 2)
    z_pass(0, 2)
    cb_copy(1).wait_recv()
    x_pass(1, 0, 1)
    cb_copy(3).wait_recv()
    x_pass(1, 1, 0)
    x_pass(1, 0, 0)
    x_pass(1, 1, 1)
    to_core(0)

    def near_terms(h, carry):
        dq = jnp.zeros((TOK, HD), F32)
        lse, delta = lse_ref[h][:1], delta_ref[h][:1]
        for t in range(2):
            probs = jnp.exp(s_near[h, t] - lse)
            ds = (probs * (dp_near[h, t] - delta) * FACTOR).astype(BF16)
            dv_sum[t * NH + h] = dot_nn(probs.astype(BF16), g_bufs[0][h])
            dk_sum[t * NH + h] = dot_nn(ds, q_bufs[0][h])
            dq += dot_tn(ds, k_all[t * NH + h])
        dq_wide[h] = dq
        for t in range(2):
            dq_wide[h, t * TILE : (t + 1) * TILE] += query_sum(0, t, h)
        return carry

    lax.fori_loop(0, NH, near_terms, 0)
    z_pass(1, 1)
    z_pass(0, 1)
    cb_copy(0).wait_recv()

    def own_sum(block, carry):
        dv_sum[block] += chip_sum(0, 0, block)
        dk_sum[block] += chip_sum(0, 1, block)
        return carry

    lax.fori_loop(0, NT, own_sum, 0)

    for t in range(2):
        for d in range(2):
            zb_copy(d, 1, t).wait_recv()
    dots = jnp.zeros((TOK, HD), F32)
    for h in range(NH):
        cols = slice(h * HD, (h + 1) * HD)
        dq = dq_wide[h] + back_z[0, 0, h].astype(F32) + back_z[1, 0, h].astype(F32)
        dq_wide[h] = dq
        dots += gain(q_gain, h) * dq * q_in[:, cols].astype(F32)
    y_out[1] = as_rows(jnp.sum(dots, axis=1, keepdims=True), 0.0)
    y_start(1)

    for t in range(2):
        for d in range(2):
            for kind in range(2):
                xb_copy(1, d, kind, t).wait_recv()
    columns = []
    for t in range(2):
        rows = slice(t * TILE, (t + 1) * TILE)
        dots = jnp.zeros((TILE, HD), F32)
        for h in range(NH):
            cols = slice(h * HD, (h + 1) * HD)
            b = t * NH + h
            dk = dk_sum[b] + x_in[0, 0, NT + b].astype(F32) + x_in[0, 1, NT + b].astype(F32)
            dk_sum[b] = dk
            dots += gain(k_gain, h) * dk * k_in[rows, cols].astype(F32)
        columns.append(jnp.sum(dots, axis=1, keepdims=True))
    y_out[2] = as_rows(jnp.concatenate(columns, axis=0), 0.0)
    y_start(2)

    def finish(wide, gains, grad, scale, dot_mean):
        return (scale * gains * grad - wide * (scale * scale * scale) * dot_mean).astype(BF16)

    for t in range(2):
        rows = slice(t * TILE, (t + 1) * TILE)
        for h in range(NH):
            b = t * NH + h
            dv = dv_sum[b] + x_in[0, 0, b].astype(F32) + x_in[0, 1, b].astype(F32)
            dv_out[rows, h * HD : (h + 1) * HD] = dv.astype(BF16)
    q_dot, _ = as_columns(y_total(1) / width_all)
    for h in range(NH):
        cols = slice(h * HD, (h + 1) * HD)
        dq_out[:, cols] = finish(
            q_in[:, cols].astype(F32), gain(q_gain, h), dq_wide[h], q_scale_ref[...], q_dot
        )
    k_dot, _ = as_columns(y_total(2) / width_all)
    for t in range(2):
        rows = slice(t * TILE, (t + 1) * TILE)
        for h in range(NH):
            cols = slice(h * HD, (h + 1) * HD)
            dk_out[rows, cols] = finish(
                k_in[rows, cols].astype(F32),
                gain(k_gain, h),
                dk_sum[t * NH + h],
                k_scale_ref[rows],
                k_dot[rows],
            )

    for n in range(3):
        for p in range(1, NY):
            y_copy(n, p).wait_send()
    for r in range(1, NZ):
        st_copy(r).wait_send()
        rp_copy(r).wait_send()
    for dx in range(NX):
        cb_copy(dx).wait_send()
    for t in range(2):
        for d in range(2):
            for level in range(1, 5):
                if level < 4 or t == d:
                    zb_copy(d, level, t).wait_send()
            for kind in range(2):
                xb_copy(1, d, kind, t).wait_send()
                if t == d:
                    xb_copy(2, d, kind, t).wait_send()


def place_results(a, b, c, a_out, b_out, c_out, held, sems):
    coming = [
        pltpu.make_async_copy(src, held.at[i], sems.at[0, i]) for i, src in enumerate((a, b, c))
    ]
    going = [
        pltpu.make_async_copy(held.at[i], dst, sems.at[1, i])
        for i, dst in enumerate((a_out, b_out, c_out))
    ]
    for copy in coming:
        copy.start()
    for came, goes in zip(coming, going):
        came.wait()
        goes.start()
    for copy in going:
        copy.wait()


def on_device(q_pre, k_pre, values, out_grad, q_gain, k_gain, selected):
    width_dev = q_pre.shape[1]
    width_all = float(width_dev * lax.axis_size("head"))
    vmem = pl.BlockSpec(memory_space=pltpu.VMEM)
    dma = pltpu.SemaphoreType.DMA
    pairs = NZ * NP
    scratch = [pltpu.VMEM((NH, TOK, HD), BF16) for _ in range(2 * NZ)] + [
        pltpu.VMEM((NP * NT, TILE, HD), BF16),
        pltpu.VMEM((NP * NT, TILE, HD), BF16),
        pltpu.VMEM((pairs, TILE, TOK), F32),
        pltpu.VMEM((pairs, TILE, TOK), F32),
        pltpu.VMEM((2 * pairs, TILE, HD), BF16),
        pltpu.VMEM((pairs, TOK, HD), BF16),
        pltpu.VMEM((2, 4, NH, TOK, HD), BF16),
        pltpu.VMEM((NX * 2 * NT, TILE, HD), BF16),
        pltpu.VMEM((NX * 2 * NT, TILE, HD), BF16),
        pltpu.VMEM((3, 2 * NT, TILE, HD), BF16),
        pltpu.VMEM((2, 2, 2 * NT, TILE, HD), BF16),
        pltpu.VMEM((NH, 2, TILE, TOK), F32),
        pltpu.VMEM((NH, 2, TILE, TOK), F32),
        pltpu.VMEM((NH, 2, 8, TOK), F32),
        pltpu.VMEM((NZ, 2, NP, TOK), F32),
        pltpu.VMEM((NZ, 2, NP, TOK), F32),
        pltpu.VMEM((16, TOK), F32),
        pltpu.VMEM((NZ, 16, TOK), F32),
        pltpu.VMEM((NZ * NH, 8, TOK), F32),
        pltpu.VMEM((NZ * NH, 8, TOK), F32),
        pltpu.VMEM((NH, TOK, HD), F32),
        pltpu.VMEM((NT, TILE, HD), F32),
        pltpu.VMEM((NT, TILE, HD), F32),
        pltpu.VMEM((TOK, 128), F32),
        pltpu.VMEM((TOK, 128), F32),
        pltpu.VMEM((3, 8, TOK), F32),
        pltpu.VMEM((3, NY - 1, 8, TOK), F32),
        pltpu.VMEM((NZ, 8, 128), jnp.int32),
        pltpu.SMEM((NZ, 8, 128), jnp.int32),
        dma((2, 16)),
        dma((2, 16)),
        dma((2, 2, 3)),
        dma((2, 2, 3)),
        dma((2, NX)),
        dma((2, NX)),
        dma((NZ,)),
        dma((NZ,)),
        dma((NZ - 1,)),
        dma((NZ - 1,)),
        dma((2, 4, 2)),
        dma((2, 4, 2)),
        dma((NX,)),
        dma((NX,)),
        dma((2, 2, 2, 2)),
        dma((2, 2, 2, 2)),
        dma((3, NY - 1)),
        dma((3, NY - 1)),
        dma((NZ - 1,)),
        dma((NZ - 1,)),
        dma((1,)),
    ]
    out = jax.ShapeDtypeStruct(q_pre.shape, BF16)
    results = pl.pallas_call(
        functools.partial(kernel, width_all),
        out_shape=(out, out, out),
        in_specs=[pl.BlockSpec(memory_space=pltpu.SMEM)] + [vmem] * 6,
        out_specs=(vmem, vmem, vmem),
        scratch_shapes=scratch,
        compiler_params=pltpu.CompilerParams(
            collective_id=0, has_side_effects=True, vmem_limit_bytes=60 * 2**20
        ),
        name="sparse_attention_backward",
    )(
        jnp.transpose(selected, (1, 0, 2)), q_pre, k_pre, values, out_grad, q_gain, k_gain
    )
    anywhere = pl.BlockSpec(memory_space=pl.ANY)
    return pl.pallas_call(
        place_results,
        out_shape=(out, out, out),
        in_specs=[anywhere] * 3,
        out_specs=(anywhere,) * 3,
        scratch_shapes=[pltpu.VMEM((3,) + q_pre.shape, BF16), dma((2, 3))],
        name="place_results",
    )(*results)


def solution(mesh):
    placed = (
        P("ctx", "head"),
        P("ctx", "head"),
        P("ctx", "head"),
        P("ctx", "head"),
        P("head"),
        P("head"),
        P("ctx", "head", None),
    )
    return jax.shard_map(
        on_device,
        mesh=mesh,
        in_specs=placed,
        out_specs=(P("ctx", "head"), P("ctx", "head"), P("ctx", "head")),
        check_vma=False,
    )
```

```python
import functools
import math

import jax
import jax.numpy as jnp
from jax import lax
from jax.experimental import pallas as pl
from jax.experimental.pallas import tpu as pltpu
from jax.sharding import PartitionSpec as P

HD = 128
TILE = 128
NH = 5
REM = 7
NT = 2 * NH
NZ = 8
NP = 8
NX = 4
NY = 4
TOK = 2 * TILE
EPS = 1e-6
FACTOR = 1.0 / math.sqrt(HD)
MESH = pl.DeviceIdType.MESH
F32 = jnp.float32
BF16 = jnp.bfloat16


def dot_nt(a, b):
    return lax.dot_general(a, b, (((1,), (1,)), ((), ())), preferred_element_type=F32)


def dot_nn(a, b):
    return lax.dot_general(a, b, (((1,), (0,)), ((), ())), preferred_element_type=F32)


def dot_tn(a, b):
    return lax.dot_general(a, b, (((0,), (0,)), ((), ())), preferred_element_type=F32)


def fold_rows(array, op):
    parts = [array[8 * i : 8 * i + 8] for i in range(array.shape[0] // 8)]
    while len(parts) > 1:
        parts = [op(parts[i], parts[i + 1]) for i in range(0, len(parts), 2)]
    return parts[0]


def kernel(width_all, *refs):
    sel, q_hbm, k_hbm, v_hbm, g_in, q_gain, k_gain, dq_out, dk_out, dv_out = refs[:10]
    scratch = list(refs[10:])
    g_bufs = [scratch.pop(0) for _ in range(NZ)]
    q_bufs = [scratch.pop(0) for _ in range(NZ)]
    moving = (g_bufs, q_bufs)
    (
        v_all,
        k_all,
        s_all,
        dp_all,
        kv_terms,
        q_terms,
        back_z,
        core_out,
        core_in,
        x_out,
        x_in,
        s_near,
        dp_near,
        near_stats,
        stat_out,
        stat_in,
        reply_out,
        reply_in,
        lse_ref,
        delta_ref,
        dq_wide,
        dk_sum,
        dv_sum,
        q_scale_ref,
        k_scale_ref,
        y_out,
        y_in,
        req_v,
        req_s,
        zf_send,
        zf_recv,
        xg_send,
        xg_recv,
        cg_send,
        cg_recv,
        st_send,
        st_recv,
        rp_send,
        rp_recv,
        zb_send,
        zb_recv,
        cb_send,
        cb_recv,
        xb_send,
        xb_recv,
        y_send,
        y_recv,
        rq_send,
        rq_recv,
        here_sem,
        q_in,
        k_in,
        v_in,
        in_sem,
    ) = scratch
    loads = [
        pltpu.make_async_copy(src, dst, in_sem.at[i])
        for i, (src, dst) in enumerate(((q_hbm, q_in), (k_hbm, k_in), (v_hbm, v_in)))
    ]
    for load in loads:
        load.start()
    fixed = (v_all, k_all)

    me = lax.axis_index("ctx")
    group = lax.axis_index("head")
    z = me // NP
    x = lax.rem(me, NP) // 2
    core = lax.rem(me, 2)

    def along_z(o):
        return {"ctx": lax.rem(z + o, NZ) * NP + lax.rem(me, NP), "head": group}

    def along_x(o):
        return {"ctx": z * NP + lax.rem(x + o, NX) * 2 + core, "head": group}

    def along_y(o):
        return {"ctx": me, "head": lax.rem(group + o, NY)}

    other_core = {"ctx": z * NP + x * 2 + (1 - core), "head": group}
    z_next = (along_z(1), along_z(NZ - 1))
    x_next = (along_x(1), along_x(NX - 1))

    barrier = pltpu.get_barrier_semaphore()
    peers = [along_z(o) for o in range(1, NZ)] + [along_y(o) for o in range(1, NY)]
    peers += [x_next[0], x_next[1], other_core]
    for peer in peers:
        pl.semaphore_signal(barrier, inc=1, device_id=peer, device_id_type=MESH)

    def remote(src, dst, send, recv, to):
        return pltpu.make_async_remote_copy(
            src_ref=src,
            dst_ref=dst,
            send_sem=send,
            recv_sem=recv,
            device_id=to,
            device_id_type=MESH,
        )

    for h in range(NH):
        cols = slice(h * HD, (h + 1) * HD)
        g_bufs[0][h] = g_in[:, cols]
    lane = lax.broadcasted_iota(jnp.int32, (8, 128), 1)
    wanted = jnp.full((8, 128), -1, jnp.int32)
    for h in range(NH):
        for c in range(REM):
            tile = sel[h, 0, c]
            wanted = jnp.where(lane == (tile >> 1), (tile & 1) * NH + h, wanted)
    req_v[0] = wanted

    def squares(ref):
        wide = ref[...].astype(F32)
        return jnp.sum(wide * wide, axis=1, keepdims=True)

    lanes_tok = lax.broadcasted_iota(jnp.int32, (TOK, 128), 1)

    def as_rows(first, second):
        both = jnp.where(lanes_tok == 0, first, jnp.where(lanes_tok == 1, second, 0.0))
        return jnp.transpose(both)[:8]

    def as_columns(rows):
        tall = jnp.transpose(jnp.concatenate([rows, jnp.zeros((120, TOK), F32)], axis=0))
        return tall[:, 0:1], tall[:, 1:2]

    def y_copy(n, p):
        return remote(
            y_out.at[n], y_in.at[n, p - 1], y_send.at[n, p - 1], y_recv.at[n, p - 1], along_y(p)
        )

    def y_start(n):
        for p in range(1, NY):
            y_copy(n, p).start()

    def y_total(n):
        for p in range(1, NY):
            y_copy(n, p).wait_recv()
        return (y_out[n] + y_in[n, 0]) + (y_in[n, 1] + y_in[n, 2])

    pl.semaphore_wait(barrier, len(peers))

    def req_copy(o):
        return remote(
            req_v.at[0], req_v.at[NZ - o], rq_send.at[o - 1], rq_recv.at[o - 1], along_z(o)
        )

    def zf_copy(d, hop, kind, t):
        source = (NZ + 1 - hop) % NZ if d == 0 else hop - 1
        target = NZ - hop if d == 0 else hop
        at = ((hop - 1) * 2 + kind) * 2 + t
        rows = pl.ds(t * TILE, TILE)
        return remote(
            moving[kind][source].at[:, rows],
            moving[kind][target].at[:, rows],
            zf_send.at[d, at],
            zf_recv.at[d, at],
            z_next[d],
        )

    def xg_copy(kind, d, n):
        if n < 2:
            src, dst = n * NH, (6 if d == 0 else 2) * NT + n * NH
        else:
            src = (6 if d == 0 else 2) * NT + d * NH
            dst = 4 * NT + d * NH
        return remote(
            fixed[kind].at[pl.ds(src, NH)],
            fixed[kind].at[pl.ds(dst, NH)],
            xg_send.at[kind, d, n],
            xg_recv.at[kind, d, n],
            x_next[d],
        )

    def cg_copy(kind, dx):
        return remote(
            fixed[kind].at[pl.ds(2 * dx * NT, NT)],
            fixed[kind].at[pl.ds((2 * dx + 1) * NT, NT)],
            cg_send.at[kind, dx],
            cg_recv.at[kind, dx],
            other_core,
        )

    for t in range(2):
        for d in range(2):
            zf_copy(d, 1, 0, t).start()
    for load in loads:
        load.wait()
    y_out[0] = as_rows(squares(q_in), squares(k_in))
    y_start(0)
    for h in range(NH):
        for t in range(2):
            v_all[t * NH + h] = v_in[t * TILE : (t + 1) * TILE, h * HD : (h + 1) * HD]
    for t in range(2):
        for d in range(2):
            xg_copy(0, d, t).start()
    for o in range(1, NZ):
        req_copy(o).start()
    cg_copy(0, 0).start()

    total = y_total(0)
    q_scale, k_scale = as_columns(lax.rsqrt(total / width_all + EPS))
    q_scale_ref[...] = jnp.broadcast_to(q_scale, (TOK, 128))
    k_scale_ref[...] = jnp.broadcast_to(k_scale, (TOK, 128))

    def gain(ref, h):
        return ref[h * HD : (h + 1) * HD].reshape(1, HD)

    for t in range(2):
        rows = slice(t * TILE, (t + 1) * TILE)
        for h in range(NH):
            cols = slice(h * HD, (h + 1) * HD)
            q_bufs[0][h, rows] = (
                q_in[rows, cols].astype(F32) * q_scale_ref[rows] * gain(q_gain, h)
            ).astype(BF16)
            k_all[t * NH + h] = (
                k_in[rows, cols].astype(F32) * k_scale_ref[rows] * gain(k_gain, h)
            ).astype(BF16)
        for d in range(2):
            zf_copy(d, 1, 1, t).start()
            xg_copy(1, d, t).start()
    cg_copy(1, 0).start()

    for o in range(1, NZ):
        req_copy(o).wait_recv()
    table = pltpu.make_async_copy(req_v, req_s, here_sem.at[0])
    table.start()
    table.wait()

    def code_of(r, place):
        dx, other = place // 2, lax.rem(place, 2)
        lane_at = z * NP + lax.rem(x + dx, NX) * 2 + lax.rem(core + other, 2)
        return req_s[r, 0, lane_at]

    def row_stats(s, dp, top):
        e = jnp.exp(s - top)
        return fold_rows(e, jnp.add), fold_rows(e * dp, jnp.add)

    def near_scores(h, carry):
        tops = []
        for t in range(2):
            s = dot_nt(k_all[t * NH + h], q_bufs[0][h]) * FACTOR
            s_near[h, t] = s
            dp_near[h, t] = dot_nt(v_all[t * NH + h], g_bufs[0][h])
            tops.append(fold_rows(s, jnp.maximum))
        top = jnp.max(jnp.maximum(tops[0], tops[1]), axis=0, keepdims=True)
        first = row_stats(s_near[h, 0], dp_near[h, 0], top)
        second = row_stats(s_near[h, 1], dp_near[h, 1], top)
        mass = jnp.sum(first[0] + second[0], axis=0, keepdims=True)
        drift = jnp.sum(first[1] + second[1], axis=0, keepdims=True)
        near_stats[h, 0] = jnp.broadcast_to(top + jnp.log(mass), (8, TOK))
        near_stats[h, 1] = jnp.broadcast_to(drift / mass, (8, TOK))
        return carry

    def st_copy(r):
        return remote(
            stat_out.at[r], stat_in.at[(NZ - r) % NZ], st_send.at[r], st_recv.at[r], along_z(r)
        )

    sub = lax.broadcasted_iota(jnp.int32, (8, TOK), 0)

    def gradient_scores(r):
        def one(i, carry):
            for half in range(2):
                place = 2 * i + half
                code = jnp.maximum(code_of(r, place), 0)
                dp_all[r * NP + place] = dot_nt(
                    v_all[place * NT + code], g_bufs[r][lax.rem(code, NH)]
                )
            return carry

        lax.fori_loop(0, NP // 2, one, 0)

    def scores(r, with_dp=True):
        def one(i, carry):
            lse8, delta8 = carry
            for half in range(2):
                place = 2 * i + half
                code = jnp.maximum(code_of(r, place), 0)
                head = lax.rem(code, NH)
                s = dot_nt(k_all[place * NT + code], q_bufs[r][head]) * FACTOR
                if with_dp:
                    dp = dot_nt(v_all[place * NT + code], g_bufs[r][head])
                    dp_all[r * NP + place] = dp
                else:
                    dp = dp_all[r * NP + place]
                s_all[r * NP + place] = s
                top = jnp.max(fold_rows(s, jnp.maximum), axis=0, keepdims=True)
                mass, drift = row_stats(s, dp, top)
                mass = jnp.sum(mass, axis=0, keepdims=True)
                drift = jnp.sum(drift, axis=0, keepdims=True)
                lse8 = jnp.where(sub == place, top + jnp.log(mass), lse8)
                delta8 = jnp.where(sub == place, drift / mass, delta8)
            return lse8, delta8

        zero = jnp.zeros((8, TOK), F32)
        lse8, delta8 = lax.fori_loop(0, NP // 2, one, (zero, zero))
        if r == 0:
            stat_in[0, 0] = lse8
            stat_in[0, 1] = delta8
        else:
            stat_out[r, 0] = lse8
            stat_out[r, 1] = delta8
            st_copy(r).start()

    def forward(hop, kind):
        for t in range(2):
            for d in range(2):
                if hop < 4 or t == d:
                    zf_copy(d, hop, kind, t).wait_recv()
                if hop < 3 or (hop == 3 and t == d):
                    zf_copy(d, hop + 1, kind, t).start()

    def plane_first(kind):
        for t in range(2):
            for d in range(2):
                xg_copy(kind, d, t).wait_recv()
                if t == d:
                    xg_copy(kind, d, 2).start()
        cg_copy(kind, 1).start()
        cg_copy(kind, 3).start()

    def plane_second(kind):
        for d in range(2):
            xg_copy(kind, d, 2).wait_recv()
        cg_copy(kind, 2).start()

    forward(1, 0)
    plane_first(0)
    lax.fori_loop(0, NH, near_scores, 0)
    forward(1, 1)
    plane_first(1)
    plane_second(0)
    forward(2, 0)
    plane_second(1)
    for kind in range(2):
        for dx in range(NX):
            cg_copy(kind, dx).wait_recv()
    scores(0)
    forward(2, 1)
    scores(7)
    scores(1)
    forward(3, 0)
    scores(6)
    scores(2)
    row_at = lax.broadcasted_iota(jnp.int32, (NZ * NP, TOK), 0)
    head_at = jnp.full((NZ * NP, TOK), -1, jnp.int32)
    for h in range(NH):
        for c in range(REM):
            owner = sel[h, 0, c] >> 1
            dz = (owner // NP - z + NZ) & (NZ - 1)
            dx = ((owner & (NP - 1)) // 2 - x + NX) & (NX - 1)
            place = dx * 2 + ((owner + core) & 1)
            head_at = jnp.where(row_at == dz * NP + place, h, head_at)
    forward(3, 1)
    scores(5)
    forward(4, 0)
    scores(3)
    gradient_scores(4)
    forward(4, 1)
    scores(4, with_dp=False)

    for r in range(1, NZ):
        st_copy(r).wait_recv()
    pair_lse = jnp.concatenate([stat_in[r, 0] for r in range(NZ)], axis=0)
    pair_delta = jnp.concatenate([stat_in[r, 1] for r in range(NZ)], axis=0)
    for h in range(NH):
        mine = head_at == h
        near_lse, near_delta = near_stats[h, 0, :1], near_stats[h, 1, :1]
        top = jnp.max(jnp.where(mine, pair_lse, -3e38), axis=0, keepdims=True)
        top = jnp.maximum(top, near_lse)
        weight = jnp.where(mine, jnp.exp(pair_lse - top), 0.0)
        near_weight = jnp.exp(near_lse - top)
        whole = jnp.sum(weight, axis=0, keepdims=True) + near_weight
        drift = jnp.where(mine, weight * pair_delta, 0.0)
        drift = jnp.sum(drift, axis=0, keepdims=True) + near_weight * near_delta
        reply_out[pl.ds(h, 1)] = top + jnp.log(whole)
        reply_out[pl.ds(8 + h, 1)] = drift / whole

    def rp_copy(o):
        return remote(
            reply_out, reply_in.at[NZ - o], rp_send.at[o - 1], rp_recv.at[o - 1], along_z(o)
        )

    for o in (4, 3, 5, 2, 6, 1, 7):
        rp_copy(o).start()
    reply_in[0] = reply_out[...]

    for o in range(1, NZ):
        req_copy(o).wait_send()
    for hop in range(1, 5):
        for kind in range(2):
            for t in range(2):
                for d in range(2):
                    if hop < 4 or t == d:
                        zf_copy(d, hop, kind, t).wait_send()
    for kind in range(2):
        for d in range(2):
            for n in range(3):
                xg_copy(kind, d, n).wait_send()
        for dx in range(NX):
            cg_copy(kind, dx).wait_send()

    for o in range(1, NZ):
        rp_copy(o).wait_recv()
    for r in range(NZ):
        for h in range(NH):
            lse_ref[r * NH + h] = jnp.broadcast_to(reply_in[r, h : h + 1], (8, TOK))
            delta_ref[r * NH + h] = jnp.broadcast_to(reply_in[r, 8 + h : 9 + h], (8, TOK))

    def term(r, place):
        pair = r * NP + place
        asked = code_of(r, place)
        code = jnp.maximum(asked, 0)
        head = lax.rem(code, NH)
        probs = jnp.exp(s_all[pair] - lse_ref[r * NH + head][:1])
        probs = jnp.where(asked >= 0, probs, 0.0)
        ds = (probs * (dp_all[pair] - delta_ref[r * NH + head][:1]) * FACTOR).astype(BF16)
        dv = dot_nn(probs.astype(BF16), g_bufs[r][head])
        dk = dot_nn(ds, q_bufs[r][head])
        dq = dot_tn(ds, k_all[place * NT + code])
        kv_terms[2 * pair] = dv.astype(BF16)
        kv_terms[2 * pair + 1] = dk.astype(BF16)
        q_terms[pair] = dq.astype(BF16)

    zero_tile = jnp.zeros((TILE, HD), BF16)

    def tree(parts):
        while len(parts) > 1:
            parts = [parts[i] + parts[i + 1] for i in range(0, len(parts), 2)]
        return parts[0].astype(F32)

    def key_sum(place, kind, block):
        return tree(
            [
                jnp.where(
                    code_of(r, place) == block, kv_terms[2 * (r * NP + place) + kind], zero_tile
                )
                for r in range(NZ)
            ]
        )

    def query_sum(r, t, h):
        rows = slice(t * TILE, (t + 1) * TILE)
        return tree(
            [
                jnp.where(
                    lax.rem(jnp.maximum(code_of(r, place), 0), NH) == h,
                    q_terms[r * NP + place, rows],
                    zero_tile,
                )
                for place in range(NP)
            ]
        )

    def cb_copy(dx):
        part = pl.ds(dx * 2 * NT, 2 * NT)
        return remote(
            core_out.at[part], core_in.at[part], cb_send.at[dx], cb_recv.at[dx], other_core
        )

    def to_core(dx):
        def one(block, carry):
            for kind in range(2):
                acc = key_sum(2 * dx + 1, kind, block)
                core_out[dx * 2 * NT + kind * NT + block] = acc.astype(BF16)
            return carry

        lax.fori_loop(0, NT, one, 0)
        cb_copy(dx).start()

    def chip_sum(dx, kind, block):
        near = core_in[dx * 2 * NT + kind * NT + block].astype(F32)
        return key_sum(2 * dx, kind, block) + near

    def xb_copy(level, d, kind, t):
        dx = 2 if level == 2 else (1 if d == 0 else 3)
        part = pl.ds(kind * NT + t * NH, NH)
        return remote(
            x_out.at[dx - 1, part],
            x_in.at[level - 1, d, part],
            xb_send.at[level - 1, d, kind, t],
            xb_recv.at[level - 1, d, kind, t],
            x_next[d],
        )

    def x_pass(level, d, t):
        dx = 2 if level == 2 else (1 if d == 0 else 3)
        chained = level == 1 and t == d
        for kind in range(2):
            if chained:
                xb_copy(2, d, kind, t).wait_recv()

            def one(b, carry):
                block = t * NH + b
                acc = chip_sum(dx, kind, block)
                if chained:
                    acc += x_in[1, d, kind * NT + block].astype(F32)
                x_out[dx - 1, kind * NT + block] = acc.astype(BF16)
                return carry

            lax.fori_loop(0, NH, one, 0)
            xb_copy(level, d, kind, t).start()

    def zb_copy(d, level, t):
        r = level if d == 0 else NZ - level
        rows = pl.ds(t * TILE, TILE)
        return remote(
            q_bufs[r].at[:, rows],
            back_z.at[d, level - 1, :, rows],
            zb_send.at[d, level - 1, t],
            zb_recv.at[d, level - 1, t],
            z_next[d],
        )

    def z_pass(d, level):
        r = level if d == 0 else NZ - level
        for t in (1 - d, d) if level == 3 else ((d,) if level == 4 else (0, 1)):
            chained = level < 3 or (level == 3 and t == d)
            rows = slice(t * TILE, (t + 1) * TILE)
            if chained:
                zb_copy(d, level + 1, t).wait_recv()

            def one(h, carry):
                acc = query_sum(r, t, h)
                if chained:
                    acc += back_z[d, level, h, rows].astype(F32)
                q_bufs[r][h, rows] = acc.astype(BF16)
                return carry

            lax.fori_loop(0, NH, one, 0)
            zb_copy(d, level, t).start()

    def rest_terms(r):
        def one(i, carry):
            for half in range(2):
                place = 2 * i + half
                term(r, place + jnp.where(i >= 2, 2, 0))
            return carry

        lax.fori_loop(0, NP // 2 - 1, one, 0)

    def opposite_terms(r):
        term(r, 4)
        term(r, 5)

    opposite_terms(4)
    rest_terms(4)
    z_pass(0, 4)
    z_pass(1, 4)
    for r in (5, 3, 6, 2, 7, 1, 0):
        opposite_terms(r)
    to_core(2)
    rest_terms(5)
    z_pass(1, 3)
    rest_terms(3)
    z_pass(0, 3)
    cb_copy(2).wait_recv()
    x_pass(2, 0, 0)
    x_pass(2, 1, 1)
    for r in (6, 2, 7, 1, 0):
        rest_terms(r)
    to_core(1)
    to_core(3)
    z_pass(1, 2)
    z_pass(0, 2)
    cb_copy(1).wait_recv()
    x_pass(1, 0, 1)
    cb_copy(3).wait_recv()
    x_pass(1, 1, 0)
    x_pass(1, 0, 0)
    x_pass(1, 1, 1)
    to_core(0)

    def near_terms(h, carry):
        dq = jnp.zeros((TOK, HD), F32)
        lse, delta = lse_ref[h][:1], delta_ref[h][:1]
        for t in range(2):
            probs = jnp.exp(s_near[h, t] - lse)
            ds = (probs * (dp_near[h, t] - delta) * FACTOR).astype(BF16)
            dv_sum[t * NH + h] = dot_nn(probs.astype(BF16), g_bufs[0][h])
            dk_sum[t * NH + h] = dot_nn(ds, q_bufs[0][h])
            dq += dot_tn(ds, k_all[t * NH + h])
        dq_wide[h] = dq
        for t in range(2):
            dq_wide[h, t * TILE : (t + 1) * TILE] += query_sum(0, t, h)
        return carry

    lax.fori_loop(0, NH, near_terms, 0)
    z_pass(1, 1)
    z_pass(0, 1)
    cb_copy(0).wait_recv()

    def own_sum(block, carry):
        dv_sum[block] += chip_sum(0, 0, block)
        dk_sum[block] += chip_sum(0, 1, block)
        return carry

    lax.fori_loop(0, NT, own_sum, 0)

    for t in range(2):
        for d in range(2):
            zb_copy(d, 1, t).wait_recv()
    dots = jnp.zeros((TOK, HD), F32)
    for h in range(NH):
        cols = slice(h * HD, (h + 1) * HD)
        dq = dq_wide[h] + back_z[0, 0, h].astype(F32) + back_z[1, 0, h].astype(F32)
        dq_wide[h] = dq
        dots += gain(q_gain, h) * dq * q_in[:, cols].astype(F32)
    y_out[1] = as_rows(jnp.sum(dots, axis=1, keepdims=True), 0.0)
    y_start(1)

    for t in range(2):
        for d in range(2):
            for kind in range(2):
                xb_copy(1, d, kind, t).wait_recv()
    columns = []
    for t in range(2):
        rows = slice(t * TILE, (t + 1) * TILE)
        dots = jnp.zeros((TILE, HD), F32)
        for h in range(NH):
            cols = slice(h * HD, (h + 1) * HD)
            b = t * NH + h
            dk = dk_sum[b] + x_in[0, 0, NT + b].astype(F32) + x_in[0, 1, NT + b].astype(F32)
            dk_sum[b] = dk
            dots += gain(k_gain, h) * dk * k_in[rows, cols].astype(F32)
        columns.append(jnp.sum(dots, axis=1, keepdims=True))
    y_out[2] = as_rows(jnp.concatenate(columns, axis=0), 0.0)
    y_start(2)

    def finish(wide, gains, grad, scale, dot_mean):
        return (scale * gains * grad - wide * (scale * scale * scale) * dot_mean).astype(BF16)

    for t in range(2):
        rows = slice(t * TILE, (t + 1) * TILE)
        for h in range(NH):
            b = t * NH + h
            dv = dv_sum[b] + x_in[0, 0, b].astype(F32) + x_in[0, 1, b].astype(F32)
            dv_out[rows, h * HD : (h + 1) * HD] = dv.astype(BF16)
    q_dot, _ = as_columns(y_total(1) / width_all)
    for h in range(NH):
        cols = slice(h * HD, (h + 1) * HD)
        dq_out[:, cols] = finish(
            q_in[:, cols].astype(F32), gain(q_gain, h), dq_wide[h], q_scale_ref[...], q_dot
        )
    k_dot, _ = as_columns(y_total(2) / width_all)
    for t in range(2):
        rows = slice(t * TILE, (t + 1) * TILE)
        for h in range(NH):
            cols = slice(h * HD, (h + 1) * HD)
            dk_out[rows, cols] = finish(
                k_in[rows, cols].astype(F32),
                gain(k_gain, h),
                dk_sum[t * NH + h],
                k_scale_ref[rows],
                k_dot[rows],
            )

    for n in range(3):
        for p in range(1, NY):
            y_copy(n, p).wait_send()
    for r in range(1, NZ):
        st_copy(r).wait_send()
        rp_copy(r).wait_send()
    for dx in range(NX):
        cb_copy(dx).wait_send()
    for t in range(2):
        for d in range(2):
            for level in range(1, 5):
                if level < 4 or t == d:
                    zb_copy(d, level, t).wait_send()
            for kind in range(2):
                xb_copy(1, d, kind, t).wait_send()
                if t == d:
                    xb_copy(2, d, kind, t).wait_send()


def place_results(a, b, c, a_out, b_out, c_out, held, sems):
    coming = [
        pltpu.make_async_copy(src, held.at[i], sems.at[0, i]) for i, src in enumerate((a, b, c))
    ]
    going = [
        pltpu.make_async_copy(held.at[i], dst, sems.at[1, i])
        for i, dst in enumerate((a_out, b_out, c_out))
    ]
    for copy in coming:
        copy.start()
    for came, goes in zip(coming, going):
        came.wait()
        goes.start()
    for copy in going:
        copy.wait()


def on_device(q_pre, k_pre, values, out_grad, q_gain, k_gain, selected):
    width_dev = q_pre.shape[1]
    width_all = float(width_dev * lax.axis_size("head"))
    vmem = pl.BlockSpec(memory_space=pltpu.VMEM)
    dma = pltpu.SemaphoreType.DMA
    pairs = NZ * NP
    scratch = [pltpu.VMEM((NH, TOK, HD), BF16) for _ in range(2 * NZ)] + [
        pltpu.VMEM((NP * NT, TILE, HD), BF16),
        pltpu.VMEM((NP * NT, TILE, HD), BF16),
        pltpu.VMEM((pairs, TILE, TOK), F32),
        pltpu.VMEM((pairs, TILE, TOK), F32),
        pltpu.VMEM((2 * pairs, TILE, HD), BF16),
        pltpu.VMEM((pairs, TOK, HD), BF16),
        pltpu.VMEM((2, 4, NH, TOK, HD), BF16),
        pltpu.VMEM((NX * 2 * NT, TILE, HD), BF16),
        pltpu.VMEM((NX * 2 * NT, TILE, HD), BF16),
        pltpu.VMEM((3, 2 * NT, TILE, HD), BF16),
        pltpu.VMEM((2, 2, 2 * NT, TILE, HD), BF16),
        pltpu.VMEM((NH, 2, TILE, TOK), F32),
        pltpu.VMEM((NH, 2, TILE, TOK), F32),
        pltpu.VMEM((NH, 2, 8, TOK), F32),
        pltpu.VMEM((NZ, 2, NP, TOK), F32),
        pltpu.VMEM((NZ, 2, NP, TOK), F32),
        pltpu.VMEM((16, TOK), F32),
        pltpu.VMEM((NZ, 16, TOK), F32),
        pltpu.VMEM((NZ * NH, 8, TOK), F32),
        pltpu.VMEM((NZ * NH, 8, TOK), F32),
        pltpu.VMEM((NH, TOK, HD), F32),
        pltpu.VMEM((NT, TILE, HD), F32),
        pltpu.VMEM((NT, TILE, HD), F32),
        pltpu.VMEM((TOK, 128), F32),
        pltpu.VMEM((TOK, 128), F32),
        pltpu.VMEM((3, 8, TOK), F32),
        pltpu.VMEM((3, NY - 1, 8, TOK), F32),
        pltpu.VMEM((NZ, 8, 128), jnp.int32),
        pltpu.SMEM((NZ, 8, 128), jnp.int32),
        dma((2, 16)),
        dma((2, 16)),
        dma((2, 2, 3)),
        dma((2, 2, 3)),
        dma((2, NX)),
        dma((2, NX)),
        dma((NZ,)),
        dma((NZ,)),
        dma((NZ - 1,)),
        dma((NZ - 1,)),
        dma((2, 4, 2)),
        dma((2, 4, 2)),
        dma((NX,)),
        dma((NX,)),
        dma((2, 2, 2, 2)),
        dma((2, 2, 2, 2)),
        dma((3, NY - 1)),
        dma((3, NY - 1)),
        dma((NZ - 1,)),
        dma((NZ - 1,)),
        dma((1,)),
        pltpu.VMEM(q_pre.shape, BF16),
        pltpu.VMEM(q_pre.shape, BF16),
        pltpu.VMEM(q_pre.shape, BF16),
        dma((3,)),
    ]
    out = jax.ShapeDtypeStruct(q_pre.shape, BF16)
    results = pl.pallas_call(
        functools.partial(kernel, width_all),
        out_shape=(out, out, out),
        in_specs=[pl.BlockSpec(memory_space=pltpu.SMEM)]
        + [pl.BlockSpec(memory_space=pl.ANY)] * 3
        + [vmem] * 3,
        out_specs=(vmem, vmem, vmem),
        scratch_shapes=scratch,
        compiler_params=pltpu.CompilerParams(
            collective_id=0, has_side_effects=True, vmem_limit_bytes=60 * 2**20
        ),
        name="sparse_attention_backward",
    )(
        jnp.transpose(selected, (1, 0, 2)), q_pre, k_pre, values, out_grad, q_gain, k_gain
    )
    anywhere = pl.BlockSpec(memory_space=pl.ANY)
    return pl.pallas_call(
        place_results,
        out_shape=(out, out, out),
        in_specs=[anywhere] * 3,
        out_specs=(anywhere,) * 3,
        scratch_shapes=[pltpu.VMEM((3,) + q_pre.shape, BF16), dma((2, 3))],
        name="place_results",
    )(*results)


def solution(mesh):
    placed = (
        P("ctx", "head"),
        P("ctx", "head"),
        P("ctx", "head"),
        P("ctx", "head"),
        P("head"),
        P("head"),
        P("ctx", "head", None),
    )
    return jax.shard_map(
        on_device,
        mesh=mesh,
        in_specs=placed,
        out_specs=(P("ctx", "head"), P("ctx", "head"), P("ctx", "head")),
        check_vma=False,
    )
```
